512 devices in a mesh: gx: 32 (over z, core), gy: 4 (over x), col: 4 (over y).
Axes of the slice: x: 4, y: 4, z: 16, core: 2. Of those that a mesh axis runs over, the one named last changes fastest.
Arguments:
- divergence: float32 [24, 24, 6144], P('gy', 'col', 'gx'), may hold values from -15 to 15
- elem_size: float32 [3, 16384], P(None, ('gx', 'gy', 'col')), may hold values from 1.5 to 4
- helm_diag: float32 [32, 32, 8192], P('gy', 'col', 'gx'), may hold values from 0.02 to 0.1
- fdm_vectors: float32 [3, 8, 8, 16384], P(None, None, None, ('gx', 'gy', 'col')), may hold values from -2 to 2
- fdm_values: float32 [3, 8, 16384], P(None, None, ('gx', 'gy', 'col')), may hold values from 0.3 to 3
- coarse_rows: float32 [16384, 512], P(('gx', 'gy', 'col')), may hold values from -3 to 56, as said below
- axial_link: float32 [32, 4, 4], P('gx', 'gy', 'col'), may hold values from 3 to 9
Outputs:
- pressure: float32 [24, 24, 6144], P('gy', 'col', 'gx')
- residual: float32 [24, 24, 6144], P('gy', 'col', 'gx')
The draws below stay inside these ranges and needn't reach their ends.
Inputs may be any that keep to these rules, and one draw needn't show every extreme that they name: `coarse_rows`: for every slab s, rows s * 512 to s * 512 + 511 form a symmetric 512 x 512 matrix.
All inputs are finite; a program needn't handle non-finite values.
Results may differ from the reference program's by a relative error of at most 0.0023.
Values sent between devices are 32-bit elements; how exact they have to be, the bound alone decides.
No kernel may reach another device: no remote copies, remote signals or barrier semaphores. Data moves between devices by JAX's collectives and lax.ppermute only.
A program may use at most 64 MiB of HBM per device.

```python
import math
import jax
import jax.numpy as jnp
import numpy as np
from jax import lax

EB = 1
EC = 1
EA = 32
ITERS = 2
CHEB = 6
ELEMENTS = 16384
GROUP = 512
SLABS = 32
NEB = 4
NEC = 4
NEA = 1024
NB = 24
NC = 24
NA = 6144
VB = 32
VC = 32
VA = 8192
N_GX = 32
N_GY = 4
N_COL = 4


def draw_divergence(key, part):
    key = jax.random.fold_in(key, 5)
    axial = jnp.arange(NA, dtype=jnp.float32) / NA
    ramp = (1.0 + 2.0 * axial)[None, None, :]
    noise = jnp.clip(jax.random.normal(key, (NB, NC, NA), jnp.float32), -4.0, 4.0)
    return noise * ramp


def draw_coarse_rows(key, part):
    key = jax.random.fold_in(key, 11)
    first_key, second_key = jax.random.split(key)
    slabs_n = ELEMENTS // GROUP
    noise = jnp.clip(jax.random.normal(first_key, (slabs_n, GROUP, GROUP), jnp.float32), -5.0, 5.0)
    paired = (noise + jnp.swapaxes(noise, 1, 2)) * (6.0 / math.sqrt(2.0 * GROUP))
    paired = jnp.clip(paired, -2.9, 2.9)
    diagonal = jax.random.uniform(second_key, (slabs_n, GROUP), jnp.float32, 40.0, 56.0)
    identity = jnp.eye(GROUP, dtype=jnp.float32)
    blocks = paired * (1.0 - identity) + identity * diagonal[:, :, None]
    return blocks.reshape(ELEMENTS, GROUP)


def shard_levels(rng, dims, shards, least, top_value):
    def one(position, shards_of):
        draws = jax.random.uniform(jax.random.fold_in(jax.random.fold_in(rng, 6), position), (shards_of,), jnp.float32, least / len(shards), top_value / len(shards))
        return jnp.repeat(jnp.exp(draws), dims[position] // shards_of).reshape((-1,) + (1,) * (len(dims) - position - 1))

    factor_of = one(*shards[0])
    for cut in shards[1:]:
        factor_of = factor_of * one(*cut)
    return factor_of


def normal_values(own_key, extent, deviation, reach, pieces=(), held_as=jnp.bfloat16):
    entries = deviation * jax.random.normal(own_key, extent, jnp.float32)
    if pieces:
        entries = entries * shard_levels(own_key, extent, pieces, -0.22, 0.18)
    return jnp.clip(entries, -reach, reach).astype(held_as)


def setup_inputs(seed: int = 0) -> dict:
    key_of = jax.random.split(jax.random.key(seed), 8)
    divergence = draw_divergence(jax.random.fold_in(key_of[7], 71), 0)
    elem_size = jnp.clip(jnp.exp(math.log(4.0) - 0.98082925 * jax.random.uniform(key_of[1], (3, ELEMENTS), jnp.float32) ** shard_levels(key_of[1], (3, ELEMENTS), ((1, 512),), -0.2, 0.2)), 1.5, 4.0)
    helm_diag = jnp.clip(jnp.exp(math.log(0.1) - 1.609438 * jax.random.uniform(key_of[2], (VB, VC, VA), jnp.float32) ** shard_levels(key_of[2], (VB, VC, VA), ((0, 4), (1, 4), (2, 32)), -0.2, 0.2)), 0.02, 0.1)
    fdm_vectors = normal_values(key_of[3], (3, 8, 8, ELEMENTS), 8 ** -0.5, 2.0, ((3, 512),), jnp.float32)
    fdm_values = jnp.clip(jnp.exp(math.log(3.0) - 2.3025851 * jax.random.uniform(key_of[4], (3, 8, ELEMENTS), jnp.float32) ** shard_levels(key_of[4], (3, 8, ELEMENTS), ((2, 512),), -0.2, 0.2)), 0.3, 3.0)
    coarse_rows = draw_coarse_rows(jax.random.fold_in(key_of[7], 71), 0)
    axial_link = jnp.clip(3.0 + 6.0 * jax.random.uniform(key_of[6], (SLABS, NEB, NEC), jnp.float32) ** shard_levels(key_of[6], (SLABS, NEB, NEC), ((0, 32), (1, 4), (2, 4)), -0.2, 0.2), 3.0, 9.0)
    return {"divergence": divergence, "elem_size": elem_size, "helm_diag": helm_diag, "fdm_vectors": fdm_vectors, "fdm_values": fdm_values, "coarse_rows": coarse_rows, "axial_link": axial_link}


LOBATTO_NODES = [-1.0, -0.8717401485096066, -0.5917001814331423, -0.2092992179024789, 0.2092992179024789, 0.5917001814331423, 0.8717401485096066, 1.0]
GAUSS_NODES = [-0.9324695142031521, -0.6612093864662645, -0.2386191860831909, 0.2386191860831909, 0.6612093864662645, 0.9324695142031521]
GAUSS_WEIGHTS = [0.1713244923791704, 0.3607615730481386, 0.4679139345726910, 0.4679139345726910, 0.3607615730481386, 0.1713244923791704]
SPECTRUM_LOW = 8.0
SPECTRUM_HIGH = 90.0
HIGHEST = lax.Precision.HIGHEST


def basis_tables():
    lobatto = np.array(LOBATTO_NODES)
    points = np.array(GAUSS_NODES)
    interp = np.ones((6, 8))
    slopes = np.zeros((6, 8))
    for p in range(6):
        for m in range(8):
            product = 1.0
            for q in range(8):
                if q != m:
                    product = product * (points[p] - lobatto[q]) / (lobatto[m] - lobatto[q])
            interp[p, m] = product
            running = 0.0
            for q in range(8):
                if q != m:
                    factor = 1.0 / (lobatto[m] - lobatto[q])
                    for k in range(8):
                        if k != m and k != q:
                            factor = factor * (points[p] - lobatto[k]) / (lobatto[m] - lobatto[k])
                    running = running + factor
            slopes[p, m] = running
    return jnp.asarray(interp, jnp.float32), jnp.asarray(slopes, jnp.float32)


def element_grid(values_in):
    leading = values_in.shape[:-1]
    k = len(leading)
    shaped = values_in.reshape(leading + (N_GX, N_GY, N_COL, EB, EC, EA))
    order = tuple(range(k)) + (k + 1, k + 3, k + 2, k + 4, k, k + 5)
    shaped = jnp.transpose(shaped, order)
    return shaped.reshape(leading + (N_GY * EB, N_COL * EC, N_GX * EA))


def to_flat(grid_values):
    shaped = grid_values.reshape(N_GY, EB, N_COL, EC, N_GX, EA)
    return jnp.transpose(shaped, (4, 0, 2, 1, 3, 5)).reshape(-1)


def nodal_expand(values_in, copies):
    return jnp.repeat(jnp.repeat(jnp.repeat(values_in, copies, -3), copies, -2), copies, -1)


def along(field, matrix, axis_at):
    moved_x = jnp.moveaxis(field, axis_at, -1)
    elements = moved_x.shape[-1] // matrix.shape[1]
    blocks = moved_x.reshape(moved_x.shape[:-1] + (elements, matrix.shape[1]))
    result = jnp.einsum("...ei,oi->...eo", blocks, matrix, precision=HIGHEST)
    result = result.reshape(moved_x.shape[:-1] + (elements * matrix.shape[0],))
    return jnp.moveaxis(result, -1, axis_at)


def assemble_line(field, axis_at, periodic):
    moved_x = jnp.moveaxis(field, axis_at, -1)
    elements = moved_x.shape[-1] // 8
    blocks = moved_x.reshape(moved_x.shape[:-1] + (elements, 8))
    carried = jnp.concatenate([jnp.zeros_like(blocks[..., :1, 7]), blocks[..., :-1, 7]], axis=-1)
    leading_col = blocks[..., 0] + carried
    rows_part = jnp.concatenate([leading_col[..., None], blocks[..., 1:7]], axis=-1)
    unique = jnp.concatenate([rows_part.reshape(moved_x.shape[:-1] + (elements * 7,)), blocks[..., -1, 7:8]], axis=-1)
    if periodic:
        unique = jnp.concatenate([unique[..., :1] + unique[..., -1:], unique[..., 1:-1]], axis=-1)
    return jnp.moveaxis(unique, -1, axis_at)


def distribute_line(unique, axis_at, periodic):
    moved_x = jnp.moveaxis(unique, axis_at, -1)
    if periodic:
        moved_x = jnp.concatenate([moved_x, moved_x[..., :1]], axis=-1)
    elements = (moved_x.shape[-1] - 1) // 7
    head_part = moved_x[..., :elements * 7].reshape(moved_x.shape[:-1] + (elements, 7))
    tail_part = moved_x[..., 1:].reshape(moved_x.shape[:-1] + (elements, 7))[..., 6:7]
    field = jnp.concatenate([head_part, tail_part], axis=-1).reshape(moved_x.shape[:-1] + (elements * 8,))
    return jnp.moveaxis(field, -1, axis_at)


def assemble_all(field):
    field = assemble_line(field, -3, False)
    field = assemble_line(field, -2, True)
    return assemble_line(field, -1, True)


def distribute_all(unique):
    unique = distribute_line(unique, -3, False)
    unique = distribute_line(unique, -2, True)
    return distribute_line(unique, -1, True)


def schur_apply(pressure_in, weights, factors, helm_total, interp, slopes):
    scaled = weights * pressure_in
    tables = ((slopes, interp, interp), (interp, slopes, interp), (interp, interp, slopes))
    gradients = []
    for comp in range(3):
        field = scaled * factors[comp]
        for axis_at in range(3):
            field = along(field, tables[comp][axis_at].T, axis_at)
        gradients.append(field)
    unique = assemble_all(jnp.stack(gradients)) / helm_total
    spread = distribute_all(unique)
    combined = None
    for comp in range(3):
        field = spread[comp]
        for axis_at in range(3):
            field = along(field, tables[comp][axis_at], axis_at)
        if combined is None:
            combined = factors[comp] * field
        else:
            combined = combined + factors[comp] * field
    return weights * combined


def wrap_fold(field, axis_at):
    moved_x = jnp.moveaxis(field, axis_at, -1)
    inner_part = moved_x[..., 1:-1]
    inner_part = inner_part.at[..., 0].add(moved_x[..., -1])
    inner_part = inner_part.at[..., -1].add(moved_x[..., 0])
    return jnp.moveaxis(inner_part, -1, axis_at)


def schwarz_apply(residual_in, vectors, values):
    padded = jnp.pad(residual_in, ((1, 1), (0, 0), (0, 0)))
    padded = jnp.concatenate([padded[:, -1:], padded, padded[:, :1]], axis=1)
    padded = jnp.concatenate([padded[:, :, -1:], padded, padded[:, :, :1]], axis=2)
    index_b = jnp.arange(NEB)[:, None] * 6 + jnp.arange(8)[None, :]
    index_c = jnp.arange(NEC)[:, None] * 6 + jnp.arange(8)[None, :]
    index_a = jnp.arange(NEA)[:, None] * 6 + jnp.arange(8)[None, :]
    spots = (index_b[:, :, None, None, None, None], index_c[None, None, :, :, None, None], index_a[None, None, None, None, :, :])
    boxes = jnp.transpose(padded[spots], (1, 3, 5, 0, 2, 4))
    modes = jnp.einsum("imbca,ijkbca->mjkbca", vectors[0], boxes, precision=HIGHEST)
    modes = jnp.einsum("jnbca,mjkbca->mnkbca", vectors[1], modes, precision=HIGHEST)
    modes = jnp.einsum("klbca,mnkbca->mnlbca", vectors[2], modes, precision=HIGHEST)
    denominator = values[0][:, None, None] + values[1][None, :, None] + values[2][None, None, :]
    modes = modes / denominator
    local_part = jnp.einsum("imbca,mnlbca->inlbca", vectors[0], modes, precision=HIGHEST)
    local_part = jnp.einsum("jnbca,inlbca->ijlbca", vectors[1], local_part, precision=HIGHEST)
    local_part = jnp.einsum("klbca,ijlbca->ijkbca", vectors[2], local_part, precision=HIGHEST)
    local_part = jnp.transpose(local_part, (3, 0, 4, 1, 5, 2))
    gathered = jnp.zeros_like(padded).at[spots].add(local_part)
    gathered = wrap_fold(gathered, 2)
    gathered = wrap_fold(gathered, 1)
    return gathered[1:-1]


def coarse_apply(vector_grid, blocks, link_grid):
    flat = to_flat(vector_grid).reshape(N_GX, GROUP)
    dense_part = jnp.einsum("sgh,sh->sg", blocks, flat, precision=HIGHEST).reshape(-1)
    result = element_grid(dense_part)
    last_face = vector_grid[:, :, EA - 1::EA]
    first_face = vector_grid[:, :, ::EA]
    link_moved = jnp.transpose(link_grid, (1, 2, 0))
    result = result.at[:, :, ::EA].add(-jnp.roll(link_moved * last_face, 1, axis=2))
    result = result.at[:, :, EA - 1::EA].add(-(link_moved * jnp.roll(first_face, -1, axis=2)))
    return result


def chebyshev_solve(source, operator):
    center = (SPECTRUM_HIGH + SPECTRUM_LOW) / 2.0
    spread = (SPECTRUM_HIGH - SPECTRUM_LOW) / 2.0
    ratio_cs = center / spread
    rho_now = 1.0 / ratio_cs
    solution = jnp.zeros_like(source)
    remainder = source
    update = source / center
    for sweep_at in range(CHEB):
        solution = solution + update
        remainder = remainder - operator(update)
        rho_next = 1.0 / (2.0 * ratio_cs - rho_now)
        update = (rho_next * rho_now) * update + (2.0 * rho_next / spread) * remainder
        rho_now = rho_next
    return solution + update


def reference(divergence, elem_size, helm_diag, fdm_vectors, fdm_values, coarse_rows, axial_link):
    interp, slopes = basis_tables()
    sizes_grid = element_grid(elem_size)
    volume = sizes_grid[0] * sizes_grid[1] * sizes_grid[2] / 8.0
    weights_1d = jnp.asarray(GAUSS_WEIGHTS, jnp.float32)
    weight_b = jnp.tile(weights_1d, NEB)
    weight_c = jnp.tile(weights_1d, NEC)
    weight_a = jnp.tile(weights_1d, NEA)
    weights = weight_b[:, None, None] * weight_c[None, :, None] * weight_a[None, None, :] * nodal_expand(volume, 6)
    factors = 2.0 / nodal_expand(sizes_grid, 6)
    helm_total = assemble_all(helm_diag[None])
    vectors = element_grid(fdm_vectors)
    values = element_grid(fdm_values)
    blocks = coarse_rows.reshape(N_GX, GROUP, GROUP)

    def operator(vector_grid):
        return coarse_apply(vector_grid, blocks, axial_link)

    def precondition(residual_in):
        local_part = schwarz_apply(residual_in, vectors, values)
        sums = residual_in.reshape(NEB, 6, NEC, 6, NEA, 6).sum(axis=(1, 3, 5))
        coarse = chebyshev_solve(sums, operator)
        return local_part + nodal_expand(coarse, 6)

    pressure = jnp.zeros_like(divergence)
    residual = divergence
    direction = divergence
    previous = jnp.float32(1.0)
    for turn in range(ITERS):
        precond = precondition(residual)
        r_dot_z = jnp.sum(residual * precond)
        if turn == 0:
            direction = precond
        else:
            direction = precond + (r_dot_z / previous) * direction
        image = schur_apply(direction, weights, factors, helm_total, interp, slopes)
        step_len = r_dot_z / jnp.sum(direction * image)
        pressure = pressure + step_len * direction
        residual = residual - step_len * image
        previous = r_dot_z
    return pressure, residual
```

```python
import jax
import jax.numpy as jnp
import ml_dtypes
import numpy as np
from jax import lax
from jax.experimental import pallas as pl
from jax.experimental.pallas import tpu as pltpu
from jax.sharding import PartitionSpec as P

EA = 32
CHEB = 6
NB = 4

LOBATTO_NODES = [
    -1.0,
    -0.8717401485096066,
    -0.5917001814331423,
    -0.2092992179024789,
    0.2092992179024789,
    0.5917001814331423,
    0.8717401485096066,
    1.0,
]
GAUSS_NODES = [
    -0.932469514203152,
    -0.6612093864662645,
    -0.2386191860831909,
    0.2386191860831909,
    0.6612093864662645,
    0.932469514203152,
]
GAUSS_WEIGHTS = [
    0.1713244923791704,
    0.3607615730481386,
    0.467913934572691,
    0.467913934572691,
    0.3607615730481386,
    0.1713244923791704,
]
SPECTRUM_LOW = 8.0
SPECTRUM_HIGH = 90.0
HIGHEST = lax.Precision.HIGHEST
F32 = jnp.float32
BF16 = jnp.bfloat16

ROWS_P = 288
ROWS_V = 512
ROWS_A = 176
ROWS_B = 224


def basis_tables():
    lobatto = np.array(LOBATTO_NODES)
    points = np.array(GAUSS_NODES)
    interp = np.ones((6, 8))
    slopes = np.zeros((6, 8))
    for p in range(6):
        for m in range(8):
            product = 1.0
            for q in range(8):
                if q != m:
                    product = product * (points[p] - lobatto[q]) / (lobatto[m] - lobatto[q])
            interp[p, m] = product
            running = 0.0
            for q in range(8):
                if q != m:
                    factor = 1.0 / (lobatto[m] - lobatto[q])
                    for k in range(8):
                        if k != m and k != q:
                            factor = factor * (points[p] - lobatto[k]) / (lobatto[m] - lobatto[k])
                    running = running + factor
            slopes[p, m] = running
    return interp, slopes


def gradient_tables():
    interp, slopes = basis_tables()
    weight = np.array(GAUSS_WEIGHTS)
    tables = []
    for comp in range(3):
        sides = [(slopes if side == comp else interp) * weight[:, None] for side in range(3)]
        full = np.zeros((8, 8, 8, 6, 6, 8))
        full[..., 1:7] = np.einsum("iu,jv,kw->wuvkij", sides[0], sides[1], sides[2])
        tables.append(full.reshape(ROWS_V, ROWS_P))
    table = np.concatenate(tables, axis=0).astype(np.float32)
    high = table.astype(ml_dtypes.bfloat16)
    low = (table - high.astype(np.float32)).astype(ml_dtypes.bfloat16)
    forward = np.concatenate([high, high, low], axis=1)
    backward = np.concatenate([high.T, high.T, low.T], axis=1)
    return forward, backward


def order_table(nodes):
    table = np.zeros((nodes * EA, nodes * EA), np.float32)
    for k in range(nodes):
        for a in range(EA):
            table[a * nodes + k, k * EA + a] = 1.0
    return table


def sweep_factors():
    center = (SPECTRUM_HIGH + SPECTRUM_LOW) / 2.0
    spread = (SPECTRUM_HIGH - SPECTRUM_LOW) / 2.0
    ratio_cs = center / spread
    rho_now = 1.0 / ratio_cs
    keep, add = [], []
    for _ in range(CHEB):
        rho_next = 1.0 / (2.0 * ratio_cs - rho_now)
        keep.append(rho_next * rho_now)
        add.append(2.0 * rho_next / spread)
        rho_now = rho_next
    return center, keep, add


CENTER, KEEP, ADD = sweep_factors()


def lanes(shape):
    return lax.broadcasted_iota(jnp.int32, shape, len(shape) - 1)


def turn(value, shift):
    shift = shift % 128
    return value if shift == 0 else pltpu.roll(value, shift, value.ndim - 1)


def at_first(value, slot=0):
    moved = turn(value, 97 + slot)
    return jnp.where(lanes(moved.shape) % EA == 0, moved, 0.0)


def at_last(value, slot=0):
    moved = turn(value, 31 - slot)
    return jnp.where(lanes(moved.shape) % EA == EA - 1, moved, 0.0)


def pack_last(blocks):
    packed = None
    for slot, block in enumerate(blocks):
        part = turn(jnp.where(lanes(block.shape) % EA == EA - 1, block, 0.0), -slot)
        packed = part if packed is None else packed + part
    return packed


def pack_first(blocks):
    packed = None
    for slot, block in enumerate(blocks):
        part = turn(jnp.where(lanes(block.shape) % EA == 0, block, 0.0), slot)
        packed = part if packed is None else packed + part
    return packed


def times(dense_ref, vector):
    columns = jnp.concatenate([vector, jnp.zeros_like(vector)], axis=0).T
    total = None
    for b in range(NB):
        part = dense_ref[b * 128 : (b + 1) * 128, :] * columns[:, b : b + 1]
        total = part if total is None else total + part
    row = jnp.sum(total, axis=0, keepdims=True)
    return jnp.concatenate([row[:, b * 128 : (b + 1) * 128] for b in range(NB)], axis=0)


def sweep_begin(dense_ref, source, link):
    update = source * (1.0 / CENTER)
    remainder = source - times(dense_ref, update)
    free = KEEP[0] * update + ADD[0] * remainder
    state = jnp.concatenate([update, remainder, update, link], axis=0)
    return state, jnp.concatenate([update, free, link, link], axis=0)


def sweep_pair(dense_ref, state, from_left, from_right, sweep_at):
    update, remainder, solution, link = [state[4 * n : 4 * n + 4] for n in range(4)]
    left = at_first(from_left)
    right = at_last(from_right)
    place = lanes(update.shape) % EA
    link_left = left[8:12]
    link_right = jnp.where(place == EA - 1, link, 0.0)
    remainder = remainder + link_left * left[0:4] + link_right * right[0:4]
    left_next = left[4:8] + ADD[sweep_at] * link_left * update
    right_next = right[4:8] + ADD[sweep_at] * link_right * update
    update = KEEP[sweep_at] * update + ADD[sweep_at] * remainder
    solution = solution + update
    remainder = remainder - times(dense_ref, update)
    remainder = remainder + link_left * left_next + link_right * right_next
    update = KEEP[sweep_at + 1] * update + ADD[sweep_at + 1] * remainder
    solution = solution + update
    if sweep_at + 2 == CHEB:
        return solution
    remainder = remainder - times(dense_ref, update)
    free = KEEP[sweep_at + 2] * update + ADD[sweep_at + 2] * remainder
    state = jnp.concatenate([update, remainder, solution, link], axis=0)
    return state, jnp.concatenate([update, free, link, link], axis=0)


def fill_boxes(field_ref, box_ref):
    box_ref[...] = jnp.zeros(box_ref.shape, F32)
    for b in range(NB):
        for k in range(6):
            box_ref[b, (k + 1) * 64 + 8 : (k + 1) * 64 + 56, :] = field_ref[b, k * 48 : (k + 1) * 48, :]
        before = box_ref[b, pl.ds(6, 64, stride=8), :]
        after = box_ref[b, pl.ds(1, 64, stride=8), :]
        box_ref[b, pl.ds(0, 64, stride=8), :] = turn(before, 32)
        box_ref[b, pl.ds(7, 64, stride=8), :] = turn(after, -32)
    for b in range(NB):
        for k in range(1, 7):
            if b > 0:
                box_ref[b, k * 64 : k * 64 + 8, :] = box_ref[b - 1, k * 64 + 48 : k * 64 + 56, :]
            if b < NB - 1:
                box_ref[b, k * 64 + 56 : k * 64 + 64, :] = box_ref[b + 1, k * 64 + 8 : k * 64 + 16, :]


def begin_kernel_part(field_ref, small_ref, dense_ref, box_ref, state_ref, ahead_ref, behind_ref, extra):
    fill_boxes(field_ref, box_ref)
    source = jnp.concatenate(
        [jnp.sum(field_ref[b], axis=0, keepdims=True) for b in range(NB)], axis=0
    )
    link = jnp.concatenate([small_ref[b, 32:33, :] for b in range(NB)], axis=0)
    state, message = sweep_begin(dense_ref, source, link)
    state_ref[...] = state
    ahead_ref[0:16, :] = message
    behind_ref[0:16, :] = message
    ahead_ref[16:80, :] = pack_last([box_ref[b, 384:448, :] for b in range(NB)] + extra[0])
    behind_ref[16:80, :] = pack_first([box_ref[b, 64:128, :] for b in range(NB)] + extra[1])


def pack_body(rhs_ref, helm_ref, vec_ref, val_ref, size_ref, rows_ref, link_ref, six_ref, eight_ref, a_ref, b_ref, tmp):
    for t in range(4):
        a_ref[t * 32 : (t + 1) * 32, :] = rows_ref[:, t * 128 : (t + 1) * 128]
        a_ref[128:176, t * 32 : (t + 1) * 32] = vec_ref[t * 48 : (t + 1) * 48, :]
    tmp[...] = jnp.zeros(tmp.shape, F32)
    for i in range(6):
        tmp[i * 8 + 1 : i * 8 + 7, :] = rhs_ref[i]
    nodes = jnp.dot(tmp[...], six_ref[...], precision=HIGHEST, preferred_element_type=F32)
    b_ref[0:48, :] = nodes[:, 0:128]
    b_ref[48:96, :] = jnp.zeros((48, 128), F32)
    b_ref[48:96, 0:64] = nodes[:, 128:192]
    b_ref[48:72, 64:96] = val_ref[...]
    b_ref[72:75, 64:96] = size_ref[...]
    b_ref[80:81, 64:96] = jnp.broadcast_to(link_ref[...], (1, 32))
    helm = jnp.dot(
        helm_ref[...].reshape(64, 256), eight_ref[...], precision=HIGHEST, preferred_element_type=F32
    )
    b_ref[96:160, :] = helm[:, 0:128]
    b_ref[160:224, :] = helm[:, 128:256]


def unpack_body(
    me_ref, a_own, a_new, b_own, b_new,
    dense_ref, rhs_ref, helm_ref, vec_ref, small_ref, box_ref, state_ref, ahead_ref, behind_ref,
):
    mine_b = me_ref[0]
    mine_c = me_ref[1]
    place = lanes((1, 128)) // EA

    for tb in range(NB):
        b = mine_b ^ tb
        halves_a, halves_b, where_c = [], [], []
        for tc in range(NB):
            c = mine_c ^ tc
            at_a = tc | (tb << 2)
            at_b = tb | (tc << 2)
            half_a = a_own.at[at_a] if at_a < 8 else a_new.at[at_a - 8]
            half_b = b_own.at[at_b] if at_b < 8 else b_new.at[at_b - 8]
            for t in range(4):
                start = pl.multiple_of((b * 4 + c) * 32, 32)
                dense_ref[pl.ds(start, 32), t * 128 : (t + 1) * 128] = half_a[t * 32 : (t + 1) * 32, :]
            halves_a.append(half_a)
            halves_b.append(half_b)
            where_c.append(c)

        def joined(halves, start, rows, quarter):
            total = None
            for half, c in zip(halves, where_c):
                moved = pltpu.roll(half[start : start + rows, :], ((c - quarter) & 3) * 32, 1)
                part = jnp.where(place == c, moved, 0.0)
                total = part if total is None else total + part
            return total

        for k in range(6):
            rhs_ref[b, k * 48 : (k + 1) * 48, :] = joined(halves_b, 48 * (k // 4), 48, k % 4)
        small_ref[b, :, :] = joined(halves_b, 48, 48, 2)
        for k in range(8):
            helm_ref[b, k * 64 : (k + 1) * 64, :] = joined(halves_b, 96 + 64 * (k // 4), 64, k % 4)
        for t in range(4):
            vec_ref[b, t * 48 : (t + 1) * 48, :] = joined(halves_a, 128, 48, t)

    begin_kernel_part(
        rhs_ref, small_ref, dense_ref, box_ref, state_ref, ahead_ref, behind_ref,
        ([helm_ref[b, 448:512, :] for b in range(NB)], [helm_ref[b, 0:64, :] for b in range(NB)]),
    )


def middle_body(dense_ref, state_ref, left_ref, right_ref, state_out, message_out):
    state, message = sweep_pair(dense_ref, state_ref[...], left_ref[0:16, :], right_ref[0:16, :], 0)
    state_out[...] = state
    message_out[...] = message


def late_body(dense_ref, state_ref, left_ref, right_ref, up_ref, down_ref, state_out, ahead_ref, behind_ref):
    state, message = sweep_pair(dense_ref, state_ref[...], left_ref[...], right_ref[...], 2)
    state_out[...] = state
    ahead_ref[0:16, :] = message
    behind_ref[0:16, :] = message
    ahead_ref[16:80, :] = up_ref[...]
    behind_ref[16:80, :] = down_ref[...]


def join_rows(ref, groups, cross):
    for b in range(NB):
        low = ref[b, pl.ds(0, groups * 8, stride=8), :]
        high = ref[b, pl.ds(7, groups * 8, stride=8), :]
        ref[b, pl.ds(0, groups * 8, stride=8), :] = low + turn(high, 32)
        ref[b, pl.ds(7, groups * 8, stride=8), :] = high + turn(low, -32)
    for b in range(NB - 1):
        for g in range(groups):
            both = ref[b, g * 64 + 56 : g * 64 + 64, :] + ref[b + 1, g * 64 : g * 64 + 8, :]
            ref[b, g * 64 + 56 : g * 64 + 64, :] = both
            ref[b + 1, g * 64 : g * 64 + 8, :] = both


def join_layers(low, high):
    place = lanes(low.shape) % EA
    new_low = low + jnp.where(place > 0, turn(high, 1), 0.0)
    new_high = high + jnp.where(place < EA - 1, turn(low, -1), 0.0)
    return new_low, new_high


def helm_body(helm_ref, left_ref, right_ref, out_ref):
    out_ref[...] = helm_ref[...]
    for b in range(NB):
        low, high = join_layers(helm_ref[b, 0:64, :], helm_ref[b, 448:512, :])
        out_ref[b, 0:64, :] = low + at_first(left_ref[16:80, :], 4 + b)
        out_ref[b, 448:512, :] = high + at_last(right_ref[16:80, :], 4 + b)
    join_rows(out_ref, 8, None)
    for b in range(NB):
        out_ref[b] = 1.0 / out_ref[b]


def schwarz_body(box_ref, vec_ref, small_ref, left_ref, right_ref, out_ref, up_ref, down_ref, one, two, full):
    def element_row(b, carry):
        def row(side, first, second):
            return vec_ref[b, pl.ds(side * 64 + first * 8 + second, 1), :]

        last = pltpu.roll(box_ref[b, 384:448, :], 1, 1)
        first = pltpu.roll(box_ref[b, 64:128, :], 127, 1)
        place = lanes((64, 128)) % EA
        from_left = pltpu.roll(left_ref[16:80, :], 97 + b, 1)
        from_right = pltpu.roll(right_ref[16:80, :], 31 - b, 1)
        one[0] = jnp.where(place == 0, from_left, last).reshape(8, 8, 128)
        one[7] = jnp.where(place == EA - 1, from_right, first).reshape(8, 8, 128)
        one[1:7] = box_ref[b, 64:448, :].reshape(6, 8, 8, 128)
        for m in range(8):
            total = None
            for i in range(8):
                part = one[:, i] * row(0, i, m)[None]
                total = part if total is None else total + part
            two[:, m] = total
        for m in range(8):
            total = None
            for i in range(8):
                part = two[i] * row(2, i, m)[None]
                total = part if total is None else total + part
            one[m] = total
        for k in range(8):
            total = None
            for j in range(8):
                part = one[k, :, j : j + 1, :] * vec_ref[b, 64 + j * 8 : 72 + j * 8, :][None]
                total = part if total is None else total + part
            bottom = small_ref[b, 0:8, :][:, None, :] + small_ref[b, 8:16, :][None, :, :]
            two[k] = total / (bottom + small_ref[b, 16 + k : 17 + k, :][None])
        for k in range(8):
            total = None
            for n in range(8):
                part = two[k, :, n : n + 1, :] * vec_ref[b, pl.ds(64 + n, 8, stride=8), :][None]
                total = part if total is None else total + part
            one[k] = total
        for i in range(8):
            total = None
            for m in range(8):
                part = one[m] * row(2, i, m)[None]
                total = part if total is None else total + part
            two[i] = total
        for i in range(8):
            total = None
            for m in range(8):
                part = two[:, m] * row(0, i, m)[None]
                total = part if total is None else total + part
            one[:, i] = total
        full[b] = one[...].reshape(512, 128)
        return carry

    lax.fori_loop(0, NB, element_row, 0)
    for b in range(NB):
        low = full[b, pl.ds(0, 64, stride=8), :]
        high = full[b, pl.ds(7, 64, stride=8), :]
        full[b, pl.ds(6, 64, stride=8), :] = full[b, pl.ds(6, 64, stride=8), :] + turn(low, -32)
        full[b, pl.ds(1, 64, stride=8), :] = full[b, pl.ds(1, 64, stride=8), :] + turn(high, 32)
        full[b, pl.ds(0, 64, stride=8), :] = jnp.zeros((64, 128), F32)
        full[b, pl.ds(7, 64, stride=8), :] = jnp.zeros((64, 128), F32)
    for b in range(NB - 1):
        for k in range(8):
            full[b, k * 64 + 48 : k * 64 + 56, :] = (
                full[b, k * 64 + 48 : k * 64 + 56, :] + full[b + 1, k * 64 : k * 64 + 8, :]
            )
            full[b + 1, k * 64 + 8 : k * 64 + 16, :] = (
                full[b + 1, k * 64 + 8 : k * 64 + 16, :] + full[b, k * 64 + 56 : k * 64 + 64, :]
            )
    up_ref[...] = pack_last([full[b, 448:512, :] for b in range(NB)])
    down_ref[...] = pack_first([full[b, 0:64, :] for b in range(NB)])
    place = lanes((48, 128)) % EA
    for b in range(NB):
        for k in range(6):
            value = full[b, (k + 1) * 64 + 8 : (k + 1) * 64 + 56, :]
            if k == 0:
                value = value + jnp.where(place > 0, turn(full[b, 456:504, :], 1), 0.0)
            if k == 5:
                value = value + jnp.where(place < EA - 1, turn(full[b, 8:56, :], -1), 0.0)
            out_ref[b, k * 48 : (k + 1) * 48, :] = value


def volume_factors(small_ref, b):
    size = [small_ref[b, 24 + d : 25 + d, :] for d in range(3)]
    volume = size[0] * size[1] * size[2] * 0.125
    return [volume * (2.0 / size[d]) for d in range(3)]


def split_parts(value):
    high = value.astype(BF16)
    return high, (value - high.astype(F32)).astype(BF16)


def gradient_body(
    dense_ref, state_ref, left_ref, right_ref, part_ref, small_ref, table_ref, z_ref, t_ref, ahead_ref, behind_ref
):
    solution = sweep_pair(dense_ref, state_ref[...], left_ref[0:16, :], right_ref[0:16, :], 4)
    inside = lax.broadcasted_iota(jnp.int32, (ROWS_P, 128), 0) % 8
    inside = (inside > 0) & (inside < 7)
    for b in range(NB):
        coarse = jnp.where(inside, solution[b : b + 1, :], 0.0)
        z_ref[b] = part_ref[b] + coarse
        z_ref[b, 0:48, :] = z_ref[b, 0:48, :] + at_first(left_ref[24:72, :], b)
        z_ref[b, 240:288, :] = z_ref[b, 240:288, :] + at_last(right_ref[24:72, :], b)
    parts = [split_parts(z_ref[b]) for b in range(NB)]
    high = jnp.concatenate([part[0] for part in parts], axis=1)
    low = jnp.concatenate([part[1] for part in parts], axis=1)
    both = jnp.concatenate([high, low, high], axis=0)
    factors = [volume_factors(small_ref, b) for b in range(NB)]
    for d in range(3):
        result = jnp.dot(table_ref[d * 512 : (d + 1) * 512, :], both, preferred_element_type=F32)
        for b in range(NB):
            t_ref[b, d * 512 : (d + 1) * 512, :] = result[:, b * 128 : (b + 1) * 128] * factors[b][d]
    join_rows(t_ref, 24, None)
    lows = [t_ref[b, d * 512 : d * 512 + 64, :] for b in range(NB) for d in range(3)]
    highs = [t_ref[b, d * 512 + 448 : d * 512 + 512, :] for b in range(NB) for d in range(3)]
    ahead_ref[...] = pack_last(highs)
    behind_ref[...] = pack_first(lows)
    for b in range(NB):
        for d in range(3):
            low, high = join_layers(lows[b * 3 + d], highs[b * 3 + d])
            t_ref[b, d * 512 : d * 512 + 64, :] = low
            t_ref[b, d * 512 + 448 : d * 512 + 512, :] = high


def divergence_part(t_ref, left_ref, right_ref, inverse_ref, small_ref, table_ref, image_ref, spread):
    for b in range(NB):
        factors = volume_factors(small_ref, b)
        for d in range(3):
            base = d * 512
            for start, rows, extra in (
                (0, 64, at_first(left_ref[...], b * 3 + d)),
                (64, 384, None),
                (448, 64, at_last(right_ref[...], b * 3 + d)),
            ):
                value = t_ref[b, base + start : base + start + rows, :]
                if extra is not None:
                    value = value + extra
                value = value * inverse_ref[b, start : start + rows, :] * factors[d]
                high, low = split_parts(value)
                spread[base + start : base + start + rows, b * 128 : (b + 1) * 128] = high
                spread[1536 + base + start : 1536 + base + start + rows, b * 128 : (b + 1) * 128] = low
    image = jnp.dot(table_ref[:, 0:3072], spread[...], preferred_element_type=F32)
    image = image + jnp.dot(table_ref[:, 3072:4608], spread[0:1536, :], preferred_element_type=F32)
    for b in range(NB):
        image_ref[b] = image[:, b * 128 : (b + 1) * 128]


def first_image_body(
    t_ref, left_ref, right_ref, inverse_ref, small_ref, table_ref, dense_ref,
    image_ref, box_ref, state_ref, ahead_ref, behind_ref, spread,
):
    divergence_part(t_ref, left_ref, right_ref, inverse_ref, small_ref, table_ref, image_ref, spread)
    begin_kernel_part(
        image_ref, small_ref, dense_ref, box_ref, state_ref, ahead_ref, behind_ref, ([], [])
    )


def last_image_body(
    t_ref, left_ref, right_ref, inverse_ref, small_ref, table_ref, r_ref, z_ref, w_ref, q_ref,
    image_ref, sums_ref, spread,
):
    divergence_part(t_ref, left_ref, right_ref, inverse_ref, small_ref, table_ref, image_ref, spread)
    products = ((r_ref, z_ref), (z_ref, w_ref), (w_ref, q_ref), (r_ref, q_ref), (q_ref, image_ref), (z_ref, image_ref))
    sums_ref[...] = jnp.zeros(sums_ref.shape, F32)
    for n, (one, two) in enumerate(products):
        total = None
        for b in range(NB):
            part = jnp.sum(one[b] * two[b], axis=0, keepdims=True)
            total = part if total is None else total + part
        sums_ref[n : n + 1, :] = total


def own_body(me_ref, z_ref, w_ref, q_ref, v_ref, table_ref, z_out, w_out, q_out, v_out):
    mine_b = me_ref[0]
    mine_c = me_ref[1]
    for field_ref, out_ref in ((z_ref, z_out), (w_ref, w_out), (q_ref, q_out), (v_ref, v_out)):
        moved = pltpu.roll(field_ref[mine_b], ((4 - mine_c) & 3) * 32, 1)
        nodes = jnp.concatenate([moved[k * 48 : (k + 1) * 48, 0:32] for k in range(6)], axis=1)
        nodes = jnp.dot(nodes, table_ref[...], precision=HIGHEST, preferred_element_type=F32)
        for i in range(6):
            out_ref[i] = nodes[i * 8 + 1 : i * 8 + 7, :]


def call(body, outs, scratch=(), scalars=0):
    vmem = pl.BlockSpec(memory_space=pltpu.VMEM)
    smem = pl.BlockSpec(memory_space=pltpu.SMEM)

    def run(*operands):
        return pl.pallas_call(
            body,
            out_shape=[jax.ShapeDtypeStruct(shape, F32) for shape in outs],
            in_specs=[smem] * scalars + [vmem] * (len(operands) - scalars),
            out_specs=[vmem] * len(outs),
            scratch_shapes=list(scratch),
            compiler_params=pltpu.CompilerParams(vmem_limit_bytes=40 * 1024 * 1024),
        )(*operands)

    return run


def swap(block, axis, bit):
    count = lax.axis_size(axis)
    return lax.ppermute(block, axis, [(i, i ^ (1 << bit)) for i in range(count)])


def local(divergence, elem_size, helm_diag, fdm_vectors, fdm_values, coarse_rows, axial_link):
    count = lax.axis_size("gx")
    ahead = [(i, (i + 1) % count) for i in range(count)]
    behind = [((i + 1) % count, i) for i in range(count)]

    def exchange(up, down):
        return lax.ppermute(up, "gx", ahead), lax.ppermute(down, "gx", behind)

    forward, backward = gradient_tables()
    six = order_table(6)
    me = jnp.stack([lax.axis_index("gy"), lax.axis_index("col")]).astype(jnp.int32)
    field = (NB, ROWS_P, 128)
    velocity = (NB, ROWS_V, 128)
    state_shape = (16, 128)
    wide = (80, 128)
    plane = (64, 128)

    half_a, half_b = call(
        pack_body, [(ROWS_A, 128), (ROWS_B, 128)], [pltpu.VMEM((48, 192), F32)]
    )(
        divergence,
        helm_diag,
        fdm_vectors.reshape(192, EA),
        fdm_values.reshape(24, EA),
        elem_size,
        coarse_rows,
        axial_link.reshape(1, 1),
        six,
        order_table(8),
    )
    a_own, b_own = half_a[None], half_b[None]
    steps_a = (("col", 0), ("col", 1), ("gy", 0), ("gy", 1))
    steps_b = (("gy", 0), ("gy", 1), ("col", 0), ("col", 1))
    for n in range(4):
        a_new = swap(a_own, *steps_a[n])
        b_new = swap(b_own, *steps_b[n])
        if n < 3:
            a_own = jnp.concatenate([a_own, a_new], axis=0)
            b_own = jnp.concatenate([b_own, b_new], axis=0)

    dense, rhs, helm, vectors, small, boxes, state, up, down = call(
        unpack_body,
        [(512, 512), field, velocity, (NB, 192, 128), (NB, 48, 128), velocity, state_shape, wide, wide],
        scalars=1,
    )(me, a_own, a_new, b_own, b_new)

    def precondition(boxes, state, left, right):
        state, message = call(middle_body, [state_shape, state_shape])(dense, state, left, right)
        left_mid, right_mid = exchange(message, message)
        part, up, down = call(
            schwarz_body,
            [field, plane, plane],
            [pltpu.VMEM((8, 8, 8, 128), F32), pltpu.VMEM((8, 8, 8, 128), F32), pltpu.VMEM(velocity, F32)],
        )(boxes, vectors, small, left, right)
        state, up, down = call(late_body, [state_shape, wide, wide])(
            dense, state, left_mid, right_mid, up, down
        )
        left, right = exchange(up, down)
        z, t, up, down = call(gradient_body, [field, (NB, 1536, 128), plane, plane])(
            dense, state, left, right, part, small, forward
        )
        left, right = exchange(up, down)
        return z, t, left, right

    spread = [pltpu.VMEM((3072, 512), BF16)]
    left, right = exchange(up, down)
    (inverse,) = call(helm_body, [velocity])(helm, left, right)
    z, t, left, right = precondition(boxes, state, left, right)
    w, boxes, state, up, down = call(
        first_image_body, [field, velocity, state_shape, wide, wide], spread
    )(t, left, right, inverse, small, backward, dense)
    left, right = exchange(up, down)
    q, t, left, right = precondition(boxes, state, left, right)
    v, sums = call(last_image_body, [field, (8, 128)], spread)(
        t, left, right, inverse, small, backward, rhs, z, w, q
    )
    own = call(own_body, [(6, 6, 192)] * 4, scalars=1)(me, z, w, q, v, six.T.copy())
    z, w, q, v = own
    for bit in range(count.bit_length() - 1):
        sums = sums + swap(sums, "gx", bit)
    rz, zw, wq, rq, qv, zv = [jnp.sum(sums[n]) for n in range(6)]
    step_first = rz / zw
    rz_next = step_first * (step_first * wq - rq)
    share = 1.0 + rz_next / rz
    curvature = share * share * zw - share * step_first * (zv + wq) + step_first * step_first * qv
    step_next = rz_next / curvature
    z_factor = step_first + step_next * share
    q_factor = step_next * step_first
    pressure = z_factor * z - q_factor * q
    residual = divergence - z_factor * w + q_factor * v
    return (pressure, residual)


def solution(mesh):
    in_specs = (
        P("gy", "col", "gx"),
        P(None, ("gx", "gy", "col")),
        P("gy", "col", "gx"),
        P(None, None, None, ("gx", "gy", "col")),
        P(None, None, ("gx", "gy", "col")),
        P(("gx", "gy", "col"), None),
        P("gx", "gy", "col"),
    )
    out_specs = (P("gy", "col", "gx"), P("gy", "col", "gx"))
    return jax.shard_map(local, mesh=mesh, in_specs=in_specs, out_specs=out_specs, check_vma=False)
```

```python
import jax
import jax.numpy as jnp
import ml_dtypes
import numpy as np
from jax import lax
from jax.experimental import pallas as pl
from jax.experimental.pallas import tpu as pltpu
from jax.sharding import PartitionSpec as P

EA = 32
CHEB = 6
NB = 4

LOBATTO_NODES = [
    -1.0,
    -0.8717401485096066,
    -0.5917001814331423,
    -0.2092992179024789,
    0.2092992179024789,
    0.5917001814331423,
    0.8717401485096066,
    1.0,
]
GAUSS_NODES = [
    -0.932469514203152,
    -0.6612093864662645,
    -0.2386191860831909,
    0.2386191860831909,
    0.6612093864662645,
    0.932469514203152,
]
GAUSS_WEIGHTS = [
    0.1713244923791704,
    0.3607615730481386,
    0.467913934572691,
    0.467913934572691,
    0.3607615730481386,
    0.1713244923791704,
]
SPECTRUM_LOW = 8.0
SPECTRUM_HIGH = 90.0
HIGHEST = lax.Precision.HIGHEST
F32 = jnp.float32
BF16 = jnp.bfloat16

ROWS_P = 288
ROWS_V = 512
ROWS_A = 176
ROWS_B = 224


def basis_tables():
    lobatto = np.array(LOBATTO_NODES)
    points = np.array(GAUSS_NODES)
    interp = np.ones((6, 8))
    slopes = np.zeros((6, 8))
    for p in range(6):
        for m in range(8):
            product = 1.0
            for q in range(8):
                if q != m:
                    product = product * (points[p] - lobatto[q]) / (lobatto[m] - lobatto[q])
            interp[p, m] = product
            running = 0.0
            for q in range(8):
                if q != m:
                    factor = 1.0 / (lobatto[m] - lobatto[q])
                    for k in range(8):
                        if k != m and k != q:
                            factor = factor * (points[p] - lobatto[k]) / (lobatto[m] - lobatto[k])
                    running = running + factor
            slopes[p, m] = running
    return interp, slopes


def gradient_tables():
    interp, slopes = basis_tables()
    weight = np.array(GAUSS_WEIGHTS)
    tables = []
    for comp in range(3):
        sides = [(slopes if side == comp else interp) * weight[:, None] for side in range(3)]
        full = np.zeros((8, 8, 8, 6, 6, 8))
        full[..., 1:7] = np.einsum("iu,jv,kw->wuvkij", sides[0], sides[1], sides[2])
        tables.append(full.reshape(ROWS_V, ROWS_P))
    table = np.concatenate(tables, axis=0).astype(np.float32)
    high = table.astype(ml_dtypes.bfloat16)
    low = (table - high.astype(np.float32)).astype(ml_dtypes.bfloat16)
    forward = np.concatenate([high, high, low], axis=1)
    backward = np.concatenate([high.T, high.T, low.T], axis=1)
    return forward, backward


def order_table(nodes):
    table = np.zeros((nodes * EA, nodes * EA), np.float32)
    for k in range(nodes):
        for a in range(EA):
            table[a * nodes + k, k * EA + a] = 1.0
    return table


def sweep_factors():
    center = (SPECTRUM_HIGH + SPECTRUM_LOW) / 2.0
    spread = (SPECTRUM_HIGH - SPECTRUM_LOW) / 2.0
    ratio_cs = center / spread
    rho_now = 1.0 / ratio_cs
    keep, add = [], []
    for _ in range(CHEB):
        rho_next = 1.0 / (2.0 * ratio_cs - rho_now)
        keep.append(rho_next * rho_now)
        add.append(2.0 * rho_next / spread)
        rho_now = rho_next
    return center, keep, add


CENTER, KEEP, ADD = sweep_factors()


def lanes(shape):
    return lax.broadcasted_iota(jnp.int32, shape, len(shape) - 1)


def turn(value, shift):
    shift = shift % 128
    return value if shift == 0 else pltpu.roll(value, shift, value.ndim - 1)


def at_first(value, slot=0):
    moved = turn(value, 97 + slot)
    return jnp.where(lanes(moved.shape) % EA == 0, moved, 0.0)


def at_last(value, slot=0):
    moved = turn(value, 31 - slot)
    return jnp.where(lanes(moved.shape) % EA == EA - 1, moved, 0.0)


def pack_last(blocks):
    packed = None
    for slot, block in enumerate(blocks):
        part = turn(jnp.where(lanes(block.shape) % EA == EA - 1, block, 0.0), -slot)
        packed = part if packed is None else packed + part
    return packed


def pack_first(blocks):
    packed = None
    for slot, block in enumerate(blocks):
        part = turn(jnp.where(lanes(block.shape) % EA == 0, block, 0.0), slot)
        packed = part if packed is None else packed + part
    return packed


def times(dense_ref, vector):
    columns = jnp.concatenate([vector, jnp.zeros_like(vector)], axis=0).T
    total = None
    for b in range(NB):
        part = dense_ref[b * 128 : (b + 1) * 128, :] * columns[:, b : b + 1]
        total = part if total is None else total + part
    row = jnp.sum(total, axis=0, keepdims=True)
    return jnp.concatenate([row[:, b * 128 : (b + 1) * 128] for b in range(NB)], axis=0)


def sweep_begin(dense_ref, source, link):
    update = source * (1.0 / CENTER)
    remainder = source - times(dense_ref, update)
    free = KEEP[0] * update + ADD[0] * remainder
    state = jnp.concatenate([update, remainder, update, link], axis=0)
    return state, jnp.concatenate([update, free, link, link], axis=0)


def sweep_pair(dense_ref, state, from_left, from_right, sweep_at):
    update, remainder, solution, link = [state[4 * n : 4 * n + 4] for n in range(4)]
    left = at_first(from_left)
    right = at_last(from_right)
    place = lanes(update.shape) % EA
    link_left = left[8:12]
    link_right = jnp.where(place == EA - 1, link, 0.0)
    remainder = remainder + link_left * left[0:4] + link_right * right[0:4]
    left_next = left[4:8] + ADD[sweep_at] * link_left * update
    right_next = right[4:8] + ADD[sweep_at] * link_right * update
    update = KEEP[sweep_at] * update + ADD[sweep_at] * remainder
    solution = solution + update
    remainder = remainder - times(dense_ref, update)
    remainder = remainder + link_left * left_next + link_right * right_next
    update = KEEP[sweep_at + 1] * update + ADD[sweep_at + 1] * remainder
    solution = solution + update
    if sweep_at + 2 == CHEB:
        return solution
    remainder = remainder - times(dense_ref, update)
    free = KEEP[sweep_at + 2] * update + ADD[sweep_at + 2] * remainder
    state = jnp.concatenate([update, remainder, solution, link], axis=0)
    return state, jnp.concatenate([update, free, link, link], axis=0)


def fill_boxes(field_ref, box_ref):
    box_ref[...] = jnp.zeros(box_ref.shape, F32)
    for b in range(NB):
        for k in range(6):
            box_ref[b, (k + 1) * 64 + 8 : (k + 1) * 64 + 56, :] = field_ref[b, k * 48 : (k + 1) * 48, :]
        before = box_ref[b, pl.ds(6, 64, stride=8), :]
        after = box_ref[b, pl.ds(1, 64, stride=8), :]
        box_ref[b, pl.ds(0, 64, stride=8), :] = turn(before, 32)
        box_ref[b, pl.ds(7, 64, stride=8), :] = turn(after, -32)
    for b in range(NB):
        for k in range(1, 7):
            if b > 0:
                box_ref[b, k * 64 : k * 64 + 8, :] = box_ref[b - 1, k * 64 + 48 : k * 64 + 56, :]
            if b < NB - 1:
                box_ref[b, k * 64 + 56 : k * 64 + 64, :] = box_ref[b + 1, k * 64 + 8 : k * 64 + 16, :]


def begin_kernel_part(field_ref, small_ref, dense_ref, box_ref, state_ref, ahead_ref, behind_ref, extra):
    fill_boxes(field_ref, box_ref)
    source = jnp.concatenate(
        [jnp.sum(field_ref[b], axis=0, keepdims=True) for b in range(NB)], axis=0
    )
    link = jnp.concatenate([small_ref[b, 32:33, :] for b in range(NB)], axis=0)
    state, message = sweep_begin(dense_ref, source, link)
    state_ref[...] = state
    ahead_ref[0:16, :] = message
    behind_ref[0:16, :] = message
    ahead_ref[16:80, :] = pack_last([box_ref[b, 384:448, :] for b in range(NB)] + extra[0])
    behind_ref[16:80, :] = pack_first([box_ref[b, 64:128, :] for b in range(NB)] + extra[1])


def pack_body(*refs):
    sources, (a_ref, b_ref), held, (tmp, ready) = refs[:9], refs[9:11], refs[11:20], refs[20:]
    copies = [pltpu.make_async_copy(sources[n], held[n], ready.at[n]) for n in range(9)]
    for copy in copies:
        copy.start()
    for copy in copies:
        copy.wait()
    rhs_ref, helm_ref, vec_ref, val_ref, size_ref, rows_ref, link_ref, six_ref, eight_ref = held
    for t in range(4):
        a_ref[t * 32 : (t + 1) * 32, :] = rows_ref[:, t * 128 : (t + 1) * 128]
        a_ref[128:176, t * 32 : (t + 1) * 32] = vec_ref[t * 48 : (t + 1) * 48, :]
    tmp[...] = jnp.zeros(tmp.shape, F32)
    for i in range(6):
        tmp[i * 8 + 1 : i * 8 + 7, :] = rhs_ref[i]
    nodes = jnp.dot(tmp[...], six_ref[...], precision=HIGHEST, preferred_element_type=F32)
    b_ref[0:48, :] = nodes[:, 0:128]
    b_ref[48:96, :] = jnp.zeros((48, 128), F32)
    b_ref[48:96, 0:64] = nodes[:, 128:192]
    b_ref[48:72, 64:96] = val_ref[...]
    b_ref[72:75, 64:96] = size_ref[...]
    b_ref[80:81, 64:96] = jnp.broadcast_to(link_ref[0], (1, 32))
    helm = jnp.dot(
        helm_ref[...].reshape(64, 256), eight_ref[...], precision=HIGHEST, preferred_element_type=F32
    )
    b_ref[96:160, :] = helm[:, 0:128]
    b_ref[160:224, :] = helm[:, 128:256]


def unpack_body(
    me_ref, a_0, a_1, a_2, a_3, b_0, b_1, b_2, b_3,
    dense_ref, rhs_ref, helm_ref, vec_ref, small_ref, box_ref, state_ref, ahead_ref, behind_ref,
):
    mine_b = me_ref[0]
    mine_c = me_ref[1]
    place = lanes((1, 128)) // EA

    for tb in range(NB):
        b = mine_b ^ tb
        halves_a, halves_b, where_c = [], [], []
        for tc in range(NB):
            c = mine_c ^ tc
            half_a = (a_0, a_1, a_2, a_3)[tb].at[tc]
            half_b = (b_0, b_1, b_2, b_3)[tc].at[tb]
            for t in range(4):
                start = pl.multiple_of((b * 4 + c) * 32, 32)
                dense_ref[pl.ds(start, 32), t * 128 : (t + 1) * 128] = half_a[t * 32 : (t + 1) * 32, :]
            halves_a.append(half_a)
            halves_b.append(half_b)
            where_c.append(c)

        def joined(halves, start, rows, quarter):
            total = None
            for half, c in zip(halves, where_c):
                moved = pltpu.roll(half[start : start + rows, :], ((c - quarter) & 3) * 32, 1)
                part = jnp.where(place == c, moved, 0.0)
                total = part if total is None else total + part
            return total

        for k in range(6):
            rhs_ref[b, k * 48 : (k + 1) * 48, :] = joined(halves_b, 48 * (k // 4), 48, k % 4)
        small_ref[b, :, :] = joined(halves_b, 48, 48, 2)
        for k in range(8):
            helm_ref[b, k * 64 : (k + 1) * 64, :] = joined(halves_b, 96 + 64 * (k // 4), 64, k % 4)
        for t in range(4):
            vec_ref[b, t * 48 : (t + 1) * 48, :] = joined(halves_a, 128, 48, t)

    begin_kernel_part(
        rhs_ref, small_ref, dense_ref, box_ref, state_ref, ahead_ref, behind_ref,
        ([helm_ref[b, 448:512, :] for b in range(NB)], [helm_ref[b, 0:64, :] for b in range(NB)]),
    )


def middle_body(dense_ref, state_ref, left_ref, right_ref, state_out, message_out):
    state, message = sweep_pair(dense_ref, state_ref[...], left_ref[0:16, :], right_ref[0:16, :], 0)
    state_out[...] = state
    message_out[...] = message


def late_body(dense_ref, state_ref, left_ref, right_ref, up_ref, down_ref, state_out, ahead_ref, behind_ref):
    state, message = sweep_pair(dense_ref, state_ref[...], left_ref[...], right_ref[...], 2)
    state_out[...] = state
    ahead_ref[0:16, :] = message
    behind_ref[0:16, :] = message
    ahead_ref[16:80, :] = up_ref[...]
    behind_ref[16:80, :] = down_ref[...]


def join_rows(ref, groups, cross):
    for b in range(NB):
        low = ref[b, pl.ds(0, groups * 8, stride=8), :]
        high = ref[b, pl.ds(7, groups * 8, stride=8), :]
        ref[b, pl.ds(0, groups * 8, stride=8), :] = low + turn(high, 32)
        ref[b, pl.ds(7, groups * 8, stride=8), :] = high + turn(low, -32)
    for b in range(NB - 1):
        for g in range(groups):
            both = ref[b, g * 64 + 56 : g * 64 + 64, :] + ref[b + 1, g * 64 : g * 64 + 8, :]
            ref[b, g * 64 + 56 : g * 64 + 64, :] = both
            ref[b + 1, g * 64 : g * 64 + 8, :] = both


def join_layers(low, high):
    place = lanes(low.shape) % EA
    new_low = low + jnp.where(place > 0, turn(high, 1), 0.0)
    new_high = high + jnp.where(place < EA - 1, turn(low, -1), 0.0)
    return new_low, new_high


def helm_body(helm_ref, left_ref, right_ref, out_ref):
    out_ref[...] = helm_ref[...]
    for b in range(NB):
        low, high = join_layers(helm_ref[b, 0:64, :], helm_ref[b, 448:512, :])
        out_ref[b, 0:64, :] = low + at_first(left_ref[16:80, :], 4 + b)
        out_ref[b, 448:512, :] = high + at_last(right_ref[16:80, :], 4 + b)
    join_rows(out_ref, 8, None)
    for b in range(NB):
        out_ref[b] = 1.0 / out_ref[b]


def schwarz_body(box_ref, vec_ref, small_ref, left_ref, right_ref, out_ref, up_ref, down_ref, one, two, full):
    def element_row(b, carry):
        def row(side, first, second):
            return vec_ref[b, pl.ds(side * 64 + first * 8 + second, 1), :]

        last = pltpu.roll(box_ref[b, 384:448, :], 1, 1)
        first = pltpu.roll(box_ref[b, 64:128, :], 127, 1)
        place = lanes((64, 128)) % EA
        from_left = pltpu.roll(left_ref[16:80, :], 97 + b, 1)
        from_right = pltpu.roll(right_ref[16:80, :], 31 - b, 1)
        one[0] = jnp.where(place == 0, from_left, last).reshape(8, 8, 128)
        one[7] = jnp.where(place == EA - 1, from_right, first).reshape(8, 8, 128)
        one[1:7] = box_ref[b, 64:448, :].reshape(6, 8, 8, 128)
        for m in range(8):
            total = None
            for i in range(8):
                part = one[:, i] * row(0, i, m)[None]
                total = part if total is None else total + part
            two[:, m] = total
        for m in range(8):
            total = None
            for i in range(8):
                part = two[i] * row(2, i, m)[None]
                total = part if total is None else total + part
            one[m] = total
        for k in range(8):
            total = None
            for j in range(8):
                part = one[k, :, j : j + 1, :] * vec_ref[b, 64 + j * 8 : 72 + j * 8, :][None]
                total = part if total is None else total + part
            bottom = small_ref[b, 0:8, :][:, None, :] + small_ref[b, 8:16, :][None, :, :]
            two[k] = total / (bottom + small_ref[b, 16 + k : 17 + k, :][None])
        for k in range(8):
            total = None
            for n in range(8):
                part = two[k, :, n : n + 1, :] * vec_ref[b, pl.ds(64 + n, 8, stride=8), :][None]
                total = part if total is None else total + part
            one[k] = total
        for i in range(8):
            total = None
            for m in range(8):
                part = one[m] * row(2, i, m)[None]
                total = part if total is None else total + part
            two[i] = total
        for i in range(8):
            total = None
            for m in range(8):
                part = two[:, m] * row(0, i, m)[None]
                total = part if total is None else total + part
            one[:, i] = total
        full[b] = one[...].reshape(512, 128)
        return carry

    lax.fori_loop(0, NB, element_row, 0)
    for b in range(NB):
        low = full[b, pl.ds(0, 64, stride=8), :]
        high = full[b, pl.ds(7, 64, stride=8), :]
        full[b, pl.ds(6, 64, stride=8), :] = full[b, pl.ds(6, 64, stride=8), :] + turn(low, -32)
        full[b, pl.ds(1, 64, stride=8), :] = full[b, pl.ds(1, 64, stride=8), :] + turn(high, 32)
        full[b, pl.ds(0, 64, stride=8), :] = jnp.zeros((64, 128), F32)
        full[b, pl.ds(7, 64, stride=8), :] = jnp.zeros((64, 128), F32)
    for b in range(NB - 1):
        for k in range(8):
            full[b, k * 64 + 48 : k * 64 + 56, :] = (
                full[b, k * 64 + 48 : k * 64 + 56, :] + full[b + 1, k * 64 : k * 64 + 8, :]
            )
            full[b + 1, k * 64 + 8 : k * 64 + 16, :] = (
                full[b + 1, k * 64 + 8 : k * 64 + 16, :] + full[b, k * 64 + 56 : k * 64 + 64, :]
            )
    up_ref[...] = pack_last([full[b, 448:512, :] for b in range(NB)])
    down_ref[...] = pack_first([full[b, 0:64, :] for b in range(NB)])
    place = lanes((48, 128)) % EA
    for b in range(NB):
        for k in range(6):
            value = full[b, (k + 1) * 64 + 8 : (k + 1) * 64 + 56, :]
            if k == 0:
                value = value + jnp.where(place > 0, turn(full[b, 456:504, :], 1), 0.0)
            if k == 5:
                value = value + jnp.where(place < EA - 1, turn(full[b, 8:56, :], -1), 0.0)
            out_ref[b, k * 48 : (k + 1) * 48, :] = value


def volume_factors(small_ref, b):
    size = [small_ref[b, 24 + d : 25 + d, :] for d in range(3)]
    volume = size[0] * size[1] * size[2] * 0.125
    return [volume * (2.0 / size[d]) for d in range(3)]


def split_parts(value):
    high = value.astype(BF16)
    return high, (value - high.astype(F32)).astype(BF16)


def gradient_body(
    dense_ref, state_ref, left_ref, right_ref, part_ref, small_ref, table_ref, z_ref, t_ref, ahead_ref, behind_ref
):
    solution = sweep_pair(dense_ref, state_ref[...], left_ref[0:16, :], right_ref[0:16, :], 4)
    inside = lax.broadcasted_iota(jnp.int32, (ROWS_P, 128), 0) % 8
    inside = (inside > 0) & (inside < 7)
    for b in range(NB):
        coarse = jnp.where(inside, solution[b : b + 1, :], 0.0)
        z_ref[b] = part_ref[b] + coarse
        z_ref[b, 0:48, :] = z_ref[b, 0:48, :] + at_first(left_ref[24:72, :], b)
        z_ref[b, 240:288, :] = z_ref[b, 240:288, :] + at_last(right_ref[24:72, :], b)
    parts = [split_parts(z_ref[b]) for b in range(NB)]
    high = jnp.concatenate([part[0] for part in parts], axis=1)
    low = jnp.concatenate([part[1] for part in parts], axis=1)
    both = jnp.concatenate([high, low, high], axis=0)
    factors = [volume_factors(small_ref, b) for b in range(NB)]
    for d in range(3):
        result = jnp.dot(table_ref[d * 512 : (d + 1) * 512, :], both, preferred_element_type=F32)
        for b in range(NB):
            t_ref[b, d * 512 : (d + 1) * 512, :] = result[:, b * 128 : (b + 1) * 128] * factors[b][d]
    join_rows(t_ref, 24, None)
    lows = [t_ref[b, d * 512 : d * 512 + 64, :] for b in range(NB) for d in range(3)]
    highs = [t_ref[b, d * 512 + 448 : d * 512 + 512, :] for b in range(NB) for d in range(3)]
    ahead_ref[...] = pack_last(highs)
    behind_ref[...] = pack_first(lows)
    for b in range(NB):
        for d in range(3):
            low, high = join_layers(lows[b * 3 + d], highs[b * 3 + d])
            t_ref[b, d * 512 : d * 512 + 64, :] = low
            t_ref[b, d * 512 + 448 : d * 512 + 512, :] = high


def divergence_part(t_ref, left_ref, right_ref, inverse_ref, small_ref, table_ref, image_ref, spread):
    for b in range(NB):
        factors = volume_factors(small_ref, b)
        for d in range(3):
            base = d * 512
            for start, rows, extra in (
                (0, 64, at_first(left_ref[...], b * 3 + d)),
                (64, 384, None),
                (448, 64, at_last(right_ref[...], b * 3 + d)),
            ):
                value = t_ref[b, base + start : base + start + rows, :]
                if extra is not None:
                    value = value + extra
                value = value * inverse_ref[b, start : start + rows, :] * factors[d]
                high, low = split_parts(value)
                spread[base + start : base + start + rows, b * 128 : (b + 1) * 128] = high
                spread[1536 + base + start : 1536 + base + start + rows, b * 128 : (b + 1) * 128] = low
    image = jnp.dot(table_ref[:, 0:3072], spread[...], preferred_element_type=F32)
    image = image + jnp.dot(table_ref[:, 3072:4608], spread[0:1536, :], preferred_element_type=F32)
    for b in range(NB):
        image_ref[b] = image[:, b * 128 : (b + 1) * 128]


def first_image_body(
    t_ref, left_ref, right_ref, inverse_ref, small_ref, table_ref, dense_ref,
    image_ref, box_ref, state_ref, ahead_ref, behind_ref, spread,
):
    divergence_part(t_ref, left_ref, right_ref, inverse_ref, small_ref, table_ref, image_ref, spread)
    begin_kernel_part(
        image_ref, small_ref, dense_ref, box_ref, state_ref, ahead_ref, behind_ref, ([], [])
    )


def last_image_body(
    t_ref, left_ref, right_ref, inverse_ref, small_ref, table_ref, r_ref, z_ref, w_ref, q_ref,
    image_ref, sums_ref, spread,
):
    divergence_part(t_ref, left_ref, right_ref, inverse_ref, small_ref, table_ref, image_ref, spread)
    products = ((r_ref, z_ref), (z_ref, w_ref), (w_ref, q_ref), (r_ref, q_ref), (q_ref, image_ref), (z_ref, image_ref))
    sums_ref[...] = jnp.zeros(sums_ref.shape, F32)
    for n, (one, two) in enumerate(products):
        total = None
        for b in range(NB):
            part = jnp.sum(one[b] * two[b], axis=0, keepdims=True)
            total = part if total is None else total + part
        sums_ref[n : n + 1, :] = total


def own_body(me_ref, z_ref, w_ref, q_ref, v_ref, table_ref, z_out, w_out, q_out, v_out):
    mine_b = me_ref[0]
    mine_c = me_ref[1]
    for field_ref, out_ref in ((z_ref, z_out), (w_ref, w_out), (q_ref, q_out), (v_ref, v_out)):
        moved = pltpu.roll(field_ref[mine_b], ((4 - mine_c) & 3) * 32, 1)
        nodes = jnp.concatenate([moved[k * 48 : (k + 1) * 48, 0:32] for k in range(6)], axis=1)
        nodes = jnp.dot(nodes, table_ref[...], precision=HIGHEST, preferred_element_type=F32)
        for i in range(6):
            out_ref[i] = nodes[i * 8 + 1 : i * 8 + 7, :]


def last_body(
    sums_ref, z_ref, w_ref, q_ref, v_ref, rhs_ref, pressure_ref, residual_ref, pressure, residual, done
):
    totals = jnp.sum(sums_ref[...], axis=1, keepdims=True)
    rz, zw, wq, rq, qv, zv = [totals[n : n + 1] for n in range(6)]
    step_first = rz / zw
    rz_next = step_first * (step_first * wq - rq)
    share = 1.0 + rz_next / rz
    curvature = share * share * zw - share * step_first * (zv + wq) + step_first * step_first * qv
    step_next = rz_next / curvature
    z_factor = (step_first + step_next * share)[None]
    q_factor = (step_next * step_first)[None]
    pressure[...] = z_factor * z_ref[...] - q_factor * q_ref[...]
    first = pltpu.make_async_copy(pressure, pressure_ref, done.at[0])
    first.start()
    residual[...] = rhs_ref[...] - z_factor * w_ref[...] + q_factor * v_ref[...]
    second = pltpu.make_async_copy(residual, residual_ref, done.at[1])
    second.start()
    first.wait()
    second.wait()


def call(body, outs, scratch=(), scalars=0):
    vmem = pl.BlockSpec(memory_space=pltpu.VMEM)
    smem = pl.BlockSpec(memory_space=pltpu.SMEM)

    def run(*operands):
        return pl.pallas_call(
            body,
            out_shape=[jax.ShapeDtypeStruct(shape, F32) for shape in outs],
            in_specs=[smem] * scalars + [vmem] * (len(operands) - scalars),
            out_specs=[vmem] * len(outs),
            scratch_shapes=list(scratch),
            compiler_params=pltpu.CompilerParams(vmem_limit_bytes=40 * 1024 * 1024),
        )(*operands)

    return run


def swap(block, axis, mask):
    count = lax.axis_size(axis)
    return lax.ppermute(block, axis, [(i, i ^ mask) for i in range(count)])


def sum_slabs(sums):
    slabs, across, around = (lax.axis_size(axis) for axis in ("gx", "gy", "col"))
    sums = sums + swap(sums, "gx", 1)
    group = across * around
    chips = slabs // 2
    span = -(-chips // group)
    total = None
    for round_at in range(span):
        pairs = []
        for slab in range(slabs):
            for n in range(group):
                away = n + group * round_at
                if away < chips:
                    source = (slab // 2 + away) % chips * 2 + slab % 2
                    pairs.append((source * group + n, slab * group + n))
        part = lax.ppermute(sums, ("gx", "gy", "col"), pairs)
        total = part if total is None else total + part
    for axis in ("col", "gy"):
        first, second, third = [swap(total, axis, n) for n in (1, 2, 3)]
        total = (total + first) + (second + third)
    return total


def local(divergence, elem_size, helm_diag, fdm_vectors, fdm_values, coarse_rows, axial_link):
    count = lax.axis_size("gx")
    ahead = [(i, (i + 1) % count) for i in range(count)]
    behind = [((i + 1) % count, i) for i in range(count)]

    def exchange(up, down):
        return lax.ppermute(up, "gx", ahead), lax.ppermute(down, "gx", behind)

    forward, backward = gradient_tables()
    six = order_table(6)
    me = jnp.stack([lax.axis_index("gy"), lax.axis_index("col")]).astype(jnp.int32)
    field = (NB, ROWS_P, 128)
    velocity = (NB, ROWS_V, 128)
    state_shape = (16, 128)
    wide = (80, 128)
    plane = (64, 128)

    arguments = (
        divergence,
        helm_diag,
        fdm_vectors.reshape(192, EA),
        fdm_values.reshape(24, EA),
        elem_size,
        coarse_rows,
        axial_link,
        six,
        order_table(8),
    )
    half_a, half_b = pl.pallas_call(
        pack_body,
        out_shape=[jax.ShapeDtypeStruct((rows, 128), F32) for rows in (ROWS_A, ROWS_B)],
        in_specs=[pl.BlockSpec(memory_space=pl.ANY)] * 9,
        out_specs=[pl.BlockSpec(memory_space=pltpu.VMEM)] * 2,
        scratch_shapes=[pltpu.VMEM(value.shape, F32) for value in arguments]
        + [pltpu.VMEM((48, 192), F32), pltpu.SemaphoreType.DMA((9,))],
        compiler_params=pltpu.CompilerParams(vmem_limit_bytes=60 * 1024 * 1024),
    )(*arguments)
    stack_a = [half_a] + [swap(half_a, "col", n) for n in (1, 2, 3)]
    stack_b = [half_b] + [swap(half_b, "gy", n) for n in (1, 2, 3)]
    stack_a, stack_b = lax.optimization_barrier((stack_a, stack_b))
    four_a, four_b = jnp.stack(stack_a), jnp.stack(stack_b)
    parts_a = [four_a] + [swap(four_a, "gy", n) for n in (1, 2, 3)]
    parts_b = [four_b] + [swap(four_b, "col", n) for n in (1, 2, 3)]

    dense, rhs, helm, vectors, small, boxes, state, up, down = call(
        unpack_body,
        [(512, 512), field, velocity, (NB, 192, 128), (NB, 48, 128), velocity, state_shape, wide, wide],
        scalars=1,
    )(me, *parts_a, *parts_b)

    def precondition(boxes, state, left, right):
        state, message = call(middle_body, [state_shape, state_shape])(dense, state, left, right)
        left_mid, right_mid = exchange(message, message)
        part, up, down = call(
            schwarz_body,
            [field, plane, plane],
            [pltpu.VMEM((8, 8, 8, 128), F32), pltpu.VMEM((8, 8, 8, 128), F32), pltpu.VMEM(velocity, F32)],
        )(boxes, vectors, small, left, right)
        state, up, down = call(late_body, [state_shape, wide, wide])(
            dense, state, left_mid, right_mid, up, down
        )
        left, right = exchange(up, down)
        z, t, up, down = call(gradient_body, [field, (NB, 1536, 128), plane, plane])(
            dense, state, left, right, part, small, forward
        )
        left, right = exchange(up, down)
        return z, t, left, right

    spread = [pltpu.VMEM((3072, 512), BF16)]
    left, right = exchange(up, down)
    (inverse,) = call(helm_body, [velocity])(helm, left, right)
    z, t, left, right = precondition(boxes, state, left, right)
    w, boxes, state, up, down = call(
        first_image_body, [field, velocity, state_shape, wide, wide], spread
    )(t, left, right, inverse, small, backward, dense)
    left, right = exchange(up, down)
    q, t, left, right = precondition(boxes, state, left, right)
    v, sums = call(last_image_body, [field, (8, 128)], spread)(
        t, left, right, inverse, small, backward, rhs, z, w, q
    )
    own = call(own_body, [(6, 6, 192)] * 4, scalars=1)(me, z, w, q, v, six.T.copy())
    sums = sum_slabs(sums)
    return tuple(
        pl.pallas_call(
            last_body,
            out_shape=[jax.ShapeDtypeStruct((6, 6, 192), F32)] * 2,
            in_specs=[pl.BlockSpec(memory_space=pltpu.VMEM)] * 6,
            out_specs=[pl.BlockSpec(memory_space=pl.ANY)] * 2,
            scratch_shapes=[pltpu.VMEM((6, 6, 192), F32)] * 2 + [pltpu.SemaphoreType.DMA((2,))],
            compiler_params=pltpu.CompilerParams(vmem_limit_bytes=40 * 1024 * 1024),
        )(sums, *own, divergence)
    )


def solution(mesh):
    in_specs = (
        P("gy", "col", "gx"),
        P(None, ("gx", "gy", "col")),
        P("gy", "col", "gx"),
        P(None, None, None, ("gx", "gy", "col")),
        P(None, None, ("gx", "gy", "col")),
        P(("gx", "gy", "col"), None),
        P("gx", "gy", "col"),
    )
    out_specs = (P("gy", "col", "gx"), P("gy", "col", "gx"))
    return jax.shard_map(local, mesh=mesh, in_specs=in_specs, out_specs=out_specs, check_vma=False)
```

```python
import jax
import jax.numpy as jnp
import ml_dtypes
import numpy as np
from jax import lax
from jax.experimental import pallas as pl
from jax.experimental.pallas import tpu as pltpu
from jax.sharding import PartitionSpec as P

EA = 32
CHEB = 6
NB = 4

LOBATTO_NODES = [
    -1.0,
    -0.8717401485096066,
    -0.5917001814331423,
    -0.2092992179024789,
    0.2092992179024789,
    0.5917001814331423,
    0.8717401485096066,
    1.0,
]
GAUSS_NODES = [
    -0.932469514203152,
    -0.6612093864662645,
    -0.2386191860831909,
    0.2386191860831909,
    0.6612093864662645,
    0.932469514203152,
]
GAUSS_WEIGHTS = [
    0.1713244923791704,
    0.3607615730481386,
    0.467913934572691,
    0.467913934572691,
    0.3607615730481386,
    0.1713244923791704,
]
SPECTRUM_LOW = 8.0
SPECTRUM_HIGH = 90.0
HIGHEST = lax.Precision.HIGHEST
F32 = jnp.float32
BF16 = jnp.bfloat16

ROWS_P = 288
ROWS_V = 512
ROWS_A = 176
ROWS = 400


def basis_tables():
    lobatto = np.array(LOBATTO_NODES)
    points = np.array(GAUSS_NODES)
    interp = np.ones((6, 8))
    slopes = np.zeros((6, 8))
    for p in range(6):
        for m in range(8):
            product = 1.0
            for q in range(8):
                if q != m:
                    product = product * (points[p] - lobatto[q]) / (lobatto[m] - lobatto[q])
            interp[p, m] = product
            running = 0.0
            for q in range(8):
                if q != m:
                    factor = 1.0 / (lobatto[m] - lobatto[q])
                    for k in range(8):
                        if k != m and k != q:
                            factor = factor * (points[p] - lobatto[k]) / (lobatto[m] - lobatto[k])
                    running = running + factor
            slopes[p, m] = running
    return interp, slopes


def gradient_tables():
    interp, slopes = basis_tables()
    weight = np.array(GAUSS_WEIGHTS)
    tables = []
    for comp in range(3):
        sides = [(slopes if side == comp else interp) * weight[:, None] for side in range(3)]
        full = np.zeros((8, 8, 8, 6, 6, 8))
        full[..., 1:7] = np.einsum("iu,jv,kw->wuvkij", sides[0], sides[1], sides[2])
        tables.append(full.reshape(ROWS_V, ROWS_P))
    table = np.concatenate(tables, axis=0).astype(np.float32)
    high = table.astype(ml_dtypes.bfloat16)
    low = (table - high.astype(np.float32)).astype(ml_dtypes.bfloat16)
    forward = np.concatenate([high, high, low], axis=1)
    backward = np.concatenate([high.T, high.T, low.T], axis=1)
    return forward, backward


def order_table(nodes):
    table = np.zeros((nodes * EA, nodes * EA), np.float32)
    for k in range(nodes):
        for a in range(EA):
            table[a * nodes + k, k * EA + a] = 1.0
    return table


def sweep_factors():
    center = (SPECTRUM_HIGH + SPECTRUM_LOW) / 2.0
    spread = (SPECTRUM_HIGH - SPECTRUM_LOW) / 2.0
    ratio_cs = center / spread
    rho_now = 1.0 / ratio_cs
    keep, add = [], []
    for _ in range(CHEB):
        rho_next = 1.0 / (2.0 * ratio_cs - rho_now)
        keep.append(rho_next * rho_now)
        add.append(2.0 * rho_next / spread)
        rho_now = rho_next
    return center, keep, add


CENTER, KEEP, ADD = sweep_factors()


def lanes(shape):
    return lax.broadcasted_iota(jnp.int32, shape, len(shape) - 1)


def turn(value, shift):
    shift = shift % 128
    return value if shift == 0 else pltpu.roll(value, shift, value.ndim - 1)


def at_first(value, slot=0):
    moved = turn(value, 97 + slot)
    return jnp.where(lanes(moved.shape) % EA == 0, moved, 0.0)


def at_last(value, slot=0):
    moved = turn(value, 31 - slot)
    return jnp.where(lanes(moved.shape) % EA == EA - 1, moved, 0.0)


def pack_last(blocks):
    packed = None
    for slot, block in enumerate(blocks):
        part = turn(jnp.where(lanes(block.shape) % EA == EA - 1, block, 0.0), -slot)
        packed = part if packed is None else packed + part
    return packed


def pack_first(blocks):
    packed = None
    for slot, block in enumerate(blocks):
        part = turn(jnp.where(lanes(block.shape) % EA == 0, block, 0.0), slot)
        packed = part if packed is None else packed + part
    return packed


def times(dense_ref, vector):
    columns = jnp.concatenate([vector, jnp.zeros_like(vector)], axis=0).T
    total = None
    for b in range(NB):
        part = dense_ref[b * 128 : (b + 1) * 128, :] * columns[:, b : b + 1]
        total = part if total is None else total + part
    row = jnp.sum(total, axis=0, keepdims=True)
    return jnp.concatenate([row[:, b * 128 : (b + 1) * 128] for b in range(NB)], axis=0)


def sweep_begin(dense_ref, source, link):
    update = source * (1.0 / CENTER)
    remainder = source - times(dense_ref, update)
    free = KEEP[0] * update + ADD[0] * remainder
    state = jnp.concatenate([update, remainder, update, link], axis=0)
    return state, jnp.concatenate([update, free, link, link], axis=0)


def sweep_pair(dense_ref, state, from_left, from_right, sweep_at):
    update, remainder, solution, link = [state[4 * n : 4 * n + 4] for n in range(4)]
    left = at_first(from_left)
    right = at_last(from_right)
    place = lanes(update.shape) % EA
    link_left = left[8:12]
    link_right = jnp.where(place == EA - 1, link, 0.0)
    remainder = remainder + link_left * left[0:4] + link_right * right[0:4]
    left_next = left[4:8] + ADD[sweep_at] * link_left * update
    right_next = right[4:8] + ADD[sweep_at] * link_right * update
    update = KEEP[sweep_at] * update + ADD[sweep_at] * remainder
    solution = solution + update
    remainder = remainder - times(dense_ref, update)
    remainder = remainder + link_left * left_next + link_right * right_next
    update = KEEP[sweep_at + 1] * update + ADD[sweep_at + 1] * remainder
    solution = solution + update
    if sweep_at + 2 == CHEB:
        return solution
    remainder = remainder - times(dense_ref, update)
    free = KEEP[sweep_at + 2] * update + ADD[sweep_at + 2] * remainder
    state = jnp.concatenate([update, remainder, solution, link], axis=0)
    return state, jnp.concatenate([update, free, link, link], axis=0)


def fill_boxes(field_ref, box_ref):
    box_ref[...] = jnp.zeros(box_ref.shape, F32)
    for b in range(NB):
        for k in range(6):
            box_ref[b, (k + 1) * 64 + 8 : (k + 1) * 64 + 56, :] = field_ref[b, k * 48 : (k + 1) * 48, :]
        before = box_ref[b, pl.ds(6, 64, stride=8), :]
        after = box_ref[b, pl.ds(1, 64, stride=8), :]
        box_ref[b, pl.ds(0, 64, stride=8), :] = turn(before, 32)
        box_ref[b, pl.ds(7, 64, stride=8), :] = turn(after, -32)
    for b in range(NB):
        for k in range(1, 7):
            if b > 0:
                box_ref[b, k * 64 : k * 64 + 8, :] = box_ref[b - 1, k * 64 + 48 : k * 64 + 56, :]
            if b < NB - 1:
                box_ref[b, k * 64 + 56 : k * 64 + 64, :] = box_ref[b + 1, k * 64 + 8 : k * 64 + 16, :]


def begin_kernel_part(field_ref, small_ref, dense_ref, box_ref, state_ref, ahead_ref, behind_ref, extra):
    fill_boxes(field_ref, box_ref)
    source = jnp.concatenate(
        [jnp.sum(field_ref[b], axis=0, keepdims=True) for b in range(NB)], axis=0
    )
    link = jnp.concatenate([small_ref[b, 32:33, :] for b in range(NB)], axis=0)
    state, message = sweep_begin(dense_ref, source, link)
    state_ref[...] = state
    ahead_ref[0:16, :] = message
    behind_ref[0:16, :] = message
    ahead_ref[16:80, :] = pack_last([box_ref[b, 384:448, :] for b in range(NB)] + extra[0])
    behind_ref[16:80, :] = pack_first([box_ref[b, 64:128, :] for b in range(NB)] + extra[1])


def pack_body(*refs):
    sources, out_ref, held, (tmp, ready) = refs[:9], refs[9], refs[10:19], refs[19:]
    a_ref, b_ref = out_ref.at[0:ROWS_A], out_ref.at[ROWS_A:ROWS]
    copies = [pltpu.make_async_copy(sources[n], held[n], ready.at[n]) for n in range(9)]
    for copy in copies:
        copy.start()
    for copy in copies:
        copy.wait()
    rhs_ref, helm_ref, vec_ref, val_ref, size_ref, rows_ref, link_ref, six_ref, eight_ref = held
    for t in range(4):
        a_ref[t * 32 : (t + 1) * 32, :] = rows_ref[:, t * 128 : (t + 1) * 128]
        a_ref[128:176, t * 32 : (t + 1) * 32] = vec_ref[t * 48 : (t + 1) * 48, :]
    tmp[...] = jnp.zeros(tmp.shape, F32)
    for i in range(6):
        tmp[i * 8 + 1 : i * 8 + 7, :] = rhs_ref[i]
    nodes = jnp.dot(tmp[...], six_ref[...], precision=HIGHEST, preferred_element_type=F32)
    b_ref[0:48, :] = nodes[:, 0:128]
    b_ref[48:96, :] = jnp.zeros((48, 128), F32)
    b_ref[48:96, 0:64] = nodes[:, 128:192]
    b_ref[48:72, 64:96] = val_ref[...]
    b_ref[72:75, 64:96] = size_ref[...]
    b_ref[80:81, 64:96] = jnp.broadcast_to(link_ref[0], (1, 32))
    helm = jnp.dot(
        helm_ref[...].reshape(64, 256), eight_ref[...], precision=HIGHEST, preferred_element_type=F32
    )
    b_ref[96:160, :] = helm[:, 0:128]
    b_ref[160:224, :] = helm[:, 128:256]


def joined(all_ref, b, start, rows, quarter):
    place = lanes((rows, 128)) // EA
    total = None
    for c in range(4):
        moved = turn(all_ref[b * 4 + c, start : start + rows, :], (c - quarter) * 32)
        part = jnp.where(place == c, moved, 0.0)
        total = part if total is None else total + part
    return total


def unpack_body(
    all_ref, dense_ref, rhs_ref, helm_ref, vec_ref, small_ref, box_ref, state_ref, ahead_ref, behind_ref
):
    for b in range(NB):
        for c in range(4):
            at = (b * 4 + c) * 32
            for t in range(4):
                dense_ref[at : at + 32, t * 128 : (t + 1) * 128] = all_ref[b * 4 + c, t * 32 : (t + 1) * 32, :]
        for t in range(4):
            vec_ref[b, t * 48 : (t + 1) * 48, :] = joined(all_ref, b, 128, 48, t)
        for k in range(6):
            rhs_ref[b, k * 48 : (k + 1) * 48, :] = joined(all_ref, b, ROWS_A + 48 * (k // 4), 48, k % 4)
        small_ref[b, :, :] = joined(all_ref, b, ROWS_A + 48, 48, 2)
        for k in range(8):
            helm_ref[b, k * 64 : (k + 1) * 64, :] = joined(
                all_ref, b, ROWS_A + 96 + 64 * (k // 4), 64, k % 4
            )
    begin_kernel_part(
        rhs_ref, small_ref, dense_ref, box_ref, state_ref, ahead_ref, behind_ref,
        ([helm_ref[b, 448:512, :] for b in range(NB)], [helm_ref[b, 0:64, :] for b in range(NB)]),
    )


def middle_body(dense_ref, state_ref, left_ref, right_ref, state_out, message_out):
    state, message = sweep_pair(dense_ref, state_ref[...], left_ref[0:16, :], right_ref[0:16, :], 0)
    state_out[...] = state
    message_out[...] = message


def late_body(dense_ref, state_ref, left_ref, right_ref, up_ref, down_ref, state_out, ahead_ref, behind_ref):
    state, message = sweep_pair(dense_ref, state_ref[...], left_ref[...], right_ref[...], 2)
    state_out[...] = state
    ahead_ref[0:16, :] = message
    behind_ref[0:16, :] = message
    ahead_ref[16:80, :] = up_ref[...]
    behind_ref[16:80, :] = down_ref[...]


def join_rows(ref, groups, cross):
    for b in range(NB):
        low = ref[b, pl.ds(0, groups * 8, stride=8), :]
        high = ref[b, pl.ds(7, groups * 8, stride=8), :]
        ref[b, pl.ds(0, groups * 8, stride=8), :] = low + turn(high, 32)
        ref[b, pl.ds(7, groups * 8, stride=8), :] = high + turn(low, -32)
    for b in range(NB - 1):
        for g in range(groups):
            both = ref[b, g * 64 + 56 : g * 64 + 64, :] + ref[b + 1, g * 64 : g * 64 + 8, :]
            ref[b, g * 64 + 56 : g * 64 + 64, :] = both
            ref[b + 1, g * 64 : g * 64 + 8, :] = both


def join_layers(low, high):
    place = lanes(low.shape) % EA
    new_low = low + jnp.where(place > 0, turn(high, 1), 0.0)
    new_high = high + jnp.where(place < EA - 1, turn(low, -1), 0.0)
    return new_low, new_high


def helm_body(helm_ref, left_ref, right_ref, out_ref):
    out_ref[...] = helm_ref[...]
    for b in range(NB):
        low, high = join_layers(helm_ref[b, 0:64, :], helm_ref[b, 448:512, :])
        out_ref[b, 0:64, :] = low + at_first(left_ref[16:80, :], 4 + b)
        out_ref[b, 448:512, :] = high + at_last(right_ref[16:80, :], 4 + b)
    join_rows(out_ref, 8, None)
    for b in range(NB):
        out_ref[b] = 1.0 / out_ref[b]


def schwarz_body(box_ref, vec_ref, small_ref, left_ref, right_ref, out_ref, up_ref, down_ref, one, two, full):
    def element_row(b, carry):
        def row(side, first, second):
            return vec_ref[b, pl.ds(side * 64 + first * 8 + second, 1), :]

        last = pltpu.roll(box_ref[b, 384:448, :], 1, 1)
        first = pltpu.roll(box_ref[b, 64:128, :], 127, 1)
        place = lanes((64, 128)) % EA
        from_left = pltpu.roll(left_ref[16:80, :], 97 + b, 1)
        from_right = pltpu.roll(right_ref[16:80, :], 31 - b, 1)
        one[0] = jnp.where(place == 0, from_left, last).reshape(8, 8, 128)
        one[7] = jnp.where(place == EA - 1, from_right, first).reshape(8, 8, 128)
        one[1:7] = box_ref[b, 64:448, :].reshape(6, 8, 8, 128)
        for m in range(8):
            total = None
            for i in range(8):
                part = one[:, i] * row(0, i, m)[None]
                total = part if total is None else total + part
            two[:, m] = total
        for m in range(8):
            total = None
            for i in range(8):
                part = two[i] * row(2, i, m)[None]
                total = part if total is None else total + part
            one[m] = total
        for k in range(8):
            total = None
            for j in range(8):
                part = one[k, :, j : j + 1, :] * vec_ref[b, 64 + j * 8 : 72 + j * 8, :][None]
                total = part if total is None else total + part
            bottom = small_ref[b, 0:8, :][:, None, :] + small_ref[b, 8:16, :][None, :, :]
            two[k] = total / (bottom + small_ref[b, 16 + k : 17 + k, :][None])
        for k in range(8):
            total = None
            for n in range(8):
                part = two[k, :, n : n + 1, :] * vec_ref[b, pl.ds(64 + n, 8, stride=8), :][None]
                total = part if total is None else total + part
            one[k] = total
        for i in range(8):
            total = None
            for m in range(8):
                part = one[m] * row(2, i, m)[None]
                total = part if total is None else total + part
            two[i] = total
        for i in range(8):
            total = None
            for m in range(8):
                part = two[:, m] * row(0, i, m)[None]
                total = part if total is None else total + part
            one[:, i] = total
        full[b] = one[...].reshape(512, 128)
        return carry

    lax.fori_loop(0, NB, element_row, 0)
    for b in range(NB):
        low = full[b, pl.ds(0, 64, stride=8), :]
        high = full[b, pl.ds(7, 64, stride=8), :]
        full[b, pl.ds(6, 64, stride=8), :] = full[b, pl.ds(6, 64, stride=8), :] + turn(low, -32)
        full[b, pl.ds(1, 64, stride=8), :] = full[b, pl.ds(1, 64, stride=8), :] + turn(high, 32)
        full[b, pl.ds(0, 64, stride=8), :] = jnp.zeros((64, 128), F32)
        full[b, pl.ds(7, 64, stride=8), :] = jnp.zeros((64, 128), F32)
    for b in range(NB - 1):
        for k in range(8):
            full[b, k * 64 + 48 : k * 64 + 56, :] = (
                full[b, k * 64 + 48 : k * 64 + 56, :] + full[b + 1, k * 64 : k * 64 + 8, :]
            )
            full[b + 1, k * 64 + 8 : k * 64 + 16, :] = (
                full[b + 1, k * 64 + 8 : k * 64 + 16, :] + full[b, k * 64 + 56 : k * 64 + 64, :]
            )
    up_ref[...] = pack_last([full[b, 448:512, :] for b in range(NB)])
    down_ref[...] = pack_first([full[b, 0:64, :] for b in range(NB)])
    place = lanes((48, 128)) % EA
    for b in range(NB):
        for k in range(6):
            value = full[b, (k + 1) * 64 + 8 : (k + 1) * 64 + 56, :]
            if k == 0:
                value = value + jnp.where(place > 0, turn(full[b, 456:504, :], 1), 0.0)
            if k == 5:
                value = value + jnp.where(place < EA - 1, turn(full[b, 8:56, :], -1), 0.0)
            out_ref[b, k * 48 : (k + 1) * 48, :] = value


def volume_factors(small_ref, b):
    size = [small_ref[b, 24 + d : 25 + d, :] for d in range(3)]
    volume = size[0] * size[1] * size[2] * 0.125
    return [volume * (2.0 / size[d]) for d in range(3)]


def split_parts(value):
    high = value.astype(BF16)
    return high, (value - high.astype(F32)).astype(BF16)


def gradient_body(
    dense_ref, state_ref, left_ref, right_ref, part_ref, small_ref, table_ref, z_ref, t_ref, ahead_ref, behind_ref
):
    solution = sweep_pair(dense_ref, state_ref[...], left_ref[0:16, :], right_ref[0:16, :], 4)
    inside = lax.broadcasted_iota(jnp.int32, (ROWS_P, 128), 0) % 8
    inside = (inside > 0) & (inside < 7)
    for b in range(NB):
        coarse = jnp.where(inside, solution[b : b + 1, :], 0.0)
        z_ref[b] = part_ref[b] + coarse
        z_ref[b, 0:48, :] = z_ref[b, 0:48, :] + at_first(left_ref[24:72, :], b)
        z_ref[b, 240:288, :] = z_ref[b, 240:288, :] + at_last(right_ref[24:72, :], b)
    parts = [split_parts(z_ref[b]) for b in range(NB)]
    high = jnp.concatenate([part[0] for part in parts], axis=1)
    low = jnp.concatenate([part[1] for part in parts], axis=1)
    both = jnp.concatenate([high, low, high], axis=0)
    factors = [volume_factors(small_ref, b) for b in range(NB)]
    for d in range(3):
        result = jnp.dot(table_ref[d * 512 : (d + 1) * 512, :], both, preferred_element_type=F32)
        for b in range(NB):
            t_ref[b, d * 512 : (d + 1) * 512, :] = result[:, b * 128 : (b + 1) * 128] * factors[b][d]
    join_rows(t_ref, 24, None)
    lows = [t_ref[b, d * 512 : d * 512 + 64, :] for b in range(NB) for d in range(3)]
    highs = [t_ref[b, d * 512 + 448 : d * 512 + 512, :] for b in range(NB) for d in range(3)]
    ahead_ref[...] = pack_last(highs)
    behind_ref[...] = pack_first(lows)
    for b in range(NB):
        for d in range(3):
            low, high = join_layers(lows[b * 3 + d], highs[b * 3 + d])
            t_ref[b, d * 512 : d * 512 + 64, :] = low
            t_ref[b, d * 512 + 448 : d * 512 + 512, :] = high


def divergence_part(t_ref, left_ref, right_ref, inverse_ref, small_ref, table_ref, image_ref, spread):
    for b in range(NB):
        factors = volume_factors(small_ref, b)
        for d in range(3):
            base = d * 512
            for start, rows, extra in (
                (0, 64, at_first(left_ref[...], b * 3 + d)),
                (64, 384, None),
                (448, 64, at_last(right_ref[...], b * 3 + d)),
            ):
                value = t_ref[b, base + start : base + start + rows, :]
                if extra is not None:
                    value = value + extra
                value = value * inverse_ref[b, start : start + rows, :] * factors[d]
                high, low = split_parts(value)
                spread[base + start : base + start + rows, b * 128 : (b + 1) * 128] = high
                spread[1536 + base + start : 1536 + base + start + rows, b * 128 : (b + 1) * 128] = low
    image = jnp.dot(table_ref[:, 0:3072], spread[...], preferred_element_type=F32)
    image = image + jnp.dot(table_ref[:, 3072:4608], spread[0:1536, :], preferred_element_type=F32)
    for b in range(NB):
        image_ref[b] = image[:, b * 128 : (b + 1) * 128]


def first_image_body(
    t_ref, left_ref, right_ref, inverse_ref, small_ref, table_ref, dense_ref,
    image_ref, box_ref, state_ref, ahead_ref, behind_ref, spread,
):
    divergence_part(t_ref, left_ref, right_ref, inverse_ref, small_ref, table_ref, image_ref, spread)
    begin_kernel_part(
        image_ref, small_ref, dense_ref, box_ref, state_ref, ahead_ref, behind_ref, ([], [])
    )


def last_image_body(
    t_ref, left_ref, right_ref, inverse_ref, small_ref, table_ref, r_ref, z_ref, w_ref, q_ref,
    image_ref, sums_ref, spread,
):
    divergence_part(t_ref, left_ref, right_ref, inverse_ref, small_ref, table_ref, image_ref, spread)
    products = ((r_ref, z_ref), (z_ref, w_ref), (w_ref, q_ref), (r_ref, q_ref), (q_ref, image_ref), (z_ref, image_ref))
    sums_ref[...] = jnp.zeros(sums_ref.shape, F32)
    for n, (one, two) in enumerate(products):
        total = None
        for b in range(NB):
            part = jnp.sum(one[b] * two[b], axis=0, keepdims=True)
            total = part if total is None else total + part
        sums_ref[n : n + 1, :] = total


def own_body(me_ref, z_ref, w_ref, q_ref, v_ref, table_ref, z_out, w_out, q_out, v_out):
    mine_b = me_ref[0]
    mine_c = me_ref[1]
    for field_ref, out_ref in ((z_ref, z_out), (w_ref, w_out), (q_ref, q_out), (v_ref, v_out)):
        moved = pltpu.roll(field_ref[mine_b], ((4 - mine_c) & 3) * 32, 1)
        nodes = jnp.concatenate([moved[k * 48 : (k + 1) * 48, 0:32] for k in range(6)], axis=1)
        nodes = jnp.dot(nodes, table_ref[...], precision=HIGHEST, preferred_element_type=F32)
        for i in range(6):
            out_ref[i] = nodes[i * 8 + 1 : i * 8 + 7, :]


def last_body(
    sums_ref, z_ref, w_ref, q_ref, v_ref, rhs_ref, pressure_ref, residual_ref, pressure, residual, done
):
    totals = jnp.sum(jnp.sum(sums_ref[...], axis=0), axis=1, keepdims=True)
    rz, zw, wq, rq, qv, zv = [totals[n : n + 1] for n in range(6)]
    step_first = rz / zw
    rz_next = step_first * (step_first * wq - rq)
    share = 1.0 + rz_next / rz
    curvature = share * share * zw - share * step_first * (zv + wq) + step_first * step_first * qv
    step_next = rz_next / curvature
    z_factor = (step_first + step_next * share)[None]
    q_factor = (step_next * step_first)[None]
    pressure[...] = z_factor * z_ref[...] - q_factor * q_ref[...]
    first = pltpu.make_async_copy(pressure, pressure_ref, done.at[0])
    first.start()
    residual[...] = rhs_ref[...] - z_factor * w_ref[...] + q_factor * v_ref[...]
    second = pltpu.make_async_copy(residual, residual_ref, done.at[1])
    second.start()
    first.wait()
    second.wait()


def call(body, outs, scratch=(), scalars=0):
    vmem = pl.BlockSpec(memory_space=pltpu.VMEM)
    smem = pl.BlockSpec(memory_space=pltpu.SMEM)

    def run(*operands):
        return pl.pallas_call(
            body,
            out_shape=[jax.ShapeDtypeStruct(shape, F32) for shape in outs],
            in_specs=[smem] * scalars + [vmem] * (len(operands) - scalars),
            out_specs=[vmem] * len(outs),
            scratch_shapes=list(scratch),
            compiler_params=pltpu.CompilerParams(vmem_limit_bytes=40 * 1024 * 1024),
        )(*operands)

    return run


def tell_all(block, axes, count):
    return lax.all_to_all(jnp.broadcast_to(block[None], (count,) + block.shape), axes, 0, 0)


def local(divergence, elem_size, helm_diag, fdm_vectors, fdm_values, coarse_rows, axial_link):
    count = lax.axis_size("gx")
    ahead = [(i, (i + 1) % count) for i in range(count)]
    behind = [((i + 1) % count, i) for i in range(count)]

    def exchange(up, down):
        return lax.ppermute(up, "gx", ahead), lax.ppermute(down, "gx", behind)

    forward, backward = gradient_tables()
    six = order_table(6)
    me = jnp.stack([lax.axis_index("gy"), lax.axis_index("col")]).astype(jnp.int32)
    field = (NB, ROWS_P, 128)
    velocity = (NB, ROWS_V, 128)
    state_shape = (16, 128)
    wide = (80, 128)
    plane = (64, 128)

    arguments = (
        divergence,
        helm_diag,
        fdm_vectors.reshape(192, EA),
        fdm_values.reshape(24, EA),
        elem_size,
        coarse_rows,
        axial_link,
        six,
        order_table(8),
    )
    own_part = pl.pallas_call(
        pack_body,
        out_shape=jax.ShapeDtypeStruct((ROWS, 128), F32),
        in_specs=[pl.BlockSpec(memory_space=pl.ANY)] * 9,
        out_specs=pl.BlockSpec(memory_space=pltpu.VMEM),
        scratch_shapes=[pltpu.VMEM(value.shape, F32) for value in arguments]
        + [pltpu.VMEM((48, 192), F32), pltpu.SemaphoreType.DMA((9,))],
        compiler_params=pltpu.CompilerParams(vmem_limit_bytes=60 * 1024 * 1024),
    )(*arguments)
    everything = tell_all(own_part, ("gy", "col"), 16)

    dense, rhs, helm, vectors, small, boxes, state, up, down = call(
        unpack_body,
        [(512, 512), field, velocity, (NB, 192, 128), (NB, 48, 128), velocity, state_shape, wide, wide],
    )(everything)

    def precondition(boxes, state, left, right):
        state, message = call(middle_body, [state_shape, state_shape])(dense, state, left, right)
        left_mid, right_mid = exchange(message, message)
        part, up, down = call(
            schwarz_body,
            [field, plane, plane],
            [pltpu.VMEM((8, 8, 8, 128), F32), pltpu.VMEM((8, 8, 8, 128), F32), pltpu.VMEM(velocity, F32)],
        )(boxes, vectors, small, left, right)
        state, up, down = call(late_body, [state_shape, wide, wide])(
            dense, state, left_mid, right_mid, up, down
        )
        left, right = exchange(up, down)
        z, t, up, down = call(gradient_body, [field, (NB, 1536, 128), plane, plane])(
            dense, state, left, right, part, small, forward
        )
        left, right = exchange(up, down)
        return z, t, left, right

    spread = [pltpu.VMEM((3072, 512), BF16)]
    left, right = exchange(up, down)
    (inverse,) = call(helm_body, [velocity])(helm, left, right)
    z, t, left, right = precondition(boxes, state, left, right)
    w, boxes, state, up, down = call(
        first_image_body, [field, velocity, state_shape, wide, wide], spread
    )(t, left, right, inverse, small, backward, dense)
    left, right = exchange(up, down)
    q, t, left, right = precondition(boxes, state, left, right)
    v, sums = call(last_image_body, [field, (8, 128)], spread)(
        t, left, right, inverse, small, backward, rhs, z, w, q
    )
    own = call(own_body, [(6, 6, 192)] * 4, scalars=1)(me, z, w, q, v, six.T.copy())
    sums = tell_all(sums, "gx", count)
    return tuple(
        pl.pallas_call(
            last_body,
            out_shape=[jax.ShapeDtypeStruct((6, 6, 192), F32)] * 2,
            in_specs=[pl.BlockSpec(memory_space=pltpu.VMEM)] * 6,
            out_specs=[pl.BlockSpec(memory_space=pl.ANY)] * 2,
            scratch_shapes=[pltpu.VMEM((6, 6, 192), F32)] * 2 + [pltpu.SemaphoreType.DMA((2,))],
            compiler_params=pltpu.CompilerParams(vmem_limit_bytes=40 * 1024 * 1024),
        )(sums, *own, divergence)
    )


def solution(mesh):
    in_specs = (
        P("gy", "col", "gx"),
        P(None, ("gx", "gy", "col")),
        P("gy", "col", "gx"),
        P(None, None, None, ("gx", "gy", "col")),
        P(None, None, ("gx", "gy", "col")),
        P(("gx", "gy", "col"), None),
        P("gx", "gy", "col"),
    )
    out_specs = (P("gy", "col", "gx"), P("gy", "col", "gx"))
    return jax.shard_map(local, mesh=mesh, in_specs=in_specs, out_specs=out_specs, check_vma=False)
```

```python
import jax
import jax.numpy as jnp
import ml_dtypes
import numpy as np
from jax import lax
from jax.experimental import pallas as pl
from jax.experimental.pallas import tpu as pltpu
from jax.sharding import PartitionSpec as P

EA = 32
CHEB = 6
NB = 4

LOBATTO_NODES = [
    -1.0,
    -0.8717401485096066,
    -0.5917001814331423,
    -0.2092992179024789,
    0.2092992179024789,
    0.5917001814331423,
    0.8717401485096066,
    1.0,
]
GAUSS_NODES = [
    -0.932469514203152,
    -0.6612093864662645,
    -0.2386191860831909,
    0.2386191860831909,
    0.6612093864662645,
    0.932469514203152,
]
GAUSS_WEIGHTS = [
    0.1713244923791704,
    0.3607615730481386,
    0.467913934572691,
    0.467913934572691,
    0.3607615730481386,
    0.1713244923791704,
]
SPECTRUM_LOW = 8.0
SPECTRUM_HIGH = 90.0
HIGHEST = lax.Precision.HIGHEST
F32 = jnp.float32
BF16 = jnp.bfloat16

ROWS_P = 288
ROWS_V = 512
ROWS_A = 176
ROWS_B = 224


def basis_tables():
    lobatto = np.array(LOBATTO_NODES)
    points = np.array(GAUSS_NODES)
    interp = np.ones((6, 8))
    slopes = np.zeros((6, 8))
    for p in range(6):
        for m in range(8):
            product = 1.0
            for q in range(8):
                if q != m:
                    product = product * (points[p] - lobatto[q]) / (lobatto[m] - lobatto[q])
            interp[p, m] = product
            running = 0.0
            for q in range(8):
                if q != m:
                    factor = 1.0 / (lobatto[m] - lobatto[q])
                    for k in range(8):
                        if k != m and k != q:
                            factor = factor * (points[p] - lobatto[k]) / (lobatto[m] - lobatto[k])
                    running = running + factor
            slopes[p, m] = running
    return interp, slopes


def gradient_tables():
    interp, slopes = basis_tables()
    weight = np.array(GAUSS_WEIGHTS)
    tables = []
    for comp in range(3):
        sides = [(slopes if side == comp else interp) * weight[:, None] for side in range(3)]
        full = np.zeros((8, 8, 8, 6, 6, 8))
        full[..., 1:7] = np.einsum("iu,jv,kw->wuvkij", sides[0], sides[1], sides[2])
        tables.append(full.reshape(ROWS_V, ROWS_P))
    table = np.concatenate(tables, axis=0).astype(np.float32)
    high = table.astype(ml_dtypes.bfloat16)
    low = (table - high.astype(np.float32)).astype(ml_dtypes.bfloat16)
    forward = np.concatenate([high, high, low], axis=1)
    backward = np.concatenate([high.T, high.T, low.T], axis=1)
    return forward, backward


def order_table(nodes):
    table = np.zeros((nodes * EA, nodes * EA), np.float32)
    for k in range(nodes):
        for a in range(EA):
            table[a * nodes + k, k * EA + a] = 1.0
    return table


def sweep_factors():
    center = (SPECTRUM_HIGH + SPECTRUM_LOW) / 2.0
    spread = (SPECTRUM_HIGH - SPECTRUM_LOW) / 2.0
    ratio_cs = center / spread
    rho_now = 1.0 / ratio_cs
    keep, add = [], []
    for _ in range(CHEB):
        rho_next = 1.0 / (2.0 * ratio_cs - rho_now)
        keep.append(rho_next * rho_now)
        add.append(2.0 * rho_next / spread)
        rho_now = rho_next
    return center, keep, add


CENTER, KEEP, ADD = sweep_factors()


def lanes(shape):
    return lax.broadcasted_iota(jnp.int32, shape, len(shape) - 1)


def turn(value, shift):
    shift = shift % 128
    return value if shift == 0 else pltpu.roll(value, shift, value.ndim - 1)


def at_first(value, slot=0):
    moved = turn(value, 97 + slot)
    return jnp.where(lanes(moved.shape) % EA == 0, moved, 0.0)


def at_last(value, slot=0):
    moved = turn(value, 31 - slot)
    return jnp.where(lanes(moved.shape) % EA == EA - 1, moved, 0.0)


def pack_last(blocks):
    packed = None
    for slot, block in enumerate(blocks):
        part = turn(jnp.where(lanes(block.shape) % EA == EA - 1, block, 0.0), -slot)
        packed = part if packed is None else packed + part
    return packed


def pack_first(blocks):
    packed = None
    for slot, block in enumerate(blocks):
        part = turn(jnp.where(lanes(block.shape) % EA == 0, block, 0.0), slot)
        packed = part if packed is None else packed + part
    return packed


def times(dense_ref, vector):
    columns = jnp.concatenate([vector, jnp.zeros_like(vector)], axis=0).T
    total = None
    for b in range(NB):
        part = dense_ref[b * 128 : (b + 1) * 128, :] * columns[:, b : b + 1]
        total = part if total is None else total + part
    row = jnp.sum(total, axis=0, keepdims=True)
    return jnp.concatenate([row[:, b * 128 : (b + 1) * 128] for b in range(NB)], axis=0)


def sweep_begin(dense_ref, source, link):
    update = source * (1.0 / CENTER)
    remainder = source - times(dense_ref, update)
    free = KEEP[0] * update + ADD[0] * remainder
    state = jnp.concatenate([update, remainder, update, link], axis=0)
    return state, jnp.concatenate([update, free, link, link], axis=0)


def sweep_pair(dense_ref, state, from_left, from_right, sweep_at):
    update, remainder, solution, link = [state[4 * n : 4 * n + 4] for n in range(4)]
    left = at_first(from_left)
    right = at_last(from_right)
    place = lanes(update.shape) % EA
    link_left = left[8:12]
    link_right = jnp.where(place == EA - 1, link, 0.0)
    remainder = remainder + link_left * left[0:4] + link_right * right[0:4]
    left_next = left[4:8] + ADD[sweep_at] * link_left * update
    right_next = right[4:8] + ADD[sweep_at] * link_right * update
    update = KEEP[sweep_at] * update + ADD[sweep_at] * remainder
    solution = solution + update
    remainder = remainder - times(dense_ref, update)
    remainder = remainder + link_left * left_next + link_right * right_next
    update = KEEP[sweep_at + 1] * update + ADD[sweep_at + 1] * remainder
    solution = solution + update
    if sweep_at + 2 == CHEB:
        return solution
    remainder = remainder - times(dense_ref, update)
    free = KEEP[sweep_at + 2] * update + ADD[sweep_at + 2] * remainder
    state = jnp.concatenate([update, remainder, solution, link], axis=0)
    return state, jnp.concatenate([update, free, link, link], axis=0)


def fill_boxes(field_ref, box_ref):
    box_ref[...] = jnp.zeros(box_ref.shape, F32)
    for b in range(NB):
        for k in range(6):
            box_ref[b, (k + 1) * 64 + 8 : (k + 1) * 64 + 56, :] = field_ref[b, k * 48 : (k + 1) * 48, :]
        before = box_ref[b, pl.ds(6, 64, stride=8), :]
        after = box_ref[b, pl.ds(1, 64, stride=8), :]
        box_ref[b, pl.ds(0, 64, stride=8), :] = turn(before, 32)
        box_ref[b, pl.ds(7, 64, stride=8), :] = turn(after, -32)
    for b in range(NB):
        for k in range(1, 7):
            if b > 0:
                box_ref[b, k * 64 : k * 64 + 8, :] = box_ref[b - 1, k * 64 + 48 : k * 64 + 56, :]
            if b < NB - 1:
                box_ref[b, k * 64 + 56 : k * 64 + 64, :] = box_ref[b + 1, k * 64 + 8 : k * 64 + 16, :]


def begin_kernel_part(field_ref, small_ref, dense_ref, box_ref, state_ref, ahead_ref, behind_ref, extra):
    fill_boxes(field_ref, box_ref)
    source = jnp.concatenate(
        [jnp.sum(field_ref[b], axis=0, keepdims=True) for b in range(NB)], axis=0
    )
    link = jnp.concatenate([small_ref[b, 32:33, :] for b in range(NB)], axis=0)
    state, message = sweep_begin(dense_ref, source, link)
    state_ref[...] = state
    ahead_ref[0:16, :] = message
    behind_ref[0:16, :] = message
    ahead_ref[16:80, :] = pack_last([box_ref[b, 384:448, :] for b in range(NB)] + extra[0])
    behind_ref[16:80, :] = pack_first([box_ref[b, 64:128, :] for b in range(NB)] + extra[1])


def pack_body(*refs):
    sources, (a_out, b_out), held, (tmp, ready) = refs[:9], refs[9:11], refs[11:20], refs[20:]
    a_ref, b_ref = a_out.at[0], b_out.at[0]
    copies = [pltpu.make_async_copy(sources[n], held[n], ready.at[n]) for n in range(9)]
    for copy in copies:
        copy.start()
    for copy in copies:
        copy.wait()
    rhs_ref, helm_ref, vec_ref, val_ref, size_ref, rows_ref, link_ref, six_ref, eight_ref = held
    for t in range(4):
        a_ref[t * 32 : (t + 1) * 32, :] = rows_ref[:, t * 128 : (t + 1) * 128]
        a_ref[128:176, t * 32 : (t + 1) * 32] = vec_ref[t * 48 : (t + 1) * 48, :]
    tmp[...] = jnp.zeros(tmp.shape, F32)
    for i in range(6):
        tmp[i * 8 + 1 : i * 8 + 7, :] = rhs_ref[i]
    nodes = jnp.dot(tmp[...], six_ref[...], precision=HIGHEST, preferred_element_type=F32)
    b_ref[0:48, :] = nodes[:, 0:128]
    b_ref[48:96, :] = jnp.zeros((48, 128), F32)
    b_ref[48:96, 0:64] = nodes[:, 128:192]
    b_ref[48:72, 64:96] = val_ref[...]
    b_ref[72:75, 64:96] = size_ref[...]
    b_ref[80:81, 64:96] = jnp.broadcast_to(link_ref[0], (1, 32))
    helm = jnp.dot(
        helm_ref[...].reshape(64, 256), eight_ref[...], precision=HIGHEST, preferred_element_type=F32
    )
    b_ref[96:160, :] = helm[:, 0:128]
    b_ref[160:224, :] = helm[:, 128:256]
    for n in range(1, 4):
        a_out[n] = a_out[0]
        b_out[n] = b_out[0]


def joined(column, start, rows, quarter):
    place = lanes((rows, 128)) // EA
    total = None
    for c in range(4):
        moved = turn(column[c][start : start + rows, :], (c - quarter) * 32)
        part = jnp.where(place == c, moved, 0.0)
        total = part if total is None else total + part
    return total


def unpack_body(
    a_ref, b_ref, dense_ref, rhs_ref, helm_ref, vec_ref, small_ref, box_ref, state_ref, ahead_ref, behind_ref
):
    for b in range(NB):
        column_a = [a_ref.at[b, c] for c in range(4)]
        column_b = [b_ref.at[c, b] for c in range(4)]
        for c in range(4):
            at = (b * 4 + c) * 32
            for t in range(4):
                dense_ref[at : at + 32, t * 128 : (t + 1) * 128] = column_a[c][t * 32 : (t + 1) * 32, :]
        for t in range(4):
            vec_ref[b, t * 48 : (t + 1) * 48, :] = joined(column_a, 128, 48, t)
        for k in range(6):
            rhs_ref[b, k * 48 : (k + 1) * 48, :] = joined(column_b, 48 * (k // 4), 48, k % 4)
        small_ref[b, :, :] = joined(column_b, 48, 48, 2)
        for k in range(8):
            helm_ref[b, k * 64 : (k + 1) * 64, :] = joined(column_b, 96 + 64 * (k // 4), 64, k % 4)
    begin_kernel_part(
        rhs_ref, small_ref, dense_ref, box_ref, state_ref, ahead_ref, behind_ref,
        ([helm_ref[b, 448:512, :] for b in range(NB)], [helm_ref[b, 0:64, :] for b in range(NB)]),
    )


def middle_body(dense_ref, state_ref, left_ref, right_ref, state_out, message_out):
    state, message = sweep_pair(dense_ref, state_ref[...], left_ref[0:16, :], right_ref[0:16, :], 0)
    state_out[...] = state
    message_out[...] = message


def late_body(dense_ref, state_ref, left_ref, right_ref, up_ref, down_ref, state_out, ahead_ref, behind_ref):
    state, message = sweep_pair(dense_ref, state_ref[...], left_ref[...], right_ref[...], 2)
    state_out[...] = state
    ahead_ref[0:16, :] = message
    behind_ref[0:16, :] = message
    ahead_ref[16:80, :] = up_ref[...]
    behind_ref[16:80, :] = down_ref[...]


def join_rows(ref, groups, cross):
    for b in range(NB):
        low = ref[b, pl.ds(0, groups * 8, stride=8), :]
        high = ref[b, pl.ds(7, groups * 8, stride=8), :]
        ref[b, pl.ds(0, groups * 8, stride=8), :] = low + turn(high, 32)
        ref[b, pl.ds(7, groups * 8, stride=8), :] = high + turn(low, -32)
    for b in range(NB - 1):
        for g in range(groups):
            both = ref[b, g * 64 + 56 : g * 64 + 64, :] + ref[b + 1, g * 64 : g * 64 + 8, :]
            ref[b, g * 64 + 56 : g * 64 + 64, :] = both
            ref[b + 1, g * 64 : g * 64 + 8, :] = both


def join_layers(low, high):
    place = lanes(low.shape) % EA
    new_low = low + jnp.where(place > 0, turn(high, 1), 0.0)
    new_high = high + jnp.where(place < EA - 1, turn(low, -1), 0.0)
    return new_low, new_high


def helm_body(helm_ref, left_ref, right_ref, out_ref):
    out_ref[...] = helm_ref[...]
    for b in range(NB):
        low, high = join_layers(helm_ref[b, 0:64, :], helm_ref[b, 448:512, :])
        out_ref[b, 0:64, :] = low + at_first(left_ref[16:80, :], 4 + b)
        out_ref[b, 448:512, :] = high + at_last(right_ref[16:80, :], 4 + b)
    join_rows(out_ref, 8, None)
    for b in range(NB):
        out_ref[b] = 1.0 / out_ref[b]


def schwarz_body(box_ref, vec_ref, small_ref, left_ref, right_ref, out_ref, up_ref, down_ref, one, two, full):
    def element_row(b, carry):
        def row(side, first, second):
            return vec_ref[b, pl.ds(side * 64 + first * 8 + second, 1), :]

        last = pltpu.roll(box_ref[b, 384:448, :], 1, 1)
        first = pltpu.roll(box_ref[b, 64:128, :], 127, 1)
        place = lanes((64, 128)) % EA
        from_left = pltpu.roll(left_ref[16:80, :], 97 + b, 1)
        from_right = pltpu.roll(right_ref[16:80, :], 31 - b, 1)
        one[0] = jnp.where(place == 0, from_left, last).reshape(8, 8, 128)
        one[7] = jnp.where(place == EA - 1, from_right, first).reshape(8, 8, 128)
        one[1:7] = box_ref[b, 64:448, :].reshape(6, 8, 8, 128)
        for m in range(8):
            total = None
            for i in range(8):
                part = one[:, i] * row(0, i, m)[None]
                total = part if total is None else total + part
            two[:, m] = total
        for m in range(8):
            total = None
            for i in range(8):
                part = two[i] * row(2, i, m)[None]
                total = part if total is None else total + part
            one[m] = total
        for k in range(8):
            total = None
            for j in range(8):
                part = one[k, :, j : j + 1, :] * vec_ref[b, 64 + j * 8 : 72 + j * 8, :][None]
                total = part if total is None else total + part
            bottom = small_ref[b, 0:8, :][:, None, :] + small_ref[b, 8:16, :][None, :, :]
            two[k] = total / (bottom + small_ref[b, 16 + k : 17 + k, :][None])
        for k in range(8):
            total = None
            for n in range(8):
                part = two[k, :, n : n + 1, :] * vec_ref[b, pl.ds(64 + n, 8, stride=8), :][None]
                total = part if total is None else total + part
            one[k] = total
        for i in range(8):
            total = None
            for m in range(8):
                part = one[m] * row(2, i, m)[None]
                total = part if total is None else total + part
            two[i] = total
        for i in range(8):
            total = None
            for m in range(8):
                part = two[:, m] * row(0, i, m)[None]
                total = part if total is None else total + part
            one[:, i] = total
        full[b] = one[...].reshape(512, 128)
        return carry

    lax.fori_loop(0, NB, element_row, 0)
    for b in range(NB):
        low = full[b, pl.ds(0, 64, stride=8), :]
        high = full[b, pl.ds(7, 64, stride=8), :]
        full[b, pl.ds(6, 64, stride=8), :] = full[b, pl.ds(6, 64, stride=8), :] + turn(low, -32)
        full[b, pl.ds(1, 64, stride=8), :] = full[b, pl.ds(1, 64, stride=8), :] + turn(high, 32)
        full[b, pl.ds(0, 64, stride=8), :] = jnp.zeros((64, 128), F32)
        full[b, pl.ds(7, 64, stride=8), :] = jnp.zeros((64, 128), F32)
    for b in range(NB - 1):
        for k in range(8):
            full[b, k * 64 + 48 : k * 64 + 56, :] = (
                full[b, k * 64 + 48 : k * 64 + 56, :] + full[b + 1, k * 64 : k * 64 + 8, :]
            )
            full[b + 1, k * 64 + 8 : k * 64 + 16, :] = (
                full[b + 1, k * 64 + 8 : k * 64 + 16, :] + full[b, k * 64 + 56 : k * 64 + 64, :]
            )
    up_ref[...] = pack_last([full[b, 448:512, :] for b in range(NB)])
    down_ref[...] = pack_first([full[b, 0:64, :] for b in range(NB)])
    place = lanes((48, 128)) % EA
    for b in range(NB):
        for k in range(6):
            value = full[b, (k + 1) * 64 + 8 : (k + 1) * 64 + 56, :]
            if k == 0:
                value = value + jnp.where(place > 0, turn(full[b, 456:504, :], 1), 0.0)
            if k == 5:
                value = value + jnp.where(place < EA - 1, turn(full[b, 8:56, :], -1), 0.0)
            out_ref[b, k * 48 : (k + 1) * 48, :] = value


def volume_factors(small_ref, b):
    size = [small_ref[b, 24 + d : 25 + d, :] for d in range(3)]
    volume = size[0] * size[1] * size[2] * 0.125
    return [volume * (2.0 / size[d]) for d in range(3)]


def split_parts(value):
    high = value.astype(BF16)
    return high, (value - high.astype(F32)).astype(BF16)


def gradient_body(
    dense_ref, state_ref, left_ref, right_ref, part_ref, small_ref, table_ref, z_ref, t_ref, ahead_ref, behind_ref
):
    solution = sweep_pair(dense_ref, state_ref[...], left_ref[0:16, :], right_ref[0:16, :], 4)
    inside = lax.broadcasted_iota(jnp.int32, (ROWS_P, 128), 0) % 8
    inside = (inside > 0) & (inside < 7)
    for b in range(NB):
        coarse = jnp.where(inside, solution[b : b + 1, :], 0.0)
        z_ref[b] = part_ref[b] + coarse
        z_ref[b, 0:48, :] = z_ref[b, 0:48, :] + at_first(left_ref[24:72, :], b)
        z_ref[b, 240:288, :] = z_ref[b, 240:288, :] + at_last(right_ref[24:72, :], b)
    parts = [split_parts(z_ref[b]) for b in range(NB)]
    high = jnp.concatenate([part[0] for part in parts], axis=1)
    low = jnp.concatenate([part[1] for part in parts], axis=1)
    both = jnp.concatenate([high, low, high], axis=0)
    factors = [volume_factors(small_ref, b) for b in range(NB)]
    for d in range(3):
        result = jnp.dot(table_ref[d * 512 : (d + 1) * 512, :], both, preferred_element_type=F32)
        for b in range(NB):
            t_ref[b, d * 512 : (d + 1) * 512, :] = result[:, b * 128 : (b + 1) * 128] * factors[b][d]
    join_rows(t_ref, 24, None)
    lows = [t_ref[b, d * 512 : d * 512 + 64, :] for b in range(NB) for d in range(3)]
    highs = [t_ref[b, d * 512 + 448 : d * 512 + 512, :] for b in range(NB) for d in range(3)]
    ahead_ref[...] = pack_last(highs)
    behind_ref[...] = pack_first(lows)
    for b in range(NB):
        for d in range(3):
            low, high = join_layers(lows[b * 3 + d], highs[b * 3 + d])
            t_ref[b, d * 512 : d * 512 + 64, :] = low
            t_ref[b, d * 512 + 448 : d * 512 + 512, :] = high


def divergence_part(t_ref, left_ref, right_ref, inverse_ref, small_ref, table_ref, image_ref, spread):
    for b in range(NB):
        factors = volume_factors(small_ref, b)
        for d in range(3):
            base = d * 512
            for start, rows, extra in (
                (0, 64, at_first(left_ref[...], b * 3 + d)),
                (64, 384, None),
                (448, 64, at_last(right_ref[...], b * 3 + d)),
            ):
                value = t_ref[b, base + start : base + start + rows, :]
                if extra is not None:
                    value = value + extra
                value = value * inverse_ref[b, start : start + rows, :] * factors[d]
                high, low = split_parts(value)
                spread[base + start : base + start + rows, b * 128 : (b + 1) * 128] = high
                spread[1536 + base + start : 1536 + base + start + rows, b * 128 : (b + 1) * 128] = low
    image = jnp.dot(table_ref[:, 0:3072], spread[...], preferred_element_type=F32)
    image = image + jnp.dot(table_ref[:, 3072:4608], spread[0:1536, :], preferred_element_type=F32)
    for b in range(NB):
        image_ref[b] = image[:, b * 128 : (b + 1) * 128]


def first_image_body(
    t_ref, left_ref, right_ref, inverse_ref, small_ref, table_ref, dense_ref,
    image_ref, box_ref, state_ref, ahead_ref, behind_ref, spread,
):
    divergence_part(t_ref, left_ref, right_ref, inverse_ref, small_ref, table_ref, image_ref, spread)
    begin_kernel_part(
        image_ref, small_ref, dense_ref, box_ref, state_ref, ahead_ref, behind_ref, ([], [])
    )


def last_image_body(
    t_ref, left_ref, right_ref, inverse_ref, small_ref, table_ref, r_ref, z_ref, w_ref, q_ref,
    image_ref, sums_ref, spread,
):
    divergence_part(t_ref, left_ref, right_ref, inverse_ref, small_ref, table_ref, image_ref, spread)
    products = ((r_ref, z_ref), (z_ref, w_ref), (w_ref, q_ref), (r_ref, q_ref), (q_ref, image_ref), (z_ref, image_ref))
    sums_ref[...] = jnp.zeros(sums_ref.shape, F32)
    for n, (one, two) in enumerate(products):
        total = None
        for b in range(NB):
            part = jnp.sum(one[b] * two[b], axis=0, keepdims=True)
            total = part if total is None else total + part
        sums_ref[n : n + 1, :] = total


def own_body(me_ref, z_ref, w_ref, q_ref, v_ref, table_ref, z_out, w_out, q_out, v_out):
    mine_b = me_ref[0]
    mine_c = me_ref[1]
    for field_ref, out_ref in ((z_ref, z_out), (w_ref, w_out), (q_ref, q_out), (v_ref, v_out)):
        moved = pltpu.roll(field_ref[mine_b], ((4 - mine_c) & 3) * 32, 1)
        nodes = jnp.concatenate([moved[k * 48 : (k + 1) * 48, 0:32] for k in range(6)], axis=1)
        nodes = jnp.dot(nodes, table_ref[...], precision=HIGHEST, preferred_element_type=F32)
        for i in range(6):
            out_ref[i] = nodes[i * 8 + 1 : i * 8 + 7, :]


def last_body(
    sums_ref, z_ref, w_ref, q_ref, v_ref, rhs_ref, pressure_ref, residual_ref, pressure, residual, done
):
    totals = jnp.sum(jnp.sum(sums_ref[...], axis=0), axis=1, keepdims=True)
    rz, zw, wq, rq, qv, zv = [totals[n : n + 1] for n in range(6)]
    step_first = rz / zw
    rz_next = step_first * (step_first * wq - rq)
    share = 1.0 + rz_next / rz
    curvature = share * share * zw - share * step_first * (zv + wq) + step_first * step_first * qv
    step_next = rz_next / curvature
    z_factor = (step_first + step_next * share)[None]
    q_factor = (step_next * step_first)[None]
    pressure[...] = z_factor * z_ref[...] - q_factor * q_ref[...]
    first = pltpu.make_async_copy(pressure, pressure_ref, done.at[0])
    first.start()
    residual[...] = rhs_ref[...] - z_factor * w_ref[...] + q_factor * v_ref[...]
    second = pltpu.make_async_copy(residual, residual_ref, done.at[1])
    second.start()
    first.wait()
    second.wait()


def call(body, outs, scratch=(), scalars=0):
    vmem = pl.BlockSpec(memory_space=pltpu.VMEM)
    smem = pl.BlockSpec(memory_space=pltpu.SMEM)

    def run(*operands):
        return pl.pallas_call(
            body,
            out_shape=[jax.ShapeDtypeStruct(shape, F32) for shape in outs],
            in_specs=[smem] * scalars + [vmem] * (len(operands) - scalars),
            out_specs=[vmem] * len(outs),
            scratch_shapes=list(scratch),
            compiler_params=pltpu.CompilerParams(vmem_limit_bytes=40 * 1024 * 1024),
        )(*operands)

    return run


def tell_all(block, axis, count, groups=None):
    copies = jnp.broadcast_to(block[None], (count,) + block.shape)
    return lax.all_to_all(copies, axis, 0, 0, axis_index_groups=groups)


def sum_slabs(sums):
    slabs = lax.axis_size("gx")
    near = [list(range(start, start + 8)) for start in range(0, slabs, 8)]
    far = [list(range(start, slabs, 8)) for start in range(8)]
    sums = jnp.sum(tell_all(sums, "gx", 8, near), axis=0)
    return tell_all(sums, "gx", slabs // 8, far)


def local(divergence, elem_size, helm_diag, fdm_vectors, fdm_values, coarse_rows, axial_link):
    count = lax.axis_size("gx")
    ahead = [(i, (i + 1) % count) for i in range(count)]
    behind = [((i + 1) % count, i) for i in range(count)]

    def exchange(up, down):
        return lax.ppermute(up, "gx", ahead), lax.ppermute(down, "gx", behind)

    forward, backward = gradient_tables()
    six = order_table(6)
    me = jnp.stack([lax.axis_index("gy"), lax.axis_index("col")]).astype(jnp.int32)
    field = (NB, ROWS_P, 128)
    velocity = (NB, ROWS_V, 128)
    state_shape = (16, 128)
    wide = (80, 128)
    plane = (64, 128)

    arguments = (
        divergence,
        helm_diag,
        fdm_vectors.reshape(192, EA),
        fdm_values.reshape(24, EA),
        elem_size,
        coarse_rows,
        axial_link,
        six,
        order_table(8),
    )
    half_a, half_b = pl.pallas_call(
        pack_body,
        out_shape=[jax.ShapeDtypeStruct((4, rows, 128), F32) for rows in (ROWS_A, ROWS_B)],
        in_specs=[pl.BlockSpec(memory_space=pl.ANY)] * 9,
        out_specs=[pl.BlockSpec(memory_space=pltpu.VMEM)] * 2,
        scratch_shapes=[pltpu.VMEM(value.shape, F32) for value in arguments]
        + [pltpu.VMEM((48, 192), F32), pltpu.SemaphoreType.DMA((9,))],
        compiler_params=pltpu.CompilerParams(vmem_limit_bytes=60 * 1024 * 1024),
    )(*arguments)
    four_a = lax.all_to_all(half_a, "col", 0, 0)
    four_b = lax.all_to_all(half_b, "gy", 0, 0)
    four_a, four_b = lax.optimization_barrier((four_a, four_b))
    all_a = tell_all(four_a, "gy", 4)
    all_b = tell_all(four_b, "col", 4)

    dense, rhs, helm, vectors, small, boxes, state, up, down = call(
        unpack_body,
        [(512, 512), field, velocity, (NB, 192, 128), (NB, 48, 128), velocity, state_shape, wide, wide],
    )(all_a, all_b)

    def precondition(boxes, state, left, right):
        state, message = call(middle_body, [state_shape, state_shape])(dense, state, left, right)
        left_mid, right_mid = exchange(message, message)
        part, up, down = call(
            schwarz_body,
            [field, plane, plane],
            [pltpu.VMEM((8, 8, 8, 128), F32), pltpu.VMEM((8, 8, 8, 128), F32), pltpu.VMEM(velocity, F32)],
        )(boxes, vectors, small, left, right)
        state, up, down = call(late_body, [state_shape, wide, wide])(
            dense, state, left_mid, right_mid, up, down
        )
        left, right = exchange(up, down)
        z, t, up, down = call(gradient_body, [field, (NB, 1536, 128), plane, plane])(
            dense, state, left, right, part, small, forward
        )
        left, right = exchange(up, down)
        return z, t, left, right

    spread = [pltpu.VMEM((3072, 512), BF16)]
    left, right = exchange(up, down)
    (inverse,) = call(helm_body, [velocity])(helm, left, right)
    z, t, left, right = precondition(boxes, state, left, right)
    w, boxes, state, up, down = call(
        first_image_body, [field, velocity, state_shape, wide, wide], spread
    )(t, left, right, inverse, small, backward, dense)
    left, right = exchange(up, down)
    q, t, left, right = precondition(boxes, state, left, right)
    v, sums = call(last_image_body, [field, (8, 128)], spread)(
        t, left, right, inverse, small, backward, rhs, z, w, q
    )
    own = call(own_body, [(6, 6, 192)] * 4, scalars=1)(me, z, w, q, v, six.T.copy())
    sums = sum_slabs(sums)
    return tuple(
        pl.pallas_call(
            last_body,
            out_shape=[jax.ShapeDtypeStruct((6, 6, 192), F32)] * 2,
            in_specs=[pl.BlockSpec(memory_space=pltpu.VMEM)] * 6,
            out_specs=[pl.BlockSpec(memory_space=pl.ANY)] * 2,
            scratch_shapes=[pltpu.VMEM((6, 6, 192), F32)] * 2 + [pltpu.SemaphoreType.DMA((2,))],
            compiler_params=pltpu.CompilerParams(vmem_limit_bytes=40 * 1024 * 1024),
        )(sums, *own, divergence)
    )


def solution(mesh):
    in_specs = (
        P("gy", "col", "gx"),
        P(None, ("gx", "gy", "col")),
        P("gy", "col", "gx"),
        P(None, None, None, ("gx", "gy", "col")),
        P(None, None, ("gx", "gy", "col")),
        P(("gx", "gy", "col"), None),
        P("gx", "gy", "col"),
    )
    out_specs = (P("gy", "col", "gx"), P("gy", "col", "gx"))
    return jax.shard_map(local, mesh=mesh, in_specs=in_specs, out_specs=out_specs, check_vma=False)
```

```python
import jax
import jax.numpy as jnp
import ml_dtypes
import numpy as np
from jax import lax
from jax.experimental import pallas as pl
from jax.experimental.pallas import tpu as pltpu
from jax.sharding import PartitionSpec as P

EA = 32
CHEB = 6
NB = 4

LOBATTO_NODES = [
    -1.0,
    -0.8717401485096066,
    -0.5917001814331423,
    -0.2092992179024789,
    0.2092992179024789,
    0.5917001814331423,
    0.8717401485096066,
    1.0,
]
GAUSS_NODES = [
    -0.932469514203152,
    -0.6612093864662645,
    -0.2386191860831909,
    0.2386191860831909,
    0.6612093864662645,
    0.932469514203152,
]
GAUSS_WEIGHTS = [
    0.1713244923791704,
    0.3607615730481386,
    0.467913934572691,
    0.467913934572691,
    0.3607615730481386,
    0.1713244923791704,
]
SPECTRUM_LOW = 8.0
SPECTRUM_HIGH = 90.0
HIGHEST = lax.Precision.HIGHEST
F32 = jnp.float32
BF16 = jnp.bfloat16

ROWS_P = 288
ROWS_V = 512
ROWS = 312


def basis_tables():
    lobatto = np.array(LOBATTO_NODES)
    points = np.array(GAUSS_NODES)
    interp = np.ones((6, 8))
    slopes = np.zeros((6, 8))
    for p in range(6):
        for m in range(8):
            product = 1.0
            for q in range(8):
                if q != m:
                    product = product * (points[p] - lobatto[q]) / (lobatto[m] - lobatto[q])
            interp[p, m] = product
            running = 0.0
            for q in range(8):
                if q != m:
                    factor = 1.0 / (lobatto[m] - lobatto[q])
                    for k in range(8):
                        if k != m and k != q:
                            factor = factor * (points[p] - lobatto[k]) / (lobatto[m] - lobatto[k])
                    running = running + factor
            slopes[p, m] = running
    return interp, slopes


def gradient_tables():
    interp, slopes = basis_tables()
    weight = np.array(GAUSS_WEIGHTS)
    tables = []
    for comp in range(3):
        sides = [(slopes if side == comp else interp) * weight[:, None] for side in range(3)]
        full = np.zeros((8, 8, 8, 6, 6, 8))
        full[..., 1:7] = np.einsum("iu,jv,kw->wuvkij", sides[0], sides[1], sides[2])
        tables.append(full.reshape(ROWS_V, ROWS_P))
    table = np.concatenate(tables, axis=0).astype(np.float32)
    high = table.astype(ml_dtypes.bfloat16)
    low = (table - high.astype(np.float32)).astype(ml_dtypes.bfloat16)
    forward = np.concatenate([high, high, low], axis=1)
    backward = np.concatenate([high.T, high.T, low.T], axis=1)
    return forward, backward


def order_table(nodes):
    table = np.zeros((nodes * EA, nodes * EA), np.float32)
    for k in range(nodes):
        for a in range(EA):
            table[a * nodes + k, k * EA + a] = 1.0
    return table


def sweep_factors():
    center = (SPECTRUM_HIGH + SPECTRUM_LOW) / 2.0
    spread = (SPECTRUM_HIGH - SPECTRUM_LOW) / 2.0
    ratio_cs = center / spread
    rho_now = 1.0 / ratio_cs
    keep, add = [], []
    for _ in range(CHEB):
        rho_next = 1.0 / (2.0 * ratio_cs - rho_now)
        keep.append(rho_next * rho_now)
        add.append(2.0 * rho_next / spread)
        rho_now = rho_next
    return center, keep, add


CENTER, KEEP, ADD = sweep_factors()


def parity(value):
    return bin(value).count("1") % 2


def block_choice():
    def extend(taken):
        t = len(taken) + 1
        if t == 16:
            return taken
        for mask in range(1, 16):
            if mask not in taken and parity(mask & t):
                done = extend(taken + [mask])
                if done:
                    return done
        return None

    masks = extend([])
    return [[0] + [t for t in range(1, 16) if not parity(masks[t - 1] & r)] for r in range(16)]


BLOCKS = block_choice()


def lanes(shape):
    return lax.broadcasted_iota(jnp.int32, shape, len(shape) - 1)


def turn(value, shift):
    shift = shift % 128
    return value if shift == 0 else pltpu.roll(value, shift, value.ndim - 1)


def at_first(value, slot=0):
    moved = turn(value, 97 + slot)
    return jnp.where(lanes(moved.shape) % EA == 0, moved, 0.0)


def at_last(value, slot=0):
    moved = turn(value, 31 - slot)
    return jnp.where(lanes(moved.shape) % EA == EA - 1, moved, 0.0)


def pack_last(blocks):
    packed = None
    for slot, block in enumerate(blocks):
        part = turn(jnp.where(lanes(block.shape) % EA == EA - 1, block, 0.0), -slot)
        packed = part if packed is None else packed + part
    return packed


def pack_first(blocks):
    packed = None
    for slot, block in enumerate(blocks):
        part = turn(jnp.where(lanes(block.shape) % EA == 0, block, 0.0), slot)
        packed = part if packed is None else packed + part
    return packed


def times(dense_ref, vector):
    columns = jnp.concatenate([vector, jnp.zeros_like(vector)], axis=0).T
    total = None
    for b in range(NB):
        part = dense_ref[:, b * 128 : (b + 1) * 128, :] * columns[:, b : b + 1][None]
        total = part if total is None else total + part
    return jnp.sum(total, axis=1)


def sweep_begin(dense_ref, source, link):
    update = source * (1.0 / CENTER)
    remainder = source - times(dense_ref, update)
    free = KEEP[0] * update + ADD[0] * remainder
    state = jnp.concatenate([update, remainder, update, link], axis=0)
    return state, jnp.concatenate([update, free, link, link], axis=0)


def sweep_pair(dense_ref, state, from_left, from_right, sweep_at):
    update, remainder, solution, link = [state[4 * n : 4 * n + 4] for n in range(4)]
    left = at_first(from_left)
    right = at_last(from_right)
    place = lanes(update.shape) % EA
    link_left = left[8:12]
    link_right = jnp.where(place == EA - 1, link, 0.0)
    remainder = remainder + link_left * left[0:4] + link_right * right[0:4]
    left_next = left[4:8] + ADD[sweep_at] * link_left * update
    right_next = right[4:8] + ADD[sweep_at] * link_right * update
    update = KEEP[sweep_at] * update + ADD[sweep_at] * remainder
    solution = solution + update
    remainder = remainder - times(dense_ref, update)
    remainder = remainder + link_left * left_next + link_right * right_next
    update = KEEP[sweep_at + 1] * update + ADD[sweep_at + 1] * remainder
    solution = solution + update
    if sweep_at + 2 == CHEB:
        return solution
    remainder = remainder - times(dense_ref, update)
    free = KEEP[sweep_at + 2] * update + ADD[sweep_at + 2] * remainder
    state = jnp.concatenate([update, remainder, solution, link], axis=0)
    return state, jnp.concatenate([update, free, link, link], axis=0)


def fill_boxes(field_ref, box_ref):
    box_ref[...] = jnp.zeros(box_ref.shape, F32)
    for b in range(NB):
        for k in range(6):
            box_ref[b, (k + 1) * 64 + 8 : (k + 1) * 64 + 56, :] = field_ref[b, k * 48 : (k + 1) * 48, :]
        before = box_ref[b, pl.ds(6, 64, stride=8), :]
        after = box_ref[b, pl.ds(1, 64, stride=8), :]
        box_ref[b, pl.ds(0, 64, stride=8), :] = turn(before, 32)
        box_ref[b, pl.ds(7, 64, stride=8), :] = turn(after, -32)
    for b in range(NB):
        for k in range(1, 7):
            if b > 0:
                box_ref[b, k * 64 : k * 64 + 8, :] = box_ref[b - 1, k * 64 + 48 : k * 64 + 56, :]
            if b < NB - 1:
                box_ref[b, k * 64 + 56 : k * 64 + 64, :] = box_ref[b + 1, k * 64 + 8 : k * 64 + 16, :]


def begin_kernel_part(field_ref, small_ref, dense_ref, box_ref, state_ref, ahead_ref, behind_ref, extra):
    fill_boxes(field_ref, box_ref)
    source = jnp.concatenate(
        [jnp.sum(field_ref[b], axis=0, keepdims=True) for b in range(NB)], axis=0
    )
    link = jnp.concatenate([small_ref[b, 32:33, :] for b in range(NB)], axis=0)
    state, message = sweep_begin(dense_ref, source, link)
    state_ref[...] = state
    ahead_ref[0:16, :] = message
    behind_ref[0:16, :] = message
    ahead_ref[16:80, :] = pack_last([box_ref[b, 384:448, :] for b in range(NB)] + extra[0])
    behind_ref[16:80, :] = pack_first([box_ref[b, 64:128, :] for b in range(NB)] + extra[1])


def flip_blocks(value, mine_c):
    block = lanes(value.shape) // EA
    swapped = jnp.where(block % 2 == 0, turn(value, -32), turn(value, 32))
    value = jnp.where((mine_c & 1) == 1, swapped, value)
    return jnp.where((mine_c & 2) == 2, turn(value, 64), value)


def place_blocks(pieces):
    total = None
    for value, source, target in pieces:
        part = jnp.where(lanes(value.shape) // EA == target, turn(value, (target - source) * 32), 0.0)
        total = part if total is None else total + part
    return total


def pack_body(*refs):
    me_ref, sources, (out_ref, own_ref), held, (tmp, common, tiles, ready) = (
        refs[0], refs[1:10], refs[10:12], refs[12:21], refs[21:]
    )
    copies = [pltpu.make_async_copy(sources[n], held[n], ready.at[n]) for n in range(9)]
    for copy in copies:
        copy.start()
    for copy in copies:
        copy.wait()
    rhs_ref, helm_ref, vec_ref, val_ref, size_ref, rows_ref, link_ref, six_ref, eight_ref = held
    mine_b = me_ref[0]
    mine_c = me_ref[1]
    for t in range(4):
        tiles[t] = rows_ref[:, t * 128 : (t + 1) * 128]
    for t in range(4):
        own_ref[t] = flip_blocks(tiles[mine_b ^ t], mine_c)
    tmp[...] = jnp.zeros(tmp.shape, F32)
    for i in range(6):
        tmp[i * 6 : i * 6 + 6, :] = rhs_ref[i]
    nodes = jnp.dot(tmp[...], six_ref[...], precision=HIGHEST, preferred_element_type=F32)
    common[0:40, :] = nodes[:, 0:128]
    common[40:80, :] = jnp.zeros((40, 128), F32)
    common[40:80, 0:64] = nodes[:, 128:192]
    common[40:64, 64:96] = val_ref[...]
    common[64:67, 64:96] = size_ref[...]
    common[72:73, 64:96] = jnp.broadcast_to(link_ref[0], (1, 32))
    common[40:80, 96:128] = vec_ref[0:40, :]
    common[80:120, :] = jnp.zeros((40, 128), F32)
    for t in range(4):
        rows = 40 if t < 3 else 32
        common[80 : 80 + rows, t * 32 : (t + 1) * 32] = vec_ref[40 + t * 40 : 40 + t * 40 + rows, :]
    helm = jnp.dot(
        helm_ref[...].reshape(64, 256), eight_ref[...], precision=HIGHEST, preferred_element_type=F32
    )
    common[120:184, :] = helm[:, 0:128]
    common[184:248, :] = helm[:, 128:256]
    for r in range(16):
        other = ((mine_b ^ (r >> 2)) << 2) | (mine_c ^ (r & 3))
        out_ref[other, 64:312, :] = common[...]
        for half in range(2):
            chosen = BLOCKS[r][half * 4 : half * 4 + 4]
            out_ref[other, half * 32 : half * 32 + 32, :] = place_blocks(
                [(own_ref[t >> 2], t & 3, n) for n, t in enumerate(chosen)]
            )


def joined(column, start, rows, quarter):
    return place_blocks([(column[c][start : start + rows, :], quarter, c) for c in range(4)])


def unpack_body(
    me_ref, all_ref, own_ref,
    dense_ref, rhs_ref, helm_ref, vec_ref, small_ref, box_ref, state_ref, ahead_ref, behind_ref, near,
):
    mine_b = me_ref[0]
    mine_c = me_ref[1]
    for t in range(4):
        near[t, 0:32, :] = own_ref[t]
    for r in range(1, 16):
        other = ((mine_b ^ (r >> 2)) << 2) | (mine_c ^ (r & 3))
        halves = [all_ref[other, half * 32 : half * 32 + 32, :] for half in range(2)]
        for tile in range(4):
            pieces = []
            for q in range(4):
                t = r ^ (tile * 4 + q)
                if t in BLOCKS[r]:
                    slot = BLOCKS[r].index(t)
                    pieces.append((halves[slot // 4], slot % 4, q))
            near[tile, r * 32 : r * 32 + 32, :] = place_blocks(pieces) if pieces else jnp.zeros((32, 128), F32)
    row_block = lax.broadcasted_iota(jnp.int32, (128, 128), 0) // 32
    for tile in range(4):
        for row_tile in range(4):
            mirrored = near[row_tile, tile * 128 : (tile + 1) * 128, :].T
            if tile == row_tile:
                mirrored = jnp.where(row_block == lanes((128, 128)) // EA, 0.0, mirrored)
            value = near[tile, row_tile * 128 : (row_tile + 1) * 128, :] + mirrored
            value = flip_blocks(value, mine_c)
            for q in range(4):
                start = pl.multiple_of((mine_b ^ row_tile) * 128 + (mine_c ^ q) * 32, 32)
                dense_ref[mine_b ^ tile, pl.ds(start, 32), :] = value[q * 32 : (q + 1) * 32, :]
    rhs_ref[...] = jnp.zeros(rhs_ref.shape, F32)
    for b in range(NB):
        column = [all_ref.at[b * 4 + c] for c in range(4)]
        for k in range(6):
            value = joined(column, 64 + 40 * (k // 4), 40, k % 4)
            for i in range(6):
                rhs_ref[b, k * 48 + i * 8 + 1 : k * 48 + i * 8 + 7, :] = value[i * 6 : i * 6 + 6, :]
        small_ref[b, :, :] = joined(column, 104, 40, 2)
        vec_ref[b, 0:40, :] = joined(column, 104, 40, 3)
        for t in range(4):
            rows = 40 if t < 3 else 32
            vec_ref[b, 40 + t * 40 : 40 + t * 40 + rows, :] = joined(column, 144, rows, t)
        for k in range(8):
            helm_ref[b, k * 64 : (k + 1) * 64, :] = joined(column, 184 + 64 * (k // 4), 64, k % 4)
    begin_kernel_part(
        rhs_ref, small_ref, dense_ref, box_ref, state_ref, ahead_ref, behind_ref,
        ([helm_ref[b, 448:512, :] for b in range(NB)], [helm_ref[b, 0:64, :] for b in range(NB)]),
    )


def middle_body(dense_ref, state_ref, left_ref, right_ref, state_out, message_out):
    state, message = sweep_pair(dense_ref, state_ref[...], left_ref[0:16, :], right_ref[0:16, :], 0)
    state_out[...] = state
    message_out[...] = message


def late_body(dense_ref, state_ref, left_ref, right_ref, up_ref, down_ref, state_out, ahead_ref, behind_ref):
    state, message = sweep_pair(dense_ref, state_ref[...], left_ref[...], right_ref[...], 2)
    state_out[...] = state
    ahead_ref[0:16, :] = message
    behind_ref[0:16, :] = message
    ahead_ref[16:80, :] = up_ref[...]
    behind_ref[16:80, :] = down_ref[...]


def join_rows(ref, groups, cross):
    for b in range(NB):
        low = ref[b, pl.ds(0, groups * 8, stride=8), :]
        high = ref[b, pl.ds(7, groups * 8, stride=8), :]
        ref[b, pl.ds(0, groups * 8, stride=8), :] = low + turn(high, 32)
        ref[b, pl.ds(7, groups * 8, stride=8), :] = high + turn(low, -32)
    for b in range(NB - 1):
        for g in range(groups):
            both = ref[b, g * 64 + 56 : g * 64 + 64, :] + ref[b + 1, g * 64 : g * 64 + 8, :]
            ref[b, g * 64 + 56 : g * 64 + 64, :] = both
            ref[b + 1, g * 64 : g * 64 + 8, :] = both


def join_layers(low, high):
    place = lanes(low.shape) % EA
    new_low = low + jnp.where(place > 0, turn(high, 1), 0.0)
    new_high = high + jnp.where(place < EA - 1, turn(low, -1), 0.0)
    return new_low, new_high


def helm_body(helm_ref, left_ref, right_ref, out_ref):
    out_ref[...] = helm_ref[...]
    for b in range(NB):
        low, high = join_layers(helm_ref[b, 0:64, :], helm_ref[b, 448:512, :])
        out_ref[b, 0:64, :] = low + at_first(left_ref[16:80, :], 4 + b)
        out_ref[b, 448:512, :] = high + at_last(right_ref[16:80, :], 4 + b)
    join_rows(out_ref, 8, None)
    for b in range(NB):
        out_ref[b] = 1.0 / out_ref[b]


def schwarz_body(box_ref, vec_ref, small_ref, left_ref, right_ref, out_ref, up_ref, down_ref, one, two, full):
    def element_row(b, carry):
        def row(side, first, second):
            return vec_ref[b, pl.ds(side * 64 + first * 8 + second, 1), :]

        last = pltpu.roll(box_ref[b, 384:448, :], 1, 1)
        first = pltpu.roll(box_ref[b, 64:128, :], 127, 1)
        place = lanes((64, 128)) % EA
        from_left = pltpu.roll(left_ref[16:80, :], 97 + b, 1)
        from_right = pltpu.roll(right_ref[16:80, :], 31 - b, 1)
        one[0] = jnp.where(place == 0, from_left, last).reshape(8, 8, 128)
        one[7] = jnp.where(place == EA - 1, from_right, first).reshape(8, 8, 128)
        one[1:7] = box_ref[b, 64:448, :].reshape(6, 8, 8, 128)
        for m in range(8):
            total = None
            for i in range(8):
                part = one[:, i] * row(0, i, m)[None]
                total = part if total is None else total + part
            two[:, m] = total
        for m in range(8):
            total = None
            for i in range(8):
                part = two[i] * row(2, i, m)[None]
                total = part if total is None else total + part
            one[m] = total
        for k in range(8):
            total = None
            for j in range(8):
                part = one[k, :, j : j + 1, :] * vec_ref[b, 64 + j * 8 : 72 + j * 8, :][None]
                total = part if total is None else total + part
            bottom = small_ref[b, 0:8, :][:, None, :] + small_ref[b, 8:16, :][None, :, :]
            two[k] = total / (bottom + small_ref[b, 16 + k : 17 + k, :][None])
        for k in range(8):
            total = None
            for n in range(8):
                part = two[k, :, n : n + 1, :] * vec_ref[b, pl.ds(64 + n, 8, stride=8), :][None]
                total = part if total is None else total + part
            one[k] = total
        for i in range(8):
            total = None
            for m in range(8):
                part = one[m] * row(2, i, m)[None]
                total = part if total is None else total + part
            two[i] = total
        for i in range(8):
            total = None
            for m in range(8):
                part = two[:, m] * row(0, i, m)[None]
                total = part if total is None else total + part
            one[:, i] = total
        full[b] = one[...].reshape(512, 128)
        return carry

    lax.fori_loop(0, NB, element_row, 0)
    for b in range(NB):
        low = full[b, pl.ds(0, 64, stride=8), :]
        high = full[b, pl.ds(7, 64, stride=8), :]
        full[b, pl.ds(6, 64, stride=8), :] = full[b, pl.ds(6, 64, stride=8), :] + turn(low, -32)
        full[b, pl.ds(1, 64, stride=8), :] = full[b, pl.ds(1, 64, stride=8), :] + turn(high, 32)
        full[b, pl.ds(0, 64, stride=8), :] = jnp.zeros((64, 128), F32)
        full[b, pl.ds(7, 64, stride=8), :] = jnp.zeros((64, 128), F32)
    for b in range(NB - 1):
        for k in range(8):
            full[b, k * 64 + 48 : k * 64 + 56, :] = (
                full[b, k * 64 + 48 : k * 64 + 56, :] + full[b + 1, k * 64 : k * 64 + 8, :]
            )
            full[b + 1, k * 64 + 8 : k * 64 + 16, :] = (
                full[b + 1, k * 64 + 8 : k * 64 + 16, :] + full[b, k * 64 + 56 : k * 64 + 64, :]
            )
    up_ref[...] = pack_last([full[b, 448:512, :] for b in range(NB)])
    down_ref[...] = pack_first([full[b, 0:64, :] for b in range(NB)])
    place = lanes((48, 128)) % EA
    for b in range(NB):
        for k in range(6):
            value = full[b, (k + 1) * 64 + 8 : (k + 1) * 64 + 56, :]
            if k == 0:
                value = value + jnp.where(place > 0, turn(full[b, 456:504, :], 1), 0.0)
            if k == 5:
                value = value + jnp.where(place < EA - 1, turn(full[b, 8:56, :], -1), 0.0)
            out_ref[b, k * 48 : (k + 1) * 48, :] = value


def volume_factors(small_ref, b):
    size = [small_ref[b, 24 + d : 25 + d, :] for d in range(3)]
    volume = size[0] * size[1] * size[2] * 0.125
    return [volume * (2.0 / size[d]) for d in range(3)]


def split_parts(value):
    high = value.astype(BF16)
    return high, (value - high.astype(F32)).astype(BF16)


def gradient_body(
    dense_ref, state_ref, left_ref, right_ref, part_ref, small_ref, table_ref, z_ref, t_ref, ahead_ref, behind_ref
):
    solution = sweep_pair(dense_ref, state_ref[...], left_ref[0:16, :], right_ref[0:16, :], 4)
    inside = lax.broadcasted_iota(jnp.int32, (ROWS_P, 128), 0) % 8
    inside = (inside > 0) & (inside < 7)
    for b in range(NB):
        coarse = jnp.where(inside, solution[b : b + 1, :], 0.0)
        z_ref[b] = part_ref[b] + coarse
        z_ref[b, 0:48, :] = z_ref[b, 0:48, :] + at_first(left_ref[24:72, :], b)
        z_ref[b, 240:288, :] = z_ref[b, 240:288, :] + at_last(right_ref[24:72, :], b)
    parts = [split_parts(z_ref[b]) for b in range(NB)]
    high = jnp.concatenate([part[0] for part in parts], axis=1)
    low = jnp.concatenate([part[1] for part in parts], axis=1)
    both = jnp.concatenate([high, low, high], axis=0)
    factors = [volume_factors(small_ref, b) for b in range(NB)]
    for d in range(3):
        result = jnp.dot(table_ref[d * 512 : (d + 1) * 512, :], both, preferred_element_type=F32)
        for b in range(NB):
            t_ref[b, d * 512 : (d + 1) * 512, :] = result[:, b * 128 : (b + 1) * 128] * factors[b][d]
    join_rows(t_ref, 24, None)
    lows = [t_ref[b, d * 512 : d * 512 + 64, :] for b in range(NB) for d in range(3)]
    highs = [t_ref[b, d * 512 + 448 : d * 512 + 512, :] for b in range(NB) for d in range(3)]
    ahead_ref[...] = pack_last(highs)
    behind_ref[...] = pack_first(lows)
    for b in range(NB):
        for d in range(3):
            low, high = join_layers(lows[b * 3 + d], highs[b * 3 + d])
            t_ref[b, d * 512 : d * 512 + 64, :] = low
            t_ref[b, d * 512 + 448 : d * 512 + 512, :] = high


def divergence_part(t_ref, left_ref, right_ref, inverse_ref, small_ref, table_ref, image_ref, spread):
    for b in range(NB):
        factors = volume_factors(small_ref, b)
        for d in range(3):
            base = d * 512
            for start, rows, extra in (
                (0, 64, at_first(left_ref[...], b * 3 + d)),
                (64, 384, None),
                (448, 64, at_last(right_ref[...], b * 3 + d)),
            ):
                value = t_ref[b, base + start : base + start + rows, :]
                if extra is not None:
                    value = value + extra
                value = value * inverse_ref[b, start : start + rows, :] * factors[d]
                high, low = split_parts(value)
                spread[base + start : base + start + rows, b * 128 : (b + 1) * 128] = high
                spread[1536 + base + start : 1536 + base + start + rows, b * 128 : (b + 1) * 128] = low
    image = jnp.dot(table_ref[:, 0:3072], spread[...], preferred_element_type=F32)
    image = image + jnp.dot(table_ref[:, 3072:4608], spread[0:1536, :], preferred_element_type=F32)
    for b in range(NB):
        image_ref[b] = image[:, b * 128 : (b + 1) * 128]


def first_image_body(
    t_ref, left_ref, right_ref, inverse_ref, small_ref, table_ref, dense_ref,
    image_ref, box_ref, state_ref, ahead_ref, behind_ref, spread,
):
    divergence_part(t_ref, left_ref, right_ref, inverse_ref, small_ref, table_ref, image_ref, spread)
    begin_kernel_part(
        image_ref, small_ref, dense_ref, box_ref, state_ref, ahead_ref, behind_ref, ([], [])
    )


def last_image_body(t_ref, left_ref, right_ref, inverse_ref, small_ref, table_ref, image_ref, spread):
    divergence_part(t_ref, left_ref, right_ref, inverse_ref, small_ref, table_ref, image_ref, spread)


def products_body(r_ref, z_ref, w_ref, q_ref, sums_ref):
    sums_ref[...] = jnp.zeros(sums_ref.shape, F32)
    for n, (one, two) in enumerate(((r_ref, z_ref), (z_ref, w_ref), (w_ref, q_ref), (r_ref, q_ref))):
        total = None
        for b in range(NB):
            part = jnp.sum(one[b] * two[b], axis=0, keepdims=True)
            total = part if total is None else total + part
        sums_ref[n : n + 1, :] = total


def energy_body(t_ref, left_ref, right_ref, inverse_ref, products_ref, sums_ref):
    row = lax.broadcasted_iota(jnp.int32, (64, 128), 0)
    i, j = row // 8, row % 8
    total = None
    for b in range(NB):
        share = jnp.where((j == 0) | (j == 7), 0.5, 1.0)
        shared_b = ((i == 0) & (b > 0)) | ((i == 7) & (b < NB - 1))
        share = jnp.where(shared_b, 0.5 * share, share)
        for k in range(8):
            squares = None
            for d in range(3):
                value = t_ref[b, d * 512 + k * 64 : d * 512 + k * 64 + 64, :]
                if k == 0:
                    value = value + at_first(left_ref[...], b * 3 + d)
                if k == 7:
                    value = value + at_last(right_ref[...], b * 3 + d)
                squares = value * value if squares is None else squares + value * value
            part = squares * inverse_ref[b, k * 64 : k * 64 + 64, :] * share
            if k in (0, 7):
                part = part * 0.5
            total = part if total is None else total + part
    sums_ref[...] = products_ref[...]
    sums_ref[4:5, :] = jnp.sum(total, axis=0, keepdims=True)


def own_body(me_ref, z_ref, w_ref, q_ref, v_ref, table_ref, z_out, w_out, q_out, v_out):
    mine_b = me_ref[0]
    mine_c = me_ref[1]
    for field_ref, out_ref in ((z_ref, z_out), (w_ref, w_out), (q_ref, q_out), (v_ref, v_out)):
        moved = pltpu.roll(field_ref[mine_b], ((4 - mine_c) & 3) * 32, 1)
        nodes = jnp.concatenate([moved[k * 48 : (k + 1) * 48, 0:32] for k in range(6)], axis=1)
        nodes = jnp.dot(nodes, table_ref[...], precision=HIGHEST, preferred_element_type=F32)
        for i in range(6):
            out_ref[i] = nodes[i * 8 + 1 : i * 8 + 7, :]


def last_body(
    sums_ref, z_ref, w_ref, q_ref, v_ref, rhs_ref, pressure_ref, residual_ref, pressure, residual, done
):
    totals = jnp.sum(jnp.sum(sums_ref[...], axis=0), axis=1, keepdims=True)
    rz, zw, wq, rq, qv = [totals[n : n + 1] for n in range(5)]
    step_first = rz / zw
    rz_next = step_first * (step_first * wq - rq)
    share = 1.0 + rz_next / rz
    curvature = share * share * zw - 2.0 * share * step_first * wq + step_first * step_first * qv
    step_next = rz_next / curvature
    z_factor = (step_first + step_next * share)[None]
    q_factor = (step_next * step_first)[None]
    pressure[...] = z_factor * z_ref[...] - q_factor * q_ref[...]
    first = pltpu.make_async_copy(pressure, pressure_ref, done.at[0])
    first.start()
    residual[...] = rhs_ref[...] - z_factor * w_ref[...] + q_factor * v_ref[...]
    second = pltpu.make_async_copy(residual, residual_ref, done.at[1])
    second.start()
    first.wait()
    second.wait()


def call(body, outs, scratch=(), scalars=0):
    vmem = pl.BlockSpec(memory_space=pltpu.VMEM)
    smem = pl.BlockSpec(memory_space=pltpu.SMEM)

    def run(*operands):
        return pl.pallas_call(
            body,
            out_shape=[jax.ShapeDtypeStruct(shape, F32) for shape in outs],
            in_specs=[smem] * scalars + [vmem] * (len(operands) - scalars),
            out_specs=[vmem] * len(outs),
            scratch_shapes=list(scratch),
            compiler_params=pltpu.CompilerParams(vmem_limit_bytes=40 * 1024 * 1024),
        )(*operands)

    return run


def tell_all(block, axes, count):
    return lax.all_to_all(jnp.broadcast_to(block[None], (count,) + block.shape), axes, 0, 0)


def sum_slabs(sums):
    slabs, across, around = (lax.axis_size(axis) for axis in ("gx", "gy", "col"))
    group = across * around
    chips = slabs // 2
    assert chips == group
    total = None
    for core in range(2):
        pairs = []
        for slab in range(slabs):
            for n in range(group):
                source = (slab // 2 + n) % chips * 2 + (slab + core) % 2
                pairs.append((source * group + n, slab * group + n))
        part = lax.ppermute(sums, ("gx", "gy", "col"), pairs)
        total = part if total is None else total + part
    return tell_all(total, ("gy", "col"), group)


def local(divergence, elem_size, helm_diag, fdm_vectors, fdm_values, coarse_rows, axial_link):
    count = lax.axis_size("gx")
    ahead = [(i, (i + 1) % count) for i in range(count)]
    behind = [((i + 1) % count, i) for i in range(count)]

    def exchange(up, down):
        return lax.ppermute(up, "gx", ahead), lax.ppermute(down, "gx", behind)

    forward, backward = gradient_tables()
    six = order_table(6)
    me = jnp.stack([lax.axis_index("gy"), lax.axis_index("col")]).astype(jnp.int32)
    field = (NB, ROWS_P, 128)
    velocity = (NB, ROWS_V, 128)
    state_shape = (16, 128)
    wide = (80, 128)
    plane = (64, 128)

    arguments = (
        divergence,
        helm_diag,
        fdm_vectors.reshape(192, EA),
        fdm_values.reshape(24, EA),
        elem_size,
        coarse_rows,
        axial_link,
        six,
        order_table(8),
    )
    vmem = pl.BlockSpec(memory_space=pltpu.VMEM)
    own_part, own_rows = pl.pallas_call(
        pack_body,
        out_shape=[jax.ShapeDtypeStruct((16, ROWS, 128), F32), jax.ShapeDtypeStruct((4, 32, 128), F32)],
        in_specs=[pl.BlockSpec(memory_space=pltpu.SMEM)] + [pl.BlockSpec(memory_space=pl.ANY)] * 9,
        out_specs=[vmem, vmem],
        scratch_shapes=[pltpu.VMEM(value.shape, F32) for value in arguments]
        + [
            pltpu.VMEM((40, 192), F32),
            pltpu.VMEM((248, 128), F32),
            pltpu.VMEM((4, 32, 128), F32),
            pltpu.SemaphoreType.DMA((9,)),
        ],
        compiler_params=pltpu.CompilerParams(vmem_limit_bytes=40 * 1024 * 1024),
    )(me, *arguments)
    everything = lax.all_to_all(own_part, ("gy", "col"), 0, 0)

    dense, rhs, helm, vectors, small, boxes, state, up, down = call(
        unpack_body,
        [(4, 512, 128), field, velocity, (NB, 192, 128), (NB, 40, 128), velocity, state_shape, wide, wide],
        [pltpu.VMEM((4, 512, 128), F32)],
        scalars=1,
    )(me, everything, own_rows)

    def precondition(boxes, state, left, right):
        state, message = call(middle_body, [state_shape, state_shape])(dense, state, left, right)
        left_mid, right_mid = exchange(message, message)
        part, up, down = call(
            schwarz_body,
            [field, plane, plane],
            [pltpu.VMEM((8, 8, 8, 128), F32), pltpu.VMEM((8, 8, 8, 128), F32), pltpu.VMEM(velocity, F32)],
        )(boxes, vectors, small, left, right)
        state, up, down = call(late_body, [state_shape, wide, wide])(
            dense, state, left_mid, right_mid, up, down
        )
        left, right = exchange(up, down)
        z, t, up, down = call(gradient_body, [field, (NB, 1536, 128), plane, plane])(
            dense, state, left, right, part, small, forward
        )
        left, right = exchange(up, down)
        return z, t, left, right

    spread = [pltpu.VMEM((3072, 512), BF16)]
    left, right = exchange(up, down)
    (inverse,) = call(helm_body, [velocity])(helm, left, right)
    z, t, left, right = precondition(boxes, state, left, right)
    w, boxes, state, up, down = call(
        first_image_body, [field, velocity, state_shape, wide, wide], spread
    )(t, left, right, inverse, small, backward, dense)
    left, right = exchange(up, down)
    q, t, left, right = precondition(boxes, state, left, right)
    (products,) = call(products_body, [(8, 128)])(rhs, z, w, q)
    (sums,) = call(energy_body, [(8, 128)])(t, left, right, inverse, products)
    sums = sum_slabs(sums)
    (v,) = call(last_image_body, [field], spread)(t, left, right, inverse, small, backward)
    own = call(own_body, [(6, 6, 192)] * 4, scalars=1)(me, z, w, q, v, six.T.copy())
    return tuple(
        pl.pallas_call(
            last_body,
            out_shape=[jax.ShapeDtypeStruct((6, 6, 192), F32)] * 2,
            in_specs=[pl.BlockSpec(memory_space=pltpu.VMEM)] * 6,
            out_specs=[pl.BlockSpec(memory_space=pl.ANY)] * 2,
            scratch_shapes=[pltpu.VMEM((6, 6, 192), F32)] * 2 + [pltpu.SemaphoreType.DMA((2,))],
            compiler_params=pltpu.CompilerParams(vmem_limit_bytes=40 * 1024 * 1024),
        )(sums, *own, divergence)
    )


def solution(mesh):
    in_specs = (
        P("gy", "col", "gx"),
        P(None, ("gx", "gy", "col")),
        P("gy", "col", "gx"),
        P(None, None, None, ("gx", "gy", "col")),
        P(None, None, ("gx", "gy", "col")),
        P(("gx", "gy", "col"), None),
        P("gx", "gy", "col"),
    )
    out_specs = (P("gy", "col", "gx"), P("gy", "col", "gx"))
    return jax.shard_map(local, mesh=mesh, in_specs=in_specs, out_specs=out_specs, check_vma=False)
```

```python
import jax
import jax.numpy as jnp
import ml_dtypes
import numpy as np
from jax import lax
from jax.experimental import pallas as pl
from jax.experimental.pallas import tpu as pltpu
from jax.sharding import PartitionSpec as P

EA = 32
CHEB = 6
NB = 4

LOBATTO_NODES = [
    -1.0,
    -0.8717401485096066,
    -0.5917001814331423,
    -0.2092992179024789,
    0.2092992179024789,
    0.5917001814331423,
    0.8717401485096066,
    1.0,
]
GAUSS_NODES = [
    -0.932469514203152,
    -0.6612093864662645,
    -0.2386191860831909,
    0.2386191860831909,
    0.6612093864662645,
    0.932469514203152,
]
GAUSS_WEIGHTS = [
    0.1713244923791704,
    0.3607615730481386,
    0.467913934572691,
    0.467913934572691,
    0.3607615730481386,
    0.1713244923791704,
]
SPECTRUM_LOW = 8.0
SPECTRUM_HIGH = 90.0
HIGHEST = lax.Precision.HIGHEST
F32 = jnp.float32
BF16 = jnp.bfloat16

ROWS_P = 288
ROWS_V = 512
ROWS = 312


def basis_tables():
    lobatto = np.array(LOBATTO_NODES)
    points = np.array(GAUSS_NODES)
    interp = np.ones((6, 8))
    slopes = np.zeros((6, 8))
    for p in range(6):
        for m in range(8):
            product = 1.0
            for q in range(8):
                if q != m:
                    product = product * (points[p] - lobatto[q]) / (lobatto[m] - lobatto[q])
            interp[p, m] = product
            running = 0.0
            for q in range(8):
                if q != m:
                    factor = 1.0 / (lobatto[m] - lobatto[q])
                    for k in range(8):
                        if k != m and k != q:
                            factor = factor * (points[p] - lobatto[k]) / (lobatto[m] - lobatto[k])
                    running = running + factor
            slopes[p, m] = running
    return interp, slopes


def gradient_tables():
    interp, slopes = basis_tables()
    weight = np.array(GAUSS_WEIGHTS)
    tables = []
    for comp in range(3):
        sides = [(slopes if side == comp else interp) * weight[:, None] for side in range(3)]
        full = np.zeros((8, 8, 8, 6, 6, 8))
        full[..., 1:7] = np.einsum("iu,jv,kw->wuvkij", sides[0], sides[1], sides[2])
        tables.append(full.reshape(ROWS_V, ROWS_P))
    table = np.concatenate(tables, axis=0).astype(np.float32)
    high = table.astype(ml_dtypes.bfloat16)
    low = (table - high.astype(np.float32)).astype(ml_dtypes.bfloat16)
    forward = np.concatenate([high, high, low], axis=1)
    backward = np.concatenate([high.T, high.T, low.T], axis=1)
    return forward, backward


def order_table(nodes):
    table = np.zeros((nodes * EA, nodes * EA), np.float32)
    for k in range(nodes):
        for a in range(EA):
            table[a * nodes + k, k * EA + a] = 1.0
    return table


def sweep_factors():
    center = (SPECTRUM_HIGH + SPECTRUM_LOW) / 2.0
    spread = (SPECTRUM_HIGH - SPECTRUM_LOW) / 2.0
    ratio_cs = center / spread
    rho_now = 1.0 / ratio_cs
    keep, add = [], []
    for _ in range(CHEB):
        rho_next = 1.0 / (2.0 * ratio_cs - rho_now)
        keep.append(rho_next * rho_now)
        add.append(2.0 * rho_next / spread)
        rho_now = rho_next
    return center, keep, add


CENTER, KEEP, ADD = sweep_factors()


def parity(value):
    return bin(value).count("1") % 2


def block_choice():
    def extend(taken):
        t = len(taken) + 1
        if t == 16:
            return taken
        for mask in range(1, 16):
            if mask not in taken and parity(mask & t):
                done = extend(taken + [mask])
                if done:
                    return done
        return None

    masks = extend([])
    return [[0] + [t for t in range(1, 16) if not parity(masks[t - 1] & r)] for r in range(16)]


BLOCKS = block_choice()


def lanes(shape):
    return lax.broadcasted_iota(jnp.int32, shape, len(shape) - 1)


def turn(value, shift):
    shift = shift % 128
    return value if shift == 0 else pltpu.roll(value, shift, value.ndim - 1)


def at_first(value, slot=0):
    moved = turn(value, 97 + slot)
    return jnp.where(lanes(moved.shape) % EA == 0, moved, 0.0)


def at_last(value, slot=0):
    moved = turn(value, 31 - slot)
    return jnp.where(lanes(moved.shape) % EA == EA - 1, moved, 0.0)


def pack_last(blocks):
    packed = None
    for slot, block in enumerate(blocks):
        part = turn(jnp.where(lanes(block.shape) % EA == EA - 1, block, 0.0), -slot)
        packed = part if packed is None else packed + part
    return packed


def pack_first(blocks):
    packed = None
    for slot, block in enumerate(blocks):
        part = turn(jnp.where(lanes(block.shape) % EA == 0, block, 0.0), slot)
        packed = part if packed is None else packed + part
    return packed


def times(dense_ref, vector):
    columns = jnp.concatenate([vector, jnp.zeros_like(vector)], axis=0).T
    total = None
    for b in range(NB):
        part = dense_ref[:, b * 128 : (b + 1) * 128, :] * columns[:, b : b + 1][None]
        total = part if total is None else total + part
    return jnp.sum(total, axis=1)


def sweep_begin(dense_ref, source, link):
    update = source * (1.0 / CENTER)
    remainder = source - times(dense_ref, update)
    free = KEEP[0] * update + ADD[0] * remainder
    state = jnp.concatenate([update, remainder, update, link], axis=0)
    return state, jnp.concatenate([update, free, link, link], axis=0)


def sweep_pair(dense_ref, state, from_left, from_right, sweep_at):
    update, remainder, solution, link = [state[4 * n : 4 * n + 4] for n in range(4)]
    left = at_first(from_left)
    right = at_last(from_right)
    place = lanes(update.shape) % EA
    link_left = left[8:12]
    link_right = jnp.where(place == EA - 1, link, 0.0)
    remainder = remainder + link_left * left[0:4] + link_right * right[0:4]
    left_next = left[4:8] + ADD[sweep_at] * link_left * update
    right_next = right[4:8] + ADD[sweep_at] * link_right * update
    update = KEEP[sweep_at] * update + ADD[sweep_at] * remainder
    solution = solution + update
    remainder = remainder - times(dense_ref, update)
    remainder = remainder + link_left * left_next + link_right * right_next
    update = KEEP[sweep_at + 1] * update + ADD[sweep_at + 1] * remainder
    solution = solution + update
    if sweep_at + 2 == CHEB:
        return solution
    remainder = remainder - times(dense_ref, update)
    free = KEEP[sweep_at + 2] * update + ADD[sweep_at + 2] * remainder
    state = jnp.concatenate([update, remainder, solution, link], axis=0)
    return state, jnp.concatenate([update, free, link, link], axis=0)


def fill_boxes(field_ref, box_ref):
    box_ref[...] = jnp.zeros(box_ref.shape, F32)
    for b in range(NB):
        for k in range(6):
            box_ref[b, (k + 1) * 64 + 8 : (k + 1) * 64 + 56, :] = field_ref[b, k * 48 : (k + 1) * 48, :]
        before = box_ref[b, pl.ds(6, 64, stride=8), :]
        after = box_ref[b, pl.ds(1, 64, stride=8), :]
        box_ref[b, pl.ds(0, 64, stride=8), :] = turn(before, 32)
        box_ref[b, pl.ds(7, 64, stride=8), :] = turn(after, -32)
    for b in range(NB):
        for k in range(1, 7):
            if b > 0:
                box_ref[b, k * 64 : k * 64 + 8, :] = box_ref[b - 1, k * 64 + 48 : k * 64 + 56, :]
            if b < NB - 1:
                box_ref[b, k * 64 + 56 : k * 64 + 64, :] = box_ref[b + 1, k * 64 + 8 : k * 64 + 16, :]


def begin_kernel_part(field_ref, small_ref, dense_ref, box_ref, state_ref, ahead_ref, behind_ref, extra):
    fill_boxes(field_ref, box_ref)
    source = jnp.concatenate(
        [jnp.sum(field_ref[b], axis=0, keepdims=True) for b in range(NB)], axis=0
    )
    link = jnp.concatenate([small_ref[b, 32:33, :] for b in range(NB)], axis=0)
    state, message = sweep_begin(dense_ref, source, link)
    state_ref[...] = state
    ahead_ref[0:16, :] = message
    behind_ref[0:16, :] = message
    ahead_ref[16:80, :] = pack_last([box_ref[b, 384:448, :] for b in range(NB)] + extra[0])
    behind_ref[16:80, :] = pack_first([box_ref[b, 64:128, :] for b in range(NB)] + extra[1])


def flip_blocks(value, mine_c):
    block = lanes(value.shape) // EA
    swapped = jnp.where(block % 2 == 0, turn(value, -32), turn(value, 32))
    value = jnp.where((mine_c & 1) == 1, swapped, value)
    return jnp.where((mine_c & 2) == 2, turn(value, 64), value)


def place_blocks(pieces):
    total = None
    for value, source, target in pieces:
        part = jnp.where(lanes(value.shape) // EA == target, turn(value, (target - source) * 32), 0.0)
        total = part if total is None else total + part
    return total


def pack_body(*refs):
    me_ref, sources, (out_ref, tiles), held, (tmp, common, own_ref, ready) = (
        refs[0], refs[1:10], refs[10:12], refs[12:21], refs[21:]
    )
    copies = [pltpu.make_async_copy(sources[n], held[n], ready.at[n]) for n in range(9)]
    for copy in copies:
        copy.start()
    for copy in copies:
        copy.wait()
    rhs_ref, helm_ref, vec_ref, val_ref, size_ref, rows_ref, link_ref, six_ref, eight_ref = held
    mine_b = me_ref[0]
    mine_c = me_ref[1]
    for t in range(4):
        tiles[t] = rows_ref[:, t * 128 : (t + 1) * 128]
    for t in range(4):
        own_ref[t] = flip_blocks(tiles[mine_b ^ t], mine_c)
    tmp[...] = jnp.zeros(tmp.shape, F32)
    for i in range(6):
        tmp[i * 6 : i * 6 + 6, :] = rhs_ref[i]
    nodes = jnp.dot(tmp[...], six_ref[...], precision=HIGHEST, preferred_element_type=F32)
    common[0:40, :] = nodes[:, 0:128]
    common[40:80, :] = jnp.zeros((40, 128), F32)
    common[40:80, 0:64] = nodes[:, 128:192]
    common[40:64, 64:96] = val_ref[...]
    common[64:67, 64:96] = size_ref[...]
    common[72:73, 64:96] = jnp.broadcast_to(link_ref[0], (1, 32))
    common[40:80, 96:128] = vec_ref[0:40, :]
    common[80:120, :] = jnp.zeros((40, 128), F32)
    for t in range(4):
        rows = 40 if t < 3 else 32
        common[80 : 80 + rows, t * 32 : (t + 1) * 32] = vec_ref[40 + t * 40 : 40 + t * 40 + rows, :]
    helm = jnp.dot(
        helm_ref[...].reshape(64, 256), eight_ref[...], precision=HIGHEST, preferred_element_type=F32
    )
    common[120:184, :] = helm[:, 0:128]
    common[184:248, :] = helm[:, 128:256]
    for r in range(16):
        other = ((mine_b ^ (r >> 2)) << 2) | (mine_c ^ (r & 3))
        out_ref[other, 64:312, :] = common[...]
        for half in range(2):
            chosen = BLOCKS[r][half * 4 : half * 4 + 4]
            out_ref[other, half * 32 : half * 32 + 32, :] = place_blocks(
                [(own_ref[t >> 2], t & 3, n) for n, t in enumerate(chosen)]
            )


def joined(column, start, rows, quarter):
    return place_blocks([(column[c][start : start + rows, :], quarter, c) for c in range(4)])


def unpack_body(
    me_ref, all_ref, own_ref,
    dense_ref, rhs_ref, small_ref, box_ref, state_ref, ahead_ref, behind_ref, half_matrix,
):
    mine_b = me_ref[0]
    mine_c = me_ref[1]
    own_at = pl.multiple_of((mine_b * 4 + mine_c) * 32, 32)
    for t in range(4):
        half_matrix[t, pl.ds(own_at, 32), :] = own_ref[t]
    block = lanes((32, 128)) // EA
    for r in range(1, 16):
        other = ((mine_b ^ (r >> 2)) << 2) | (mine_c ^ (r & 3))
        halves = [all_ref[other, half * 32 : half * 32 + 32, :] for half in range(2)]
        at = pl.multiple_of(other * 32, 32)
        for tile in range(4):
            total = jnp.zeros((32, 128), F32)
            for q in range(4):
                t = r ^ (tile * 4 + q)
                if t in BLOCKS[r]:
                    slot = BLOCKS[r].index(t)
                    target = mine_c ^ q
                    moved = pltpu.roll(halves[slot // 4], ((target - slot) & 3) * 32, 1)
                    total = jnp.where(block == target, moved, total)
            half_matrix[mine_b ^ tile, pl.ds(at, 32), :] = total
    row_block = lax.broadcasted_iota(jnp.int32, (128, 128), 0) // 32
    for tile in range(4):
        for row_tile in range(4):
            mirrored = half_matrix[row_tile, tile * 128 : (tile + 1) * 128, :].T
            if tile == row_tile:
                mirrored = jnp.where(row_block == lanes((128, 128)) // EA, 0.0, mirrored)
            rows = slice(row_tile * 128, (row_tile + 1) * 128)
            dense_ref[tile, rows, :] = half_matrix[tile, rows, :] + mirrored
    rhs_ref[...] = jnp.zeros(rhs_ref.shape, F32)
    helm_first, helm_last = [], []
    for b in range(NB):
        column = [all_ref.at[b * 4 + c] for c in range(4)]
        for k in range(6):
            value = joined(column, 64 + 40 * (k // 4), 40, k % 4)
            for i in range(6):
                rhs_ref[b, k * 48 + i * 8 + 1 : k * 48 + i * 8 + 7, :] = value[i * 6 : i * 6 + 6, :]
        small_ref[b, :, :] = joined(column, 104, 40, 2)
        helm_first.append(joined(column, 184, 64, 0))
        helm_last.append(joined(column, 248, 64, 3))
    begin_kernel_part(
        rhs_ref, small_ref, dense_ref, box_ref, state_ref, ahead_ref, behind_ref, (helm_last, helm_first)
    )


def unpack_rest_body(all_ref, helm_ref, vec_ref):
    for b in range(NB):
        column = [all_ref.at[b * 4 + c] for c in range(4)]
        vec_ref[b, 0:40, :] = joined(column, 104, 40, 3)
        for t in range(4):
            rows = 40 if t < 3 else 32
            vec_ref[b, 40 + t * 40 : 40 + t * 40 + rows, :] = joined(column, 144, rows, t)
        for k in range(8):
            helm_ref[b, k * 64 : (k + 1) * 64, :] = joined(column, 184 + 64 * (k // 4), 64, k % 4)


def middle_body(dense_ref, state_ref, left_ref, right_ref, state_out, message_out):
    state, message = sweep_pair(dense_ref, state_ref[...], left_ref[0:16, :], right_ref[0:16, :], 0)
    state_out[...] = state
    message_out[...] = message


def late_body(dense_ref, state_ref, left_ref, right_ref, up_ref, down_ref, state_out, ahead_ref, behind_ref):
    state, message = sweep_pair(dense_ref, state_ref[...], left_ref[...], right_ref[...], 2)
    state_out[...] = state
    ahead_ref[0:16, :] = message
    behind_ref[0:16, :] = message
    ahead_ref[16:80, :] = up_ref[...]
    behind_ref[16:80, :] = down_ref[...]


def join_rows(ref, groups, cross):
    for b in range(NB):
        low = ref[b, pl.ds(0, groups * 8, stride=8), :]
        high = ref[b, pl.ds(7, groups * 8, stride=8), :]
        ref[b, pl.ds(0, groups * 8, stride=8), :] = low + turn(high, 32)
        ref[b, pl.ds(7, groups * 8, stride=8), :] = high + turn(low, -32)
    for b in range(NB - 1):
        for g in range(groups):
            both = ref[b, g * 64 + 56 : g * 64 + 64, :] + ref[b + 1, g * 64 : g * 64 + 8, :]
            ref[b, g * 64 + 56 : g * 64 + 64, :] = both
            ref[b + 1, g * 64 : g * 64 + 8, :] = both


def join_layers(low, high):
    place = lanes(low.shape) % EA
    new_low = low + jnp.where(place > 0, turn(high, 1), 0.0)
    new_high = high + jnp.where(place < EA - 1, turn(low, -1), 0.0)
    return new_low, new_high


def helm_body(helm_ref, left_ref, right_ref, out_ref):
    out_ref[...] = helm_ref[...]
    for b in range(NB):
        low, high = join_layers(helm_ref[b, 0:64, :], helm_ref[b, 448:512, :])
        out_ref[b, 0:64, :] = low + at_first(left_ref[16:80, :], 4 + b)
        out_ref[b, 448:512, :] = high + at_last(right_ref[16:80, :], 4 + b)
    join_rows(out_ref, 8, None)
    for b in range(NB):
        out_ref[b] = 1.0 / out_ref[b]


def schwarz_body(box_ref, vec_ref, small_ref, left_ref, right_ref, out_ref, up_ref, down_ref, one, two, full):
    def element_row(b, carry):
        def row(side, first, second):
            return vec_ref[b, pl.ds(side * 64 + first * 8 + second, 1), :]

        last = pltpu.roll(box_ref[b, 384:448, :], 1, 1)
        first = pltpu.roll(box_ref[b, 64:128, :], 127, 1)
        place = lanes((64, 128)) % EA
        from_left = pltpu.roll(left_ref[16:80, :], 97 + b, 1)
        from_right = pltpu.roll(right_ref[16:80, :], 31 - b, 1)
        one[0] = jnp.where(place == 0, from_left, last).reshape(8, 8, 128)
        one[7] = jnp.where(place == EA - 1, from_right, first).reshape(8, 8, 128)
        one[1:7] = box_ref[b, 64:448, :].reshape(6, 8, 8, 128)
        for m in range(8):
            total = None
            for i in range(8):
                part = one[:, i] * row(0, i, m)[None]
                total = part if total is None else total + part
            two[:, m] = total
        for m in range(8):
            total = None
            for i in range(8):
                part = two[i] * row(2, i, m)[None]
                total = part if total is None else total + part
            one[m] = total
        for k in range(8):
            total = None
            for j in range(8):
                part = one[k, :, j : j + 1, :] * vec_ref[b, 64 + j * 8 : 72 + j * 8, :][None]
                total = part if total is None else total + part
            bottom = small_ref[b, 0:8, :][:, None, :] + small_ref[b, 8:16, :][None, :, :]
            two[k] = total / (bottom + small_ref[b, 16 + k : 17 + k, :][None])
        for k in range(8):
            total = None
            for n in range(8):
                part = two[k, :, n : n + 1, :] * vec_ref[b, pl.ds(64 + n, 8, stride=8), :][None]
                total = part if total is None else total + part
            one[k] = total
        for i in range(8):
            total = None
            for m in range(8):
                part = one[m] * row(2, i, m)[None]
                total = part if total is None else total + part
            two[i] = total
        for i in range(8):
            total = None
            for m in range(8):
                part = two[:, m] * row(0, i, m)[None]
                total = part if total is None else total + part
            one[:, i] = total
        full[b] = one[...].reshape(512, 128)
        return carry

    lax.fori_loop(0, NB, element_row, 0)
    for b in range(NB):
        low = full[b, pl.ds(0, 64, stride=8), :]
        high = full[b, pl.ds(7, 64, stride=8), :]
        full[b, pl.ds(6, 64, stride=8), :] = full[b, pl.ds(6, 64, stride=8), :] + turn(low, -32)
        full[b, pl.ds(1, 64, stride=8), :] = full[b, pl.ds(1, 64, stride=8), :] + turn(high, 32)
        full[b, pl.ds(0, 64, stride=8), :] = jnp.zeros((64, 128), F32)
        full[b, pl.ds(7, 64, stride=8), :] = jnp.zeros((64, 128), F32)
    for b in range(NB - 1):
        for k in range(8):
            full[b, k * 64 + 48 : k * 64 + 56, :] = (
                full[b, k * 64 + 48 : k * 64 + 56, :] + full[b + 1, k * 64 : k * 64 + 8, :]
            )
            full[b + 1, k * 64 + 8 : k * 64 + 16, :] = (
                full[b + 1, k * 64 + 8 : k * 64 + 16, :] + full[b, k * 64 + 56 : k * 64 + 64, :]
            )
    up_ref[...] = pack_last([full[b, 448:512, :] for b in range(NB)])
    down_ref[...] = pack_first([full[b, 0:64, :] for b in range(NB)])
    place = lanes((48, 128)) % EA
    for b in range(NB):
        for k in range(6):
            value = full[b, (k + 1) * 64 + 8 : (k + 1) * 64 + 56, :]
            if k == 0:
                value = value + jnp.where(place > 0, turn(full[b, 456:504, :], 1), 0.0)
            if k == 5:
                value = value + jnp.where(place < EA - 1, turn(full[b, 8:56, :], -1), 0.0)
            out_ref[b, k * 48 : (k + 1) * 48, :] = value


def volume_factors(small_ref, b):
    size = [small_ref[b, 24 + d : 25 + d, :] for d in range(3)]
    volume = size[0] * size[1] * size[2] * 0.125
    return [volume * (2.0 / size[d]) for d in range(3)]


def split_parts(value):
    high = value.astype(BF16)
    return high, (value - high.astype(F32)).astype(BF16)


def gradient_body(
    dense_ref, state_ref, left_ref, right_ref, part_ref, small_ref, table_ref, z_ref, t_ref, ahead_ref, behind_ref
):
    solution = sweep_pair(dense_ref, state_ref[...], left_ref[0:16, :], right_ref[0:16, :], 4)
    inside = lax.broadcasted_iota(jnp.int32, (ROWS_P, 128), 0) % 8
    inside = (inside > 0) & (inside < 7)
    for b in range(NB):
        coarse = jnp.where(inside, solution[b : b + 1, :], 0.0)
        z_ref[b] = part_ref[b] + coarse
        z_ref[b, 0:48, :] = z_ref[b, 0:48, :] + at_first(left_ref[24:72, :], b)
        z_ref[b, 240:288, :] = z_ref[b, 240:288, :] + at_last(right_ref[24:72, :], b)
    parts = [split_parts(z_ref[b]) for b in range(NB)]
    high = jnp.concatenate([part[0] for part in parts], axis=1)
    low = jnp.concatenate([part[1] for part in parts], axis=1)
    both = jnp.concatenate([high, low, high], axis=0)
    factors = [volume_factors(small_ref, b) for b in range(NB)]
    for d in range(3):
        result = jnp.dot(table_ref[d * 512 : (d + 1) * 512, :], both, preferred_element_type=F32)
        for b in range(NB):
            t_ref[b, d * 512 : (d + 1) * 512, :] = result[:, b * 128 : (b + 1) * 128] * factors[b][d]
    join_rows(t_ref, 24, None)
    lows = [t_ref[b, d * 512 : d * 512 + 64, :] for b in range(NB) for d in range(3)]
    highs = [t_ref[b, d * 512 + 448 : d * 512 + 512, :] for b in range(NB) for d in range(3)]
    ahead_ref[...] = pack_last(highs)
    behind_ref[...] = pack_first(lows)
    for b in range(NB):
        for d in range(3):
            low, high = join_layers(lows[b * 3 + d], highs[b * 3 + d])
            t_ref[b, d * 512 : d * 512 + 64, :] = low
            t_ref[b, d * 512 + 448 : d * 512 + 512, :] = high


def divergence_part(t_ref, left_ref, right_ref, inverse_ref, small_ref, table_ref, image_ref, spread):
    for b in range(NB):
        factors = volume_factors(small_ref, b)
        for d in range(3):
            base = d * 512
            for start, rows, extra in (
                (0, 64, at_first(left_ref[...], b * 3 + d)),
                (64, 384, None),
                (448, 64, at_last(right_ref[...], b * 3 + d)),
            ):
                value = t_ref[b, base + start : base + start + rows, :]
                if extra is not None:
                    value = value + extra
                value = value * inverse_ref[b, start : start + rows, :] * factors[d]
                high, low = split_parts(value)
                spread[base + start : base + start + rows, b * 128 : (b + 1) * 128] = high
                spread[1536 + base + start : 1536 + base + start + rows, b * 128 : (b + 1) * 128] = low
    image = jnp.dot(table_ref[:, 0:3072], spread[...], preferred_element_type=F32)
    image = image + jnp.dot(table_ref[:, 3072:4608], spread[0:1536, :], preferred_element_type=F32)
    for b in range(NB):
        image_ref[b] = image[:, b * 128 : (b + 1) * 128]


def first_image_body(
    t_ref, left_ref, right_ref, inverse_ref, small_ref, table_ref, dense_ref,
    image_ref, box_ref, state_ref, ahead_ref, behind_ref, spread,
):
    divergence_part(t_ref, left_ref, right_ref, inverse_ref, small_ref, table_ref, image_ref, spread)
    begin_kernel_part(
        image_ref, small_ref, dense_ref, box_ref, state_ref, ahead_ref, behind_ref, ([], [])
    )


def last_image_body(t_ref, left_ref, right_ref, inverse_ref, small_ref, table_ref, image_ref, spread):
    divergence_part(t_ref, left_ref, right_ref, inverse_ref, small_ref, table_ref, image_ref, spread)


def products_body(r_ref, z_ref, w_ref, q_ref, sums_ref):
    sums_ref[...] = jnp.zeros(sums_ref.shape, F32)
    for n, (one, two) in enumerate(((r_ref, z_ref), (z_ref, w_ref), (w_ref, q_ref), (r_ref, q_ref))):
        total = None
        for b in range(NB):
            part = jnp.sum(one[b] * two[b], axis=0, keepdims=True)
            total = part if total is None else total + part
        sums_ref[n : n + 1, :] = total


def energy_body(t_ref, left_ref, right_ref, inverse_ref, products_ref, sums_ref):
    row = lax.broadcasted_iota(jnp.int32, (64, 128), 0)
    i, j = row // 8, row % 8
    total = None
    for b in range(NB):
        share = jnp.where((j == 0) | (j == 7), 0.5, 1.0)
        shared_b = ((i == 0) & (b > 0)) | ((i == 7) & (b < NB - 1))
        share = jnp.where(shared_b, 0.5 * share, share)
        for k in range(8):
            squares = None
            for d in range(3):
                value = t_ref[b, d * 512 + k * 64 : d * 512 + k * 64 + 64, :]
                if k == 0:
                    value = value + at_first(left_ref[...], b * 3 + d)
                if k == 7:
                    value = value + at_last(right_ref[...], b * 3 + d)
                squares = value * value if squares is None else squares + value * value
            part = squares * inverse_ref[b, k * 64 : k * 64 + 64, :] * share
            if k in (0, 7):
                part = part * 0.5
            total = part if total is None else total + part
    sums_ref[...] = products_ref[...]
    sums_ref[4:5, :] = jnp.sum(total, axis=0, keepdims=True)


def own_body(me_ref, z_ref, w_ref, q_ref, v_ref, table_ref, z_out, w_out, q_out, v_out):
    mine_b = me_ref[0]
    mine_c = me_ref[1]
    for field_ref, out_ref in ((z_ref, z_out), (w_ref, w_out), (q_ref, q_out), (v_ref, v_out)):
        moved = pltpu.roll(field_ref[mine_b], ((4 - mine_c) & 3) * 32, 1)
        nodes = jnp.concatenate([moved[k * 48 : (k + 1) * 48, 0:32] for k in range(6)], axis=1)
        nodes = jnp.dot(nodes, table_ref[...], precision=HIGHEST, preferred_element_type=F32)
        for i in range(6):
            out_ref[i] = nodes[i * 8 + 1 : i * 8 + 7, :]


def last_body(
    sums_ref, z_ref, w_ref, q_ref, v_ref, rhs_ref, pressure_ref, residual_ref, pressure, residual, done
):
    totals = jnp.sum(jnp.sum(sums_ref[...], axis=0), axis=1, keepdims=True)
    rz, zw, wq, rq, qv = [totals[n : n + 1] for n in range(5)]
    step_first = rz / zw
    rz_next = step_first * (step_first * wq - rq)
    share = 1.0 + rz_next / rz
    curvature = share * share * zw - 2.0 * share * step_first * wq + step_first * step_first * qv
    step_next = rz_next / curvature
    z_factor = (step_first + step_next * share)[None]
    q_factor = (step_next * step_first)[None]
    pressure[...] = z_factor * z_ref[...] - q_factor * q_ref[...]
    first = pltpu.make_async_copy(pressure, pressure_ref, done.at[0])
    first.start()
    residual[...] = rhs_ref[...] - z_factor * w_ref[...] + q_factor * v_ref[...]
    second = pltpu.make_async_copy(residual, residual_ref, done.at[1])
    second.start()
    first.wait()
    second.wait()


def call(body, outs, scratch=(), scalars=0):
    vmem = pl.BlockSpec(memory_space=pltpu.VMEM)
    smem = pl.BlockSpec(memory_space=pltpu.SMEM)

    def run(*operands):
        return pl.pallas_call(
            body,
            out_shape=[jax.ShapeDtypeStruct(shape, F32) for shape in outs],
            in_specs=[smem] * scalars + [vmem] * (len(operands) - scalars),
            out_specs=[vmem] * len(outs),
            scratch_shapes=list(scratch),
            compiler_params=pltpu.CompilerParams(vmem_limit_bytes=40 * 1024 * 1024),
        )(*operands)

    return run


def tell_all(block, axes, count):
    return lax.all_to_all(jnp.broadcast_to(block[None], (count,) + block.shape), axes, 0, 0)


def local(divergence, elem_size, helm_diag, fdm_vectors, fdm_values, coarse_rows, axial_link):
    count = lax.axis_size("gx")
    ahead = [(i, (i + 1) % count) for i in range(count)]
    behind = [((i + 1) % count, i) for i in range(count)]

    def exchange(up, down):
        return lax.ppermute(up, "gx", ahead), lax.ppermute(down, "gx", behind)

    forward, backward = gradient_tables()
    six = order_table(6)
    me = jnp.stack([lax.axis_index("gy"), lax.axis_index("col")]).astype(jnp.int32)
    field = (NB, ROWS_P, 128)
    velocity = (NB, ROWS_V, 128)
    state_shape = (16, 128)
    wide = (80, 128)
    plane = (64, 128)

    arguments = (
        divergence,
        helm_diag,
        fdm_vectors.reshape(192, EA),
        fdm_values.reshape(24, EA),
        elem_size,
        coarse_rows,
        axial_link,
        six,
        order_table(8),
    )
    vmem = pl.BlockSpec(memory_space=pltpu.VMEM)
    own_part, own_rows = pl.pallas_call(
        pack_body,
        out_shape=[jax.ShapeDtypeStruct((16, ROWS, 128), F32), jax.ShapeDtypeStruct((4, 32, 128), F32)],
        in_specs=[pl.BlockSpec(memory_space=pltpu.SMEM)] + [pl.BlockSpec(memory_space=pl.ANY)] * 9,
        out_specs=[vmem, vmem],
        scratch_shapes=[pltpu.VMEM(value.shape, F32) for value in arguments]
        + [
            pltpu.VMEM((40, 192), F32),
            pltpu.VMEM((248, 128), F32),
            pltpu.VMEM((4, 32, 128), F32),
            pltpu.SemaphoreType.DMA((9,)),
        ],
        compiler_params=pltpu.CompilerParams(vmem_limit_bytes=60 * 1024 * 1024),
    )(me, *arguments)
    everything = lax.all_to_all(own_part, ("gy", "col"), 0, 0)

    dense, rhs, small, boxes, state, up, down = call(
        unpack_body,
        [(4, 512, 128), field, (NB, 40, 128), velocity, state_shape, wide, wide],
        [pltpu.VMEM((4, 512, 128), F32)],
        scalars=1,
    )(me, everything, own_rows)
    helm, vectors = call(unpack_rest_body, [velocity, (NB, 192, 128)])(everything)

    def precondition(boxes, state, left, right):
        state, message = call(middle_body, [state_shape, state_shape])(dense, state, left, right)
        left_mid, right_mid = exchange(message, message)
        part, up, down = call(
            schwarz_body,
            [field, plane, plane],
            [pltpu.VMEM((8, 8, 8, 128), F32), pltpu.VMEM((8, 8, 8, 128), F32), pltpu.VMEM(velocity, F32)],
        )(boxes, vectors, small, left, right)
        state, up, down = call(late_body, [state_shape, wide, wide])(
            dense, state, left_mid, right_mid, up, down
        )
        left, right = exchange(up, down)
        z, t, up, down = call(gradient_body, [field, (NB, 1536, 128), plane, plane])(
            dense, state, left, right, part, small, forward
        )
        left, right = exchange(up, down)
        return z, t, left, right

    spread = [pltpu.VMEM((3072, 512), BF16)]
    left, right = exchange(up, down)
    left, right, helm, vectors = lax.optimization_barrier((left, right, helm, vectors))
    (inverse,) = call(helm_body, [velocity])(helm, left, right)
    z, t, left, right = precondition(boxes, state, left, right)
    w, boxes, state, up, down = call(
        first_image_body, [field, velocity, state_shape, wide, wide], spread
    )(t, left, right, inverse, small, backward, dense)
    left, right = exchange(up, down)
    q, t, left, right = precondition(boxes, state, left, right)
    (products,) = call(products_body, [(8, 128)])(rhs, z, w, q)
    (sums,) = call(energy_body, [(8, 128)])(t, left, right, inverse, products)
    sums = tell_all(sums, "gx", count)
    (v,) = call(last_image_body, [field], spread)(t, left, right, inverse, small, backward)
    own = call(own_body, [(6, 6, 192)] * 4, scalars=1)(me, z, w, q, v, six.T.copy())
    return tuple(
        pl.pallas_call(
            last_body,
            out_shape=[jax.ShapeDtypeStruct((6, 6, 192), F32)] * 2,
            in_specs=[pl.BlockSpec(memory_space=pltpu.VMEM)] * 6,
            out_specs=[pl.BlockSpec(memory_space=pl.ANY)] * 2,
            scratch_shapes=[pltpu.VMEM((6, 6, 192), F32)] * 2 + [pltpu.SemaphoreType.DMA((2,))],
            compiler_params=pltpu.CompilerParams(vmem_limit_bytes=40 * 1024 * 1024),
        )(sums, *own, divergence)
    )


def solution(mesh):
    in_specs = (
        P("gy", "col", "gx"),
        P(None, ("gx", "gy", "col")),
        P("gy", "col", "gx"),
        P(None, None, None, ("gx", "gy", "col")),
        P(None, None, ("gx", "gy", "col")),
        P(("gx", "gy", "col"), None),
        P("gx", "gy", "col"),
    )
    out_specs = (P("gy", "col", "gx"), P("gy", "col", "gx"))
    return jax.shard_map(local, mesh=mesh, in_specs=in_specs, out_specs=out_specs, check_vma=False)
```

```python
import jax
import jax.numpy as jnp
import ml_dtypes
import numpy as np
from jax import lax
from jax.experimental import pallas as pl
from jax.experimental.pallas import tpu as pltpu
from jax.sharding import PartitionSpec as P

EA = 32
CHEB = 6
NB = 4

LOBATTO_NODES = [
    -1.0,
    -0.8717401485096066,
    -0.5917001814331423,
    -0.2092992179024789,
    0.2092992179024789,
    0.5917001814331423,
    0.8717401485096066,
    1.0,
]
GAUSS_NODES = [
    -0.932469514203152,
    -0.6612093864662645,
    -0.2386191860831909,
    0.2386191860831909,
    0.6612093864662645,
    0.932469514203152,
]
GAUSS_WEIGHTS = [
    0.1713244923791704,
    0.3607615730481386,
    0.467913934572691,
    0.467913934572691,
    0.3607615730481386,
    0.1713244923791704,
]
SPECTRUM_LOW = 8.0
SPECTRUM_HIGH = 90.0
HIGHEST = lax.Precision.HIGHEST
F32 = jnp.float32
BF16 = jnp.bfloat16

ROWS_P = 288
ROWS_V = 512
ROWS = 312


def basis_tables():
    lobatto = np.array(LOBATTO_NODES)
    points = np.array(GAUSS_NODES)
    interp = np.ones((6, 8))
    slopes = np.zeros((6, 8))
    for p in range(6):
        for m in range(8):
            product = 1.0
            for q in range(8):
                if q != m:
                    product = product * (points[p] - lobatto[q]) / (lobatto[m] - lobatto[q])
            interp[p, m] = product
            running = 0.0
            for q in range(8):
                if q != m:
                    factor = 1.0 / (lobatto[m] - lobatto[q])
                    for k in range(8):
                        if k != m and k != q:
                            factor = factor * (points[p] - lobatto[k]) / (lobatto[m] - lobatto[k])
                    running = running + factor
            slopes[p, m] = running
    return interp, slopes


def gradient_tables():
    interp, slopes = basis_tables()
    weight = np.array(GAUSS_WEIGHTS)
    tables = []
    for comp in range(3):
        sides = [(slopes if side == comp else interp) * weight[:, None] for side in range(3)]
        full = np.zeros((8, 8, 8, 6, 6, 8))
        full[..., 1:7] = np.einsum("iu,jv,kw->wuvkij", sides[0], sides[1], sides[2])
        tables.append(full.reshape(ROWS_V, ROWS_P))
    table = np.concatenate(tables, axis=0).astype(np.float32)
    high = table.astype(ml_dtypes.bfloat16)
    low = (table - high.astype(np.float32)).astype(ml_dtypes.bfloat16)
    forward = np.concatenate([high, high, low], axis=1)
    backward = np.concatenate([high.T, high.T, low.T], axis=1)
    return forward, backward


def order_table(nodes):
    table = np.zeros((nodes * EA, nodes * EA), np.float32)
    for k in range(nodes):
        for a in range(EA):
            table[a * nodes + k, k * EA + a] = 1.0
    return table


def sweep_factors():
    center = (SPECTRUM_HIGH + SPECTRUM_LOW) / 2.0
    spread = (SPECTRUM_HIGH - SPECTRUM_LOW) / 2.0
    ratio_cs = center / spread
    rho_now = 1.0 / ratio_cs
    keep, add = [], []
    for _ in range(CHEB):
        rho_next = 1.0 / (2.0 * ratio_cs - rho_now)
        keep.append(rho_next * rho_now)
        add.append(2.0 * rho_next / spread)
        rho_now = rho_next
    return center, keep, add


CENTER, KEEP, ADD = sweep_factors()


def parity(value):
    return bin(value).count("1") % 2


def block_choice():
    def extend(taken):
        t = len(taken) + 1
        if t == 16:
            return taken
        for mask in range(1, 16):
            if mask not in taken and parity(mask & t):
                done = extend(taken + [mask])
                if done:
                    return done
        return None

    masks = extend([])
    return [[0] + [t for t in range(1, 16) if not parity(masks[t - 1] & r)] for r in range(16)]


BLOCKS = block_choice()


def lanes(shape):
    return lax.broadcasted_iota(jnp.int32, shape, len(shape) - 1)


def turn(value, shift):
    shift = shift % 128
    return value if shift == 0 else pltpu.roll(value, shift, value.ndim - 1)


def at_first(value, slot=0):
    moved = turn(value, 97 + slot)
    return jnp.where(lanes(moved.shape) % EA == 0, moved, 0.0)


def at_last(value, slot=0):
    moved = turn(value, 31 - slot)
    return jnp.where(lanes(moved.shape) % EA == EA - 1, moved, 0.0)


def pack_last(blocks):
    packed = None
    for slot, block in enumerate(blocks):
        part = turn(jnp.where(lanes(block.shape) % EA == EA - 1, block, 0.0), -slot)
        packed = part if packed is None else packed + part
    return packed


def pack_first(blocks):
    packed = None
    for slot, block in enumerate(blocks):
        part = turn(jnp.where(lanes(block.shape) % EA == 0, block, 0.0), slot)
        packed = part if packed is None else packed + part
    return packed


def times(dense_ref, vector):
    columns = jnp.concatenate([vector, jnp.zeros_like(vector)], axis=0).T
    total = None
    for b in range(NB):
        part = dense_ref[:, b * 128 : (b + 1) * 128, :] * columns[:, b : b + 1][None]
        total = part if total is None else total + part
    return jnp.sum(total, axis=1)


def sweep_begin(dense_ref, source, link):
    update = source * (1.0 / CENTER)
    remainder = source - times(dense_ref, update)
    free = KEEP[0] * update + ADD[0] * remainder
    state = jnp.concatenate([update, remainder, update, link], axis=0)
    return state, jnp.concatenate([update, free, link, link], axis=0)


def sweep_pair(dense_ref, state, from_left, from_right, sweep_at):
    update, remainder, solution, link = [state[4 * n : 4 * n + 4] for n in range(4)]
    left = at_first(from_left)
    right = at_last(from_right)
    place = lanes(update.shape) % EA
    link_left = left[8:12]
    link_right = jnp.where(place == EA - 1, link, 0.0)
    remainder = remainder + link_left * left[0:4] + link_right * right[0:4]
    left_next = left[4:8] + ADD[sweep_at] * link_left * update
    right_next = right[4:8] + ADD[sweep_at] * link_right * update
    update = KEEP[sweep_at] * update + ADD[sweep_at] * remainder
    solution = solution + update
    remainder = remainder - times(dense_ref, update)
    remainder = remainder + link_left * left_next + link_right * right_next
    update = KEEP[sweep_at + 1] * update + ADD[sweep_at + 1] * remainder
    solution = solution + update
    if sweep_at + 2 == CHEB:
        return solution
    remainder = remainder - times(dense_ref, update)
    free = KEEP[sweep_at + 2] * update + ADD[sweep_at + 2] * remainder
    state = jnp.concatenate([update, remainder, solution, link], axis=0)
    return state, jnp.concatenate([update, free, link, link], axis=0)


def fill_boxes(field_ref, box_ref):
    box_ref[...] = jnp.zeros(box_ref.shape, F32)
    for b in range(NB):
        for k in range(6):
            box_ref[b, (k + 1) * 64 + 8 : (k + 1) * 64 + 56, :] = field_ref[b, k * 48 : (k + 1) * 48, :]
        before = box_ref[b, pl.ds(6, 64, stride=8), :]
        after = box_ref[b, pl.ds(1, 64, stride=8), :]
        box_ref[b, pl.ds(0, 64, stride=8), :] = turn(before, 32)
        box_ref[b, pl.ds(7, 64, stride=8), :] = turn(after, -32)
    for b in range(NB):
        for k in range(1, 7):
            if b > 0:
                box_ref[b, k * 64 : k * 64 + 8, :] = box_ref[b - 1, k * 64 + 48 : k * 64 + 56, :]
            if b < NB - 1:
                box_ref[b, k * 64 + 56 : k * 64 + 64, :] = box_ref[b + 1, k * 64 + 8 : k * 64 + 16, :]


def begin_kernel_part(field_ref, small_ref, dense_ref, box_ref, state_ref, ahead_ref, behind_ref, extra):
    fill_boxes(field_ref, box_ref)
    source = jnp.concatenate(
        [jnp.sum(field_ref[b], axis=0, keepdims=True) for b in range(NB)], axis=0
    )
    link = jnp.concatenate([small_ref[b, 32:33, :] for b in range(NB)], axis=0)
    state, message = sweep_begin(dense_ref, source, link)
    state_ref[...] = state
    ahead_ref[0:16, :] = message
    behind_ref[0:16, :] = message
    ahead_ref[16:80, :] = pack_last([box_ref[b, 384:448, :] for b in range(NB)] + extra[0])
    behind_ref[16:80, :] = pack_first([box_ref[b, 64:128, :] for b in range(NB)] + extra[1])


def flip_blocks(value, mine_c):
    block = lanes(value.shape) // EA
    swapped = jnp.where(block % 2 == 0, turn(value, -32), turn(value, 32))
    value = jnp.where((mine_c & 1) == 1, swapped, value)
    return jnp.where((mine_c & 2) == 2, turn(value, 64), value)


def place_blocks(pieces):
    total = None
    for value, source, target in pieces:
        part = jnp.where(lanes(value.shape) // EA == target, turn(value, (target - source) * 32), 0.0)
        total = part if total is None else total + part
    return total


def pack_body(*refs):
    me_ref, sources, (out_ref, tiles), held, (tmp, common, chosen_blocks, own_ref, ready) = (
        refs[0], refs[1:10], refs[10:12], refs[12:21], refs[21:]
    )
    copies = [pltpu.make_async_copy(sources[n], held[n], ready.at[n]) for n in range(9)]
    for copy in copies:
        copy.start()
    for copy in copies:
        copy.wait()
    rhs_ref, helm_ref, vec_ref, val_ref, size_ref, rows_ref, link_ref, six_ref, eight_ref = held
    mine_b = me_ref[0]
    mine_c = me_ref[1]
    for t in range(4):
        tiles[t] = rows_ref[:, t * 128 : (t + 1) * 128]
    for t in range(4):
        own_ref[t] = flip_blocks(tiles[mine_b ^ t], mine_c)
    tmp[...] = jnp.zeros(tmp.shape, F32)
    for i in range(6):
        tmp[i * 6 : i * 6 + 6, :] = rhs_ref[i]
    nodes = jnp.dot(tmp[...], six_ref[...], precision=HIGHEST, preferred_element_type=F32)
    common[0:40, :] = nodes[:, 0:128]
    common[40:80, :] = jnp.zeros((40, 128), F32)
    common[40:80, 0:64] = nodes[:, 128:192]
    common[40:64, 64:96] = val_ref[...]
    common[64:67, 64:96] = size_ref[...]
    common[72:73, 64:96] = jnp.broadcast_to(link_ref[0], (1, 32))
    common[40:80, 96:128] = vec_ref[0:40, :]
    common[80:120, :] = jnp.zeros((40, 128), F32)
    for t in range(4):
        rows = 40 if t < 3 else 32
        common[80 : 80 + rows, t * 32 : (t + 1) * 32] = vec_ref[40 + t * 40 : 40 + t * 40 + rows, :]
    helm = jnp.dot(
        helm_ref[...].reshape(64, 256), eight_ref[...], precision=HIGHEST, preferred_element_type=F32
    )
    common[120:184, :] = helm[:, 0:128]
    common[184:248, :] = helm[:, 128:256]
    sends = [pltpu.make_async_copy(common, out_ref.at[n, 64:312], ready.at[9 + n]) for n in range(16)]
    sends += [
        pltpu.make_async_copy(chosen_blocks.at[n], out_ref.at[n, 0:64], ready.at[25 + n]) for n in range(16)
    ]
    for send in sends[:16]:
        send.start()
    for r in range(16):
        other = ((mine_b ^ (r >> 2)) << 2) | (mine_c ^ (r & 3))
        for half in range(2):
            chosen = BLOCKS[r][half * 4 : half * 4 + 4]
            chosen_blocks[other, half * 32 : half * 32 + 32, :] = place_blocks(
                [(own_ref[t >> 2], t & 3, n) for n, t in enumerate(chosen)]
            )
    for send in sends[16:]:
        send.start()
    for send in sends:
        send.wait()


def joined(column, start, rows, quarter):
    return place_blocks([(column[c][start : start + rows, :], quarter, c) for c in range(4)])


def unpack_body(
    me_ref, all_ref, own_ref,
    dense_ref, rhs_ref, small_ref, box_ref, state_ref, ahead_ref, behind_ref, half_matrix,
):
    mine_b = me_ref[0]
    mine_c = me_ref[1]
    own_at = pl.multiple_of((mine_b * 4 + mine_c) * 32, 32)
    for t in range(4):
        half_matrix[t, pl.ds(own_at, 32), :] = own_ref[t]
    block = lanes((32, 128)) // EA
    for r in range(1, 16):
        other = ((mine_b ^ (r >> 2)) << 2) | (mine_c ^ (r & 3))
        halves = [all_ref[other, half * 32 : half * 32 + 32, :] for half in range(2)]
        at = pl.multiple_of(other * 32, 32)
        for tile in range(4):
            total = jnp.zeros((32, 128), F32)
            for q in range(4):
                t = r ^ (tile * 4 + q)
                if t in BLOCKS[r]:
                    slot = BLOCKS[r].index(t)
                    target = mine_c ^ q
                    moved = pltpu.roll(halves[slot // 4], ((target - slot) & 3) * 32, 1)
                    total = jnp.where(block == target, moved, total)
            half_matrix[mine_b ^ tile, pl.ds(at, 32), :] = total
    row_block = lax.broadcasted_iota(jnp.int32, (128, 128), 0) // 32
    for tile in range(4):
        for row_tile in range(4):
            mirrored = half_matrix[row_tile, tile * 128 : (tile + 1) * 128, :].T
            if tile == row_tile:
                mirrored = jnp.where(row_block == lanes((128, 128)) // EA, 0.0, mirrored)
            rows = slice(row_tile * 128, (row_tile + 1) * 128)
            dense_ref[tile, rows, :] = half_matrix[tile, rows, :] + mirrored
    rhs_ref[...] = jnp.zeros(rhs_ref.shape, F32)
    helm_first, helm_last = [], []
    for b in range(NB):
        column = [all_ref.at[b * 4 + c] for c in range(4)]
        for k in range(6):
            value = joined(column, 64 + 40 * (k // 4), 40, k % 4)
            for i in range(6):
                rhs_ref[b, k * 48 + i * 8 + 1 : k * 48 + i * 8 + 7, :] = value[i * 6 : i * 6 + 6, :]
        small_ref[b, :, :] = joined(column, 104, 40, 2)
        helm_first.append(joined(column, 184, 64, 0))
        helm_last.append(joined(column, 248, 64, 3))
    begin_kernel_part(
        rhs_ref, small_ref, dense_ref, box_ref, state_ref, ahead_ref, behind_ref, (helm_last, helm_first)
    )


def unpack_rest_body(all_ref, helm_ref, vec_ref):
    for b in range(NB):
        column = [all_ref.at[b * 4 + c] for c in range(4)]
        vec_ref[b, 0:40, :] = joined(column, 104, 40, 3)
        for t in range(4):
            rows = 40 if t < 3 else 32
            vec_ref[b, 40 + t * 40 : 40 + t * 40 + rows, :] = joined(column, 144, rows, t)
        for k in range(8):
            helm_ref[b, k * 64 : (k + 1) * 64, :] = joined(column, 184 + 64 * (k // 4), 64, k % 4)


def middle_body(dense_ref, state_ref, left_ref, right_ref, state_out, message_out):
    state, message = sweep_pair(dense_ref, state_ref[...], left_ref[0:16, :], right_ref[0:16, :], 0)
    state_out[...] = state
    message_out[...] = message


def late_body(dense_ref, state_ref, left_ref, right_ref, up_ref, down_ref, state_out, ahead_ref, behind_ref):
    state, message = sweep_pair(dense_ref, state_ref[...], left_ref[...], right_ref[...], 2)
    state_out[...] = state
    ahead_ref[0:16, :] = message
    behind_ref[0:16, :] = message
    ahead_ref[16:80, :] = up_ref[...]
    behind_ref[16:80, :] = down_ref[...]


def join_rows(ref, groups, cross):
    for b in range(NB):
        low = ref[b, pl.ds(0, groups * 8, stride=8), :]
        high = ref[b, pl.ds(7, groups * 8, stride=8), :]
        ref[b, pl.ds(0, groups * 8, stride=8), :] = low + turn(high, 32)
        ref[b, pl.ds(7, groups * 8, stride=8), :] = high + turn(low, -32)
    for b in range(NB - 1):
        for g in range(groups):
            both = ref[b, g * 64 + 56 : g * 64 + 64, :] + ref[b + 1, g * 64 : g * 64 + 8, :]
            ref[b, g * 64 + 56 : g * 64 + 64, :] = both
            ref[b + 1, g * 64 : g * 64 + 8, :] = both


def join_layers(low, high):
    place = lanes(low.shape) % EA
    new_low = low + jnp.where(place > 0, turn(high, 1), 0.0)
    new_high = high + jnp.where(place < EA - 1, turn(low, -1), 0.0)
    return new_low, new_high


def helm_body(helm_ref, left_ref, right_ref, out_ref):
    out_ref[...] = helm_ref[...]
    for b in range(NB):
        low, high = join_layers(helm_ref[b, 0:64, :], helm_ref[b, 448:512, :])
        out_ref[b, 0:64, :] = low + at_first(left_ref[16:80, :], 4 + b)
        out_ref[b, 448:512, :] = high + at_last(right_ref[16:80, :], 4 + b)
    join_rows(out_ref, 8, None)
    for b in range(NB):
        out_ref[b] = 1.0 / out_ref[b]


def across_planes(planes, vec_ref, b, mid):
    for m in range(8):
        total = None
        for i in range(8):
            part = planes[:, i] * vec_ref[b, pl.ds(i * 8 + m, 1), :][None]
            total = part if total is None else total + part
        mid[:, m] = total
    results = []
    for k in range(planes.shape[0]):
        total = None
        for j in range(8):
            part = mid[k, :, j : j + 1, :] * vec_ref[b, 64 + j * 8 : 72 + j * 8, :][None]
            total = part if total is None else total + part
        results.append(total)
    return results


def schwarz_front_body(box_ref, vec_ref, out_ref, mid):
    def element_row(b, carry):
        results = across_planes(box_ref[b, 64:448, :].reshape(6, 8, 8, 128), vec_ref, b, mid)
        for k in range(6):
            out_ref[b, k * 64 : (k + 1) * 64, :] = results[k].reshape(64, 128)
        return carry

    lax.fori_loop(0, NB, element_row, 0)


def schwarz_body(
    box_ref, front_ref, vec_ref, small_ref, left_ref, right_ref, out_ref, up_ref, down_ref,
    one, two, full, ends, mid,
):
    def element_row(b, carry):
        def row(side, first, second):
            return vec_ref[b, pl.ds(side * 64 + first * 8 + second, 1), :]

        last = pltpu.roll(box_ref[b, 384:448, :], 1, 1)
        first = pltpu.roll(box_ref[b, 64:128, :], 127, 1)
        place = lanes((64, 128)) % EA
        from_left = pltpu.roll(left_ref[16:80, :], 97 + b, 1)
        from_right = pltpu.roll(right_ref[16:80, :], 31 - b, 1)
        ends[0] = jnp.where(place == 0, from_left, last).reshape(8, 8, 128)
        ends[1] = jnp.where(place == EA - 1, from_right, first).reshape(8, 8, 128)
        two[0], two[7] = across_planes(ends, vec_ref, b, mid)
        two[1:7] = front_ref[b].reshape(6, 8, 8, 128)
        for m in range(8):
            total = None
            for i in range(8):
                part = two[i] * row(2, i, m)[None]
                total = part if total is None else total + part
            bottom = small_ref[b, 0:8, :][:, None, :] + small_ref[b, 8:16, :][None, :, :]
            one[m] = total / (bottom + small_ref[b, pl.ds(16 + m, 1), :][None])
        for k in range(8):
            total = None
            for n in range(8):
                part = one[k, :, n : n + 1, :] * vec_ref[b, pl.ds(64 + n, 8, stride=8), :][None]
                total = part if total is None else total + part
            two[k] = total
        for i in range(8):
            total = None
            for m in range(8):
                part = two[m] * row(2, i, m)[None]
                total = part if total is None else total + part
            one[i] = total
        for i in range(8):
            total = None
            for m in range(8):
                part = one[:, m] * row(0, i, m)[None]
                total = part if total is None else total + part
            two[:, i] = total
        full[b] = two[...].reshape(512, 128)
        return carry

    lax.fori_loop(0, NB, element_row, 0)
    for b in range(NB):
        low = full[b, pl.ds(0, 64, stride=8), :]
        high = full[b, pl.ds(7, 64, stride=8), :]
        full[b, pl.ds(6, 64, stride=8), :] = full[b, pl.ds(6, 64, stride=8), :] + turn(low, -32)
        full[b, pl.ds(1, 64, stride=8), :] = full[b, pl.ds(1, 64, stride=8), :] + turn(high, 32)
        full[b, pl.ds(0, 64, stride=8), :] = jnp.zeros((64, 128), F32)
        full[b, pl.ds(7, 64, stride=8), :] = jnp.zeros((64, 128), F32)
    for b in range(NB - 1):
        for k in range(8):
            full[b, k * 64 + 48 : k * 64 + 56, :] = (
                full[b, k * 64 + 48 : k * 64 + 56, :] + full[b + 1, k * 64 : k * 64 + 8, :]
            )
            full[b + 1, k * 64 + 8 : k * 64 + 16, :] = (
                full[b + 1, k * 64 + 8 : k * 64 + 16, :] + full[b, k * 64 + 56 : k * 64 + 64, :]
            )
    up_ref[...] = pack_last([full[b, 448:512, :] for b in range(NB)])
    down_ref[...] = pack_first([full[b, 0:64, :] for b in range(NB)])
    place = lanes((48, 128)) % EA
    for b in range(NB):
        for k in range(6):
            value = full[b, (k + 1) * 64 + 8 : (k + 1) * 64 + 56, :]
            if k == 0:
                value = value + jnp.where(place > 0, turn(full[b, 456:504, :], 1), 0.0)
            if k == 5:
                value = value + jnp.where(place < EA - 1, turn(full[b, 8:56, :], -1), 0.0)
            out_ref[b, k * 48 : (k + 1) * 48, :] = value


def volume_factors(small_ref, b):
    size = [small_ref[b, 24 + d : 25 + d, :] for d in range(3)]
    volume = size[0] * size[1] * size[2] * 0.125
    return [volume * (2.0 / size[d]) for d in range(3)]


def split_parts(value):
    high = value.astype(BF16)
    return high, (value - high.astype(F32)).astype(BF16)


def gradient_body(
    dense_ref, state_ref, left_ref, right_ref, part_ref, small_ref, table_ref, z_ref, t_ref, ahead_ref, behind_ref
):
    solution = sweep_pair(dense_ref, state_ref[...], left_ref[0:16, :], right_ref[0:16, :], 4)
    inside = lax.broadcasted_iota(jnp.int32, (ROWS_P, 128), 0) % 8
    inside = (inside > 0) & (inside < 7)
    for b in range(NB):
        coarse = jnp.where(inside, solution[b : b + 1, :], 0.0)
        z_ref[b] = part_ref[b] + coarse
        z_ref[b, 0:48, :] = z_ref[b, 0:48, :] + at_first(left_ref[24:72, :], b)
        z_ref[b, 240:288, :] = z_ref[b, 240:288, :] + at_last(right_ref[24:72, :], b)
    parts = [split_parts(z_ref[b]) for b in range(NB)]
    high = jnp.concatenate([part[0] for part in parts], axis=1)
    low = jnp.concatenate([part[1] for part in parts], axis=1)
    both = jnp.concatenate([high, low, high], axis=0)
    factors = [volume_factors(small_ref, b) for b in range(NB)]
    for d in range(3):
        result = jnp.dot(table_ref[d * 512 : (d + 1) * 512, :], both, preferred_element_type=F32)
        for b in range(NB):
            t_ref[b, d * 512 : (d + 1) * 512, :] = result[:, b * 128 : (b + 1) * 128] * factors[b][d]
    join_rows(t_ref, 24, None)
    lows = [t_ref[b, d * 512 : d * 512 + 64, :] for b in range(NB) for d in range(3)]
    highs = [t_ref[b, d * 512 + 448 : d * 512 + 512, :] for b in range(NB) for d in range(3)]
    ahead_ref[...] = pack_last(highs)
    behind_ref[...] = pack_first(lows)
    for b in range(NB):
        for d in range(3):
            low, high = join_layers(lows[b * 3 + d], highs[b * 3 + d])
            t_ref[b, d * 512 : d * 512 + 64, :] = low
            t_ref[b, d * 512 + 448 : d * 512 + 512, :] = high


def divergence_part(t_ref, left_ref, right_ref, inverse_ref, small_ref, table_ref, image_ref, spread):
    for b in range(NB):
        factors = volume_factors(small_ref, b)
        for d in range(3):
            base = d * 512
            for start, rows, extra in (
                (0, 64, at_first(left_ref[...], b * 3 + d)),
                (64, 384, None),
                (448, 64, at_last(right_ref[...], b * 3 + d)),
            ):
                value = t_ref[b, base + start : base + start + rows, :]
                if extra is not None:
                    value = value + extra
                value = value * inverse_ref[b, start : start + rows, :] * factors[d]
                high, low = split_parts(value)
                spread[base + start : base + start + rows, b * 128 : (b + 1) * 128] = high
                spread[1536 + base + start : 1536 + base + start + rows, b * 128 : (b + 1) * 128] = low
    image = jnp.dot(table_ref[:, 0:3072], spread[...], preferred_element_type=F32)
    image = image + jnp.dot(table_ref[:, 3072:4608], spread[0:1536, :], preferred_element_type=F32)
    for b in range(NB):
        image_ref[b] = image[:, b * 128 : (b + 1) * 128]


def first_image_body(
    t_ref, left_ref, right_ref, inverse_ref, small_ref, table_ref, dense_ref,
    image_ref, box_ref, state_ref, ahead_ref, behind_ref, spread,
):
    divergence_part(t_ref, left_ref, right_ref, inverse_ref, small_ref, table_ref, image_ref, spread)
    begin_kernel_part(
        image_ref, small_ref, dense_ref, box_ref, state_ref, ahead_ref, behind_ref, ([], [])
    )


def last_image_body(t_ref, left_ref, right_ref, inverse_ref, small_ref, table_ref, image_ref, spread):
    divergence_part(t_ref, left_ref, right_ref, inverse_ref, small_ref, table_ref, image_ref, spread)


def products_body(r_ref, z_ref, w_ref, q_ref, sums_ref):
    sums_ref[...] = jnp.zeros(sums_ref.shape, F32)
    for n, (one, two) in enumerate(((r_ref, z_ref), (z_ref, w_ref), (w_ref, q_ref), (r_ref, q_ref))):
        total = None
        for b in range(NB):
            part = jnp.sum(one[b] * two[b], axis=0, keepdims=True)
            total = part if total is None else total + part
        sums_ref[n : n + 1, :] = total


def energy_body(t_ref, left_ref, right_ref, inverse_ref, products_ref, sums_ref):
    row = lax.broadcasted_iota(jnp.int32, (64, 128), 0)
    i, j = row // 8, row % 8
    total = None
    for b in range(NB):
        share = jnp.where((j == 0) | (j == 7), 0.5, 1.0)
        shared_b = ((i == 0) & (b > 0)) | ((i == 7) & (b < NB - 1))
        share = jnp.where(shared_b, 0.5 * share, share)
        for k in range(8):
            squares = None
            for d in range(3):
                value = t_ref[b, d * 512 + k * 64 : d * 512 + k * 64 + 64, :]
                if k == 0:
                    value = value + at_first(left_ref[...], b * 3 + d)
                if k == 7:
                    value = value + at_last(right_ref[...], b * 3 + d)
                squares = value * value if squares is None else squares + value * value
            part = squares * inverse_ref[b, k * 64 : k * 64 + 64, :] * share
            if k in (0, 7):
                part = part * 0.5
            total = part if total is None else total + part
    row = lax.broadcasted_iota(jnp.int32, (8, 128), 0)
    sums = jnp.where(row == 4, jnp.sum(total, axis=0, keepdims=True), products_ref[...])
    for n in range(sums_ref.shape[0]):
        sums_ref[n] = sums


def own_body(me_ref, z_ref, w_ref, q_ref, v_ref, table_ref, z_out, w_out, q_out, v_out):
    mine_b = me_ref[0]
    mine_c = me_ref[1]
    for field_ref, out_ref in ((z_ref, z_out), (w_ref, w_out), (q_ref, q_out), (v_ref, v_out)):
        moved = pltpu.roll(field_ref[mine_b], ((4 - mine_c) & 3) * 32, 1)
        nodes = jnp.concatenate([moved[k * 48 : (k + 1) * 48, 0:32] for k in range(6)], axis=1)
        nodes = jnp.dot(nodes, table_ref[...], precision=HIGHEST, preferred_element_type=F32)
        for i in range(6):
            out_ref[i] = nodes[i * 8 + 1 : i * 8 + 7, :]


def last_body(
    sums_ref, z_ref, w_ref, q_ref, v_ref, rhs_ref, pressure_ref, residual_ref, pressure, residual, done
):
    totals = jnp.sum(jnp.sum(sums_ref[...], axis=0), axis=1, keepdims=True)
    rz, zw, wq, rq, qv = [totals[n : n + 1] for n in range(5)]
    step_first = rz / zw
    rz_next = step_first * (step_first * wq - rq)
    share = 1.0 + rz_next / rz
    curvature = share * share * zw - 2.0 * share * step_first * wq + step_first * step_first * qv
    step_next = rz_next / curvature
    z_factor = (step_first + step_next * share)[None]
    q_factor = (step_next * step_first)[None]
    pressure[...] = z_factor * z_ref[...] - q_factor * q_ref[...]
    first = pltpu.make_async_copy(pressure, pressure_ref, done.at[0])
    first.start()
    residual[...] = rhs_ref[...] - z_factor * w_ref[...] + q_factor * v_ref[...]
    second = pltpu.make_async_copy(residual, residual_ref, done.at[1])
    second.start()
    first.wait()
    second.wait()


def call(body, outs, scratch=(), scalars=0):
    vmem = pl.BlockSpec(memory_space=pltpu.VMEM)
    smem = pl.BlockSpec(memory_space=pltpu.SMEM)

    def run(*operands):
        return pl.pallas_call(
            body,
            out_shape=[jax.ShapeDtypeStruct(shape, F32) for shape in outs],
            in_specs=[smem] * scalars + [vmem] * (len(operands) - scalars),
            out_specs=[vmem] * len(outs),
            scratch_shapes=list(scratch),
            compiler_params=pltpu.CompilerParams(vmem_limit_bytes=40 * 1024 * 1024),
        )(*operands)

    return run


def local(divergence, elem_size, helm_diag, fdm_vectors, fdm_values, coarse_rows, axial_link):
    count = lax.axis_size("gx")
    ahead = [(i, (i + 1) % count) for i in range(count)]
    behind = [((i + 1) % count, i) for i in range(count)]

    def exchange(up, down):
        return lax.ppermute(up, "gx", ahead), lax.ppermute(down, "gx", behind)

    forward, backward = gradient_tables()
    six = order_table(6)
    me = jnp.stack([lax.axis_index("gy"), lax.axis_index("col")]).astype(jnp.int32)
    field = (NB, ROWS_P, 128)
    velocity = (NB, ROWS_V, 128)
    state_shape = (16, 128)
    wide = (80, 128)
    plane = (64, 128)

    arguments = (
        divergence,
        helm_diag,
        fdm_vectors.reshape(192, EA),
        fdm_values.reshape(24, EA),
        elem_size,
        coarse_rows,
        axial_link,
        six,
        order_table(8),
    )
    vmem = pl.BlockSpec(memory_space=pltpu.VMEM)
    own_part, own_rows = pl.pallas_call(
        pack_body,
        out_shape=[jax.ShapeDtypeStruct((16, ROWS, 128), F32), jax.ShapeDtypeStruct((4, 32, 128), F32)],
        in_specs=[pl.BlockSpec(memory_space=pltpu.SMEM)] + [pl.BlockSpec(memory_space=pl.ANY)] * 9,
        out_specs=[pl.BlockSpec(memory_space=pl.ANY), vmem],
        scratch_shapes=[pltpu.VMEM(value.shape, F32) for value in arguments]
        + [
            pltpu.VMEM((40, 192), F32),
            pltpu.VMEM((248, 128), F32),
            pltpu.VMEM((16, 64, 128), F32),
            pltpu.VMEM((4, 32, 128), F32),
            pltpu.SemaphoreType.DMA((41,)),
        ],
        compiler_params=pltpu.CompilerParams(vmem_limit_bytes=60 * 1024 * 1024),
    )(me, *arguments)
    everything = lax.all_to_all(own_part, ("gy", "col"), 0, 0)

    dense, rhs, small, boxes, state, up, down = call(
        unpack_body,
        [(4, 512, 128), field, (NB, 40, 128), velocity, state_shape, wide, wide],
        [pltpu.VMEM((4, 512, 128), F32)],
        scalars=1,
    )(me, everything, own_rows)
    helm, vectors = call(unpack_rest_body, [velocity, (NB, 192, 128)])(everything)

    def schwarz_front(boxes):
        return call(schwarz_front_body, [(NB, 384, 128)], [pltpu.VMEM((6, 8, 8, 128), F32)])(boxes, vectors)[0]

    def precondition(boxes, state, left, right, front):
        state, message = call(middle_body, [state_shape, state_shape])(dense, state, left, right)
        left_mid, right_mid = exchange(message, message)
        part, up, down = call(
            schwarz_body,
            [field, plane, plane],
            [
                pltpu.VMEM((8, 8, 8, 128), F32),
                pltpu.VMEM((8, 8, 8, 128), F32),
                pltpu.VMEM(velocity, F32),
                pltpu.VMEM((2, 8, 8, 128), F32),
                pltpu.VMEM((2, 8, 8, 128), F32),
            ],
        )(boxes, front, vectors, small, left, right)
        state, up, down = call(late_body, [state_shape, wide, wide])(
            dense, state, left_mid, right_mid, up, down
        )
        left, right = exchange(up, down)
        z, t, up, down = call(gradient_body, [field, (NB, 1536, 128), plane, plane])(
            dense, state, left, right, part, small, forward
        )
        left, right = exchange(up, down)
        return z, t, left, right

    spread = [pltpu.VMEM((3072, 512), BF16)]
    left, right = exchange(up, down)
    front = schwarz_front(boxes)
    left, right, helm, front = lax.optimization_barrier((left, right, helm, front))
    (inverse,) = call(helm_body, [velocity])(helm, left, right)
    z, t, left, right = precondition(boxes, state, left, right, front)
    w, boxes, state, up, down = call(
        first_image_body, [field, velocity, state_shape, wide, wide], spread
    )(t, left, right, inverse, small, backward, dense)
    left, right = exchange(up, down)
    front = schwarz_front(boxes)
    left, right, front = lax.optimization_barrier((left, right, front))
    q, t, left, right = precondition(boxes, state, left, right, front)
    (products,) = call(products_body, [(8, 128)])(rhs, z, w, q)
    (sums,) = call(energy_body, [(count, 8, 128)])(t, left, right, inverse, products)
    sums = lax.all_to_all(sums, "gx", 0, 0)
    (v,) = call(last_image_body, [field], spread)(t, left, right, inverse, small, backward)
    own = call(own_body, [(6, 6, 192)] * 4, scalars=1)(me, z, w, q, v, six.T.copy())
    return tuple(
        pl.pallas_call(
            last_body,
            out_shape=[jax.ShapeDtypeStruct((6, 6, 192), F32)] * 2,
            in_specs=[pl.BlockSpec(memory_space=pltpu.VMEM)] * 6,
            out_specs=[pl.BlockSpec(memory_space=pl.ANY)] * 2,
            scratch_shapes=[pltpu.VMEM((6, 6, 192), F32)] * 2 + [pltpu.SemaphoreType.DMA((2,))],
            compiler_params=pltpu.CompilerParams(vmem_limit_bytes=40 * 1024 * 1024),
        )(sums, *own, divergence)
    )


def solution(mesh):
    in_specs = (
        P("gy", "col", "gx"),
        P(None, ("gx", "gy", "col")),
        P("gy", "col", "gx"),
        P(None, None, None, ("gx", "gy", "col")),
        P(None, None, ("gx", "gy", "col")),
        P(("gx", "gy", "col"), None),
        P("gx", "gy", "col"),
    )
    out_specs = (P("gy", "col", "gx"), P("gy", "col", "gx"))
    return jax.shard_map(local, mesh=mesh, in_specs=in_specs, out_specs=out_specs, check_vma=False)
```

```python
import jax
import jax.numpy as jnp
import ml_dtypes
import numpy as np
from jax import lax
from jax.experimental import pallas as pl
from jax.experimental.pallas import tpu as pltpu
from jax.sharding import PartitionSpec as P

EA = 32
CHEB = 6
NB = 4

LOBATTO_NODES = [
    -1.0,
    -0.8717401485096066,
    -0.5917001814331423,
    -0.2092992179024789,
    0.2092992179024789,
    0.5917001814331423,
    0.8717401485096066,
    1.0,
]
GAUSS_NODES = [
    -0.932469514203152,
    -0.6612093864662645,
    -0.2386191860831909,
    0.2386191860831909,
    0.6612093864662645,
    0.932469514203152,
]
GAUSS_WEIGHTS = [
    0.1713244923791704,
    0.3607615730481386,
    0.467913934572691,
    0.467913934572691,
    0.3607615730481386,
    0.1713244923791704,
]
SPECTRUM_LOW = 8.0
SPECTRUM_HIGH = 90.0
HIGHEST = lax.Precision.HIGHEST
F32 = jnp.float32
BF16 = jnp.bfloat16

ROWS_P = 288
ROWS_V = 512
ROWS = 312


def basis_tables():
    lobatto = np.array(LOBATTO_NODES)
    points = np.array(GAUSS_NODES)
    interp = np.ones((6, 8))
    slopes = np.zeros((6, 8))
    for p in range(6):
        for m in range(8):
            product = 1.0
            for q in range(8):
                if q != m:
                    product = product * (points[p] - lobatto[q]) / (lobatto[m] - lobatto[q])
            interp[p, m] = product
            running = 0.0
            for q in range(8):
                if q != m:
                    factor = 1.0 / (lobatto[m] - lobatto[q])
                    for k in range(8):
                        if k != m and k != q:
                            factor = factor * (points[p] - lobatto[k]) / (lobatto[m] - lobatto[k])
                    running = running + factor
            slopes[p, m] = running
    return interp, slopes


def gradient_tables():
    interp, slopes = basis_tables()
    weight = np.array(GAUSS_WEIGHTS)
    tables = []
    for comp in range(3):
        sides = [(slopes if side == comp else interp) * weight[:, None] for side in range(3)]
        full = np.zeros((8, 8, 8, 6, 6, 8))
        full[..., 1:7] = np.einsum("iu,jv,kw->wuvkij", sides[0], sides[1], sides[2])
        tables.append(full.reshape(ROWS_V, ROWS_P))
    table = np.concatenate(tables, axis=0).astype(np.float32)
    high = table.astype(ml_dtypes.bfloat16)
    low = (table - high.astype(np.float32)).astype(ml_dtypes.bfloat16)
    forward = np.concatenate([high, high, low], axis=1)
    backward = np.concatenate([high.T, high.T, low.T], axis=1)
    return forward, backward


def order_table(nodes):
    table = np.zeros((nodes * EA, nodes * EA), np.float32)
    for k in range(nodes):
        for a in range(EA):
            table[a * nodes + k, k * EA + a] = 1.0
    return table


def sweep_factors():
    center = (SPECTRUM_HIGH + SPECTRUM_LOW) / 2.0
    spread = (SPECTRUM_HIGH - SPECTRUM_LOW) / 2.0
    ratio_cs = center / spread
    rho_now = 1.0 / ratio_cs
    keep, add = [], []
    for _ in range(CHEB):
        rho_next = 1.0 / (2.0 * ratio_cs - rho_now)
        keep.append(rho_next * rho_now)
        add.append(2.0 * rho_next / spread)
        rho_now = rho_next
    return center, keep, add


CENTER, KEEP, ADD = sweep_factors()


def parity(value):
    return bin(value).count("1") % 2


def block_choice():
    def extend(taken):
        t = len(taken) + 1
        if t == 16:
            return taken
        for mask in range(1, 16):
            if mask not in taken and parity(mask & t):
                done = extend(taken + [mask])
                if done:
                    return done
        return None

    masks = extend([])
    return [[0] + [t for t in range(1, 16) if not parity(masks[t - 1] & r)] for r in range(16)]


BLOCKS = block_choice()


def lanes(shape):
    return lax.broadcasted_iota(jnp.int32, shape, len(shape) - 1)


def turn(value, shift):
    shift = shift % 128
    return value if shift == 0 else pltpu.roll(value, shift, value.ndim - 1)


def at_first(value, slot=0):
    moved = turn(value, 97 + slot)
    return jnp.where(lanes(moved.shape) % EA == 0, moved, 0.0)


def at_last(value, slot=0):
    moved = turn(value, 31 - slot)
    return jnp.where(lanes(moved.shape) % EA == EA - 1, moved, 0.0)


def pack_last(blocks):
    packed = None
    for slot, block in enumerate(blocks):
        part = turn(jnp.where(lanes(block.shape) % EA == EA - 1, block, 0.0), -slot)
        packed = part if packed is None else packed + part
    return packed


def pack_first(blocks):
    packed = None
    for slot, block in enumerate(blocks):
        part = turn(jnp.where(lanes(block.shape) % EA == 0, block, 0.0), slot)
        packed = part if packed is None else packed + part
    return packed


def times(dense_ref, vector):
    columns = jnp.concatenate([vector, jnp.zeros_like(vector)], axis=0).T
    total = None
    for b in range(NB):
        part = dense_ref[:, b * 128 : (b + 1) * 128, :] * columns[:, b : b + 1][None]
        total = part if total is None else total + part
    return jnp.sum(total, axis=1)


def sweep_begin(dense_ref, source, link):
    update = source * (1.0 / CENTER)
    remainder = source - times(dense_ref, update)
    free = KEEP[0] * update + ADD[0] * remainder
    state = jnp.concatenate([update, remainder, update, link], axis=0)
    return state, jnp.concatenate([update, free, link, link], axis=0)


def sweep_pair(dense_ref, state, from_left, from_right, sweep_at):
    update, remainder, solution, link = [state[4 * n : 4 * n + 4] for n in range(4)]
    left = at_first(from_left)
    right = at_last(from_right)
    place = lanes(update.shape) % EA
    link_left = left[8:12]
    link_right = jnp.where(place == EA - 1, link, 0.0)
    remainder = remainder + link_left * left[0:4] + link_right * right[0:4]
    left_next = left[4:8] + ADD[sweep_at] * link_left * update
    right_next = right[4:8] + ADD[sweep_at] * link_right * update
    update = KEEP[sweep_at] * update + ADD[sweep_at] * remainder
    solution = solution + update
    remainder = remainder - times(dense_ref, update)
    remainder = remainder + link_left * left_next + link_right * right_next
    update = KEEP[sweep_at + 1] * update + ADD[sweep_at + 1] * remainder
    solution = solution + update
    if sweep_at + 2 == CHEB:
        return solution
    remainder = remainder - times(dense_ref, update)
    free = KEEP[sweep_at + 2] * update + ADD[sweep_at + 2] * remainder
    state = jnp.concatenate([update, remainder, solution, link], axis=0)
    return state, jnp.concatenate([update, free, link, link], axis=0)


def fill_boxes(field_ref, box_ref):
    box_ref[...] = jnp.zeros(box_ref.shape, F32)
    for b in range(NB):
        for k in range(6):
            box_ref[b, (k + 1) * 64 + 8 : (k + 1) * 64 + 56, :] = field_ref[b, k * 48 : (k + 1) * 48, :]
        before = box_ref[b, pl.ds(6, 64, stride=8), :]
        after = box_ref[b, pl.ds(1, 64, stride=8), :]
        box_ref[b, pl.ds(0, 64, stride=8), :] = turn(before, 32)
        box_ref[b, pl.ds(7, 64, stride=8), :] = turn(after, -32)
    for b in range(NB):
        for k in range(1, 7):
            if b > 0:
                box_ref[b, k * 64 : k * 64 + 8, :] = box_ref[b - 1, k * 64 + 48 : k * 64 + 56, :]
            if b < NB - 1:
                box_ref[b, k * 64 + 56 : k * 64 + 64, :] = box_ref[b + 1, k * 64 + 8 : k * 64 + 16, :]


def begin_kernel_part(field_ref, small_ref, dense_ref, box_ref, state_ref, ahead_ref, behind_ref, extra):
    fill_boxes(field_ref, box_ref)
    source = jnp.concatenate(
        [jnp.sum(field_ref[b], axis=0, keepdims=True) for b in range(NB)], axis=0
    )
    link = jnp.concatenate([small_ref[b, 32:33, :] for b in range(NB)], axis=0)
    state, message = sweep_begin(dense_ref, source, link)
    state_ref[...] = state
    ahead_ref[0:16, :] = message
    behind_ref[0:16, :] = message
    ahead_ref[16:80, :] = pack_last([box_ref[b, 384:448, :] for b in range(NB)] + extra[0])
    behind_ref[16:80, :] = pack_first([box_ref[b, 64:128, :] for b in range(NB)] + extra[1])


def flip_blocks(value, mine_c):
    block = lanes(value.shape) // EA
    swapped = jnp.where(block % 2 == 0, turn(value, -32), turn(value, 32))
    value = jnp.where((mine_c & 1) == 1, swapped, value)
    return jnp.where((mine_c & 2) == 2, turn(value, 64), value)


def place_blocks(pieces):
    total = None
    for value, source, target in pieces:
        part = jnp.where(lanes(value.shape) // EA == target, turn(value, (target - source) * 32), 0.0)
        total = part if total is None else total + part
    return total


def pack_body(*refs):
    (b_ref, c_ref), sources, (out_ref, tiles), held, (tmp, common, own_ref, ready) = (
        refs[:2], refs[2:11], refs[11:13], refs[13:22], refs[22:]
    )
    copies = [pltpu.make_async_copy(sources[n], held[n], ready.at[n]) for n in range(9)]
    for copy in copies:
        copy.start()
    for copy in copies:
        copy.wait()
    rhs_ref, helm_ref, vec_ref, val_ref, size_ref, rows_ref, link_ref, six_ref, eight_ref = held
    mine_b = b_ref[0]
    mine_c = c_ref[0]
    for t in range(4):
        tiles[t] = rows_ref[:, t * 128 : (t + 1) * 128]
    for t in range(4):
        own_ref[t] = flip_blocks(tiles[mine_b ^ t], mine_c)
    tmp[...] = jnp.zeros(tmp.shape, F32)
    for i in range(6):
        tmp[i * 6 : i * 6 + 6, :] = rhs_ref[i]
    nodes = jnp.dot(tmp[...], six_ref[...], precision=HIGHEST, preferred_element_type=F32)
    common[0:40, :] = nodes[:, 0:128]
    common[40:80, :] = jnp.zeros((40, 128), F32)
    common[40:80, 0:64] = nodes[:, 128:192]
    common[40:64, 64:96] = val_ref[...]
    common[64:67, 64:96] = size_ref[...]
    common[72:73, 64:96] = jnp.broadcast_to(link_ref[0], (1, 32))
    common[40:80, 96:128] = vec_ref[0:40, :]
    common[80:120, :] = jnp.zeros((40, 128), F32)
    for t in range(4):
        rows = 40 if t < 3 else 32
        common[80 : 80 + rows, t * 32 : (t + 1) * 32] = vec_ref[40 + t * 40 : 40 + t * 40 + rows, :]
    helm = jnp.dot(
        helm_ref[...].reshape(64, 256), eight_ref[...], precision=HIGHEST, preferred_element_type=F32
    )
    common[120:184, :] = helm[:, 0:128]
    common[184:248, :] = helm[:, 128:256]
    for r in range(16):
        other = ((mine_b ^ (r >> 2)) << 2) | (mine_c ^ (r & 3))
        out_ref[other, 64:312, :] = common[...]
        for half in range(2):
            chosen = BLOCKS[r][half * 4 : half * 4 + 4]
            out_ref[other, half * 32 : half * 32 + 32, :] = place_blocks(
                [(own_ref[t >> 2], t & 3, n) for n, t in enumerate(chosen)]
            )


def joined(column, start, rows, quarter):
    return place_blocks([(column[c][start : start + rows, :], quarter, c) for c in range(4)])


def unpack_body(
    b_ref, c_ref, all_ref, own_ref,
    dense_ref, rhs_ref, small_ref, box_ref, state_ref, ahead_ref, behind_ref, half_matrix,
):
    mine_b = b_ref[0]
    mine_c = c_ref[0]
    own_at = pl.multiple_of((mine_b * 4 + mine_c) * 32, 32)
    for t in range(4):
        half_matrix[t, pl.ds(own_at, 32), :] = own_ref[t]
    block = lanes((32, 128)) // EA
    for r in range(1, 16):
        other = ((mine_b ^ (r >> 2)) << 2) | (mine_c ^ (r & 3))
        halves = [all_ref[other, half * 32 : half * 32 + 32, :] for half in range(2)]
        at = pl.multiple_of(other * 32, 32)
        for tile in range(4):
            total = jnp.zeros((32, 128), F32)
            for q in range(4):
                t = r ^ (tile * 4 + q)
                if t in BLOCKS[r]:
                    slot = BLOCKS[r].index(t)
                    target = mine_c ^ q
                    moved = pltpu.roll(halves[slot // 4], ((target - slot) & 3) * 32, 1)
                    total = jnp.where(block == target, moved, total)
            half_matrix[mine_b ^ tile, pl.ds(at, 32), :] = total
    row_block = lax.broadcasted_iota(jnp.int32, (128, 128), 0) // 32
    for tile in range(4):
        for row_tile in range(4):
            mirrored = half_matrix[row_tile, tile * 128 : (tile + 1) * 128, :].T
            if tile == row_tile:
                mirrored = jnp.where(row_block == lanes((128, 128)) // EA, 0.0, mirrored)
            rows = slice(row_tile * 128, (row_tile + 1) * 128)
            dense_ref[tile, rows, :] = half_matrix[tile, rows, :] + mirrored
    rhs_ref[...] = jnp.zeros(rhs_ref.shape, F32)
    helm_first, helm_last = [], []
    for b in range(NB):
        column = [all_ref.at[b * 4 + c] for c in range(4)]
        for k in range(6):
            value = joined(column, 64 + 40 * (k // 4), 40, k % 4)
            for i in range(6):
                rhs_ref[b, k * 48 + i * 8 + 1 : k * 48 + i * 8 + 7, :] = value[i * 6 : i * 6 + 6, :]
        small_ref[b, :, :] = joined(column, 104, 40, 2)
        helm_first.append(joined(column, 184, 64, 0))
        helm_last.append(joined(column, 248, 64, 3))
    begin_kernel_part(
        rhs_ref, small_ref, dense_ref, box_ref, state_ref, ahead_ref, behind_ref, (helm_last, helm_first)
    )


def unpack_rest_body(all_ref, helm_ref, vec_ref):
    for b in range(NB):
        column = [all_ref.at[b * 4 + c] for c in range(4)]
        vec_ref[b, 0:40, :] = joined(column, 104, 40, 3)
        for t in range(4):
            rows = 40 if t < 3 else 32
            vec_ref[b, 40 + t * 40 : 40 + t * 40 + rows, :] = joined(column, 144, rows, t)
        for k in range(8):
            helm_ref[b, k * 64 : (k + 1) * 64, :] = joined(column, 184 + 64 * (k // 4), 64, k % 4)


def middle_body(dense_ref, state_ref, left_ref, right_ref, state_out, message_out):
    state, message = sweep_pair(dense_ref, state_ref[...], left_ref[0:16, :], right_ref[0:16, :], 0)
    state_out[...] = state
    message_out[...] = message


def late_body(dense_ref, state_ref, left_ref, right_ref, up_ref, down_ref, state_out, ahead_ref, behind_ref):
    state, message = sweep_pair(dense_ref, state_ref[...], left_ref[...], right_ref[...], 2)
    state_out[...] = state
    ahead_ref[0:16, :] = message
    behind_ref[0:16, :] = message
    ahead_ref[16:80, :] = up_ref[...]
    behind_ref[16:80, :] = down_ref[...]


def join_rows(ref, groups, cross):
    for b in range(NB):
        low = ref[b, pl.ds(0, groups * 8, stride=8), :]
        high = ref[b, pl.ds(7, groups * 8, stride=8), :]
        ref[b, pl.ds(0, groups * 8, stride=8), :] = low + turn(high, 32)
        ref[b, pl.ds(7, groups * 8, stride=8), :] = high + turn(low, -32)
    for b in range(NB - 1):
        for g in range(groups):
            both = ref[b, g * 64 + 56 : g * 64 + 64, :] + ref[b + 1, g * 64 : g * 64 + 8, :]
            ref[b, g * 64 + 56 : g * 64 + 64, :] = both
            ref[b + 1, g * 64 : g * 64 + 8, :] = both


def join_layers(low, high):
    place = lanes(low.shape) % EA
    new_low = low + jnp.where(place > 0, turn(high, 1), 0.0)
    new_high = high + jnp.where(place < EA - 1, turn(low, -1), 0.0)
    return new_low, new_high


def helm_body(helm_ref, left_ref, right_ref, out_ref):
    out_ref[...] = helm_ref[...]
    for b in range(NB):
        low, high = join_layers(helm_ref[b, 0:64, :], helm_ref[b, 448:512, :])
        out_ref[b, 0:64, :] = low + at_first(left_ref[16:80, :], 4 + b)
        out_ref[b, 448:512, :] = high + at_last(right_ref[16:80, :], 4 + b)
    join_rows(out_ref, 8, None)
    for b in range(NB):
        out_ref[b] = 1.0 / out_ref[b]


def across_planes(planes, vec_ref, b, mid):
    for m in range(8):
        total = None
        for i in range(8):
            part = planes[:, i] * vec_ref[b, pl.ds(i * 8 + m, 1), :][None]
            total = part if total is None else total + part
        mid[:, m] = total
    results = []
    for k in range(planes.shape[0]):
        total = None
        for j in range(8):
            part = mid[k, :, j : j + 1, :] * vec_ref[b, 64 + j * 8 : 72 + j * 8, :][None]
            total = part if total is None else total + part
        results.append(total)
    return results


def schwarz_front_body(box_ref, vec_ref, out_ref, mid):
    def element_row(b, carry):
        results = across_planes(box_ref[b, 64:448, :].reshape(6, 8, 8, 128), vec_ref, b, mid)
        for k in range(6):
            out_ref[b, k * 64 : (k + 1) * 64, :] = results[k].reshape(64, 128)
        return carry

    lax.fori_loop(0, NB, element_row, 0)


def schwarz_body(
    box_ref, front_ref, vec_ref, small_ref, left_ref, right_ref, out_ref, up_ref, down_ref,
    one, two, full, ends, mid,
):
    def element_row(b, carry):
        def row(side, first, second):
            return vec_ref[b, pl.ds(side * 64 + first * 8 + second, 1), :]

        last = pltpu.roll(box_ref[b, 384:448, :], 1, 1)
        first = pltpu.roll(box_ref[b, 64:128, :], 127, 1)
        place = lanes((64, 128)) % EA
        from_left = pltpu.roll(left_ref[16:80, :], 97 + b, 1)
        from_right = pltpu.roll(right_ref[16:80, :], 31 - b, 1)
        ends[0] = jnp.where(place == 0, from_left, last).reshape(8, 8, 128)
        ends[1] = jnp.where(place == EA - 1, from_right, first).reshape(8, 8, 128)
        two[0], two[7] = across_planes(ends, vec_ref, b, mid)
        two[1:7] = front_ref[b].reshape(6, 8, 8, 128)
        for m in range(8):
            total = None
            for i in range(8):
                part = two[i] * row(2, i, m)[None]
                total = part if total is None else total + part
            bottom = small_ref[b, 0:8, :][:, None, :] + small_ref[b, 8:16, :][None, :, :]
            one[m] = total / (bottom + small_ref[b, pl.ds(16 + m, 1), :][None])
        for k in range(8):
            total = None
            for n in range(8):
                part = one[k, :, n : n + 1, :] * vec_ref[b, pl.ds(64 + n, 8, stride=8), :][None]
                total = part if total is None else total + part
            two[k] = total
        for i in range(8):
            total = None
            for m in range(8):
                part = two[m] * row(2, i, m)[None]
                total = part if total is None else total + part
            one[i] = total
        for i in range(8):
            total = None
            for m in range(8):
                part = one[:, m] * row(0, i, m)[None]
                total = part if total is None else total + part
            two[:, i] = total
        full[b] = two[...].reshape(512, 128)
        return carry

    lax.fori_loop(0, NB, element_row, 0)
    for b in range(NB):
        low = full[b, pl.ds(0, 64, stride=8), :]
        high = full[b, pl.ds(7, 64, stride=8), :]
        full[b, pl.ds(6, 64, stride=8), :] = full[b, pl.ds(6, 64, stride=8), :] + turn(low, -32)
        full[b, pl.ds(1, 64, stride=8), :] = full[b, pl.ds(1, 64, stride=8), :] + turn(high, 32)
        full[b, pl.ds(0, 64, stride=8), :] = jnp.zeros((64, 128), F32)
        full[b, pl.ds(7, 64, stride=8), :] = jnp.zeros((64, 128), F32)
    for b in range(NB - 1):
        for k in range(8):
            full[b, k * 64 + 48 : k * 64 + 56, :] = (
                full[b, k * 64 + 48 : k * 64 + 56, :] + full[b + 1, k * 64 : k * 64 + 8, :]
            )
            full[b + 1, k * 64 + 8 : k * 64 + 16, :] = (
                full[b + 1, k * 64 + 8 : k * 64 + 16, :] + full[b, k * 64 + 56 : k * 64 + 64, :]
            )
    up_ref[...] = pack_last([full[b, 448:512, :] for b in range(NB)])
    down_ref[...] = pack_first([full[b, 0:64, :] for b in range(NB)])
    place = lanes((48, 128)) % EA
    for b in range(NB):
        for k in range(6):
            value = full[b, (k + 1) * 64 + 8 : (k + 1) * 64 + 56, :]
            if k == 0:
                value = value + jnp.where(place > 0, turn(full[b, 456:504, :], 1), 0.0)
            if k == 5:
                value = value + jnp.where(place < EA - 1, turn(full[b, 8:56, :], -1), 0.0)
            out_ref[b, k * 48 : (k + 1) * 48, :] = value


def volume_factors(small_ref, b):
    size = [small_ref[b, 24 + d : 25 + d, :] for d in range(3)]
    volume = size[0] * size[1] * size[2] * 0.125
    return [volume * (2.0 / size[d]) for d in range(3)]


def split_parts(value):
    high = value.astype(BF16)
    return high, (value - high.astype(F32)).astype(BF16)


def gradient_body(
    dense_ref, state_ref, left_ref, right_ref, part_ref, small_ref, table_ref, z_ref, t_ref, ahead_ref, behind_ref
):
    solution = sweep_pair(dense_ref, state_ref[...], left_ref[0:16, :], right_ref[0:16, :], 4)
    inside = lax.broadcasted_iota(jnp.int32, (ROWS_P, 128), 0) % 8
    inside = (inside > 0) & (inside < 7)
    for b in range(NB):
        coarse = jnp.where(inside, solution[b : b + 1, :], 0.0)
        z_ref[b] = part_ref[b] + coarse
        z_ref[b, 0:48, :] = z_ref[b, 0:48, :] + at_first(left_ref[24:72, :], b)
        z_ref[b, 240:288, :] = z_ref[b, 240:288, :] + at_last(right_ref[24:72, :], b)
    parts = [split_parts(z_ref[b]) for b in range(NB)]
    high = jnp.concatenate([part[0] for part in parts], axis=1)
    low = jnp.concatenate([part[1] for part in parts], axis=1)
    both = jnp.concatenate([high, low, high], axis=0)
    factors = [volume_factors(small_ref, b) for b in range(NB)]
    for d in range(3):
        result = jnp.dot(table_ref[d * 512 : (d + 1) * 512, :], both, preferred_element_type=F32)
        for b in range(NB):
            t_ref[b, d * 512 : (d + 1) * 512, :] = result[:, b * 128 : (b + 1) * 128] * factors[b][d]
    join_rows(t_ref, 24, None)
    lows = [t_ref[b, d * 512 : d * 512 + 64, :] for b in range(NB) for d in range(3)]
    highs = [t_ref[b, d * 512 + 448 : d * 512 + 512, :] for b in range(NB) for d in range(3)]
    ahead_ref[...] = pack_last(highs)
    behind_ref[...] = pack_first(lows)
    for b in range(NB):
        for d in range(3):
            low, high = join_layers(lows[b * 3 + d], highs[b * 3 + d])
            t_ref[b, d * 512 : d * 512 + 64, :] = low
            t_ref[b, d * 512 + 448 : d * 512 + 512, :] = high


def divergence_part(t_ref, left_ref, right_ref, inverse_ref, small_ref, table_ref, image_ref, spread):
    for b in range(NB):
        factors = volume_factors(small_ref, b)
        for d in range(3):
            base = d * 512
            for start, rows, extra in (
                (0, 64, at_first(left_ref[...], b * 3 + d)),
                (64, 384, None),
                (448, 64, at_last(right_ref[...], b * 3 + d)),
            ):
                value = t_ref[b, base + start : base + start + rows, :]
                if extra is not None:
                    value = value + extra
                value = value * inverse_ref[b, start : start + rows, :] * factors[d]
                high, low = split_parts(value)
                spread[base + start : base + start + rows, b * 128 : (b + 1) * 128] = high
                spread[1536 + base + start : 1536 + base + start + rows, b * 128 : (b + 1) * 128] = low
    image = jnp.dot(table_ref[:, 0:3072], spread[...], preferred_element_type=F32)
    image = image + jnp.dot(table_ref[:, 3072:4608], spread[0:1536, :], preferred_element_type=F32)
    for b in range(NB):
        image_ref[b] = image[:, b * 128 : (b + 1) * 128]


def first_image_body(
    t_ref, left_ref, right_ref, inverse_ref, small_ref, table_ref, dense_ref,
    image_ref, box_ref, state_ref, ahead_ref, behind_ref, spread,
):
    divergence_part(t_ref, left_ref, right_ref, inverse_ref, small_ref, table_ref, image_ref, spread)
    begin_kernel_part(
        image_ref, small_ref, dense_ref, box_ref, state_ref, ahead_ref, behind_ref, ([], [])
    )


def last_image_body(t_ref, left_ref, right_ref, inverse_ref, small_ref, table_ref, image_ref, spread):
    divergence_part(t_ref, left_ref, right_ref, inverse_ref, small_ref, table_ref, image_ref, spread)


def products_body(r_ref, z_ref, w_ref, q_ref, sums_ref):
    sums_ref[...] = jnp.zeros(sums_ref.shape, F32)
    for n, (one, two) in enumerate(((r_ref, z_ref), (z_ref, w_ref), (w_ref, q_ref), (r_ref, q_ref))):
        total = None
        for b in range(NB):
            part = jnp.sum(one[b] * two[b], axis=0, keepdims=True)
            total = part if total is None else total + part
        sums_ref[n : n + 1, :] = total


def energy_body(t_ref, left_ref, right_ref, inverse_ref, products_ref, sums_ref):
    row = lax.broadcasted_iota(jnp.int32, (64, 128), 0)
    i, j = row // 8, row % 8
    total = None
    for b in range(NB):
        share = jnp.where((j == 0) | (j == 7), 0.5, 1.0)
        shared_b = ((i == 0) & (b > 0)) | ((i == 7) & (b < NB - 1))
        share = jnp.where(shared_b, 0.5 * share, share)
        for k in range(8):
            squares = None
            for d in range(3):
                value = t_ref[b, d * 512 + k * 64 : d * 512 + k * 64 + 64, :]
                if k == 0:
                    value = value + at_first(left_ref[...], b * 3 + d)
                if k == 7:
                    value = value + at_last(right_ref[...], b * 3 + d)
                squares = value * value if squares is None else squares + value * value
            part = squares * inverse_ref[b, k * 64 : k * 64 + 64, :] * share
            if k in (0, 7):
                part = part * 0.5
            total = part if total is None else total + part
    sums_ref[...] = products_ref[...]
    sums_ref[4:5, :] = jnp.sum(total, axis=0, keepdims=True)


def own_body(b_ref, c_ref, z_ref, w_ref, q_ref, v_ref, table_ref, z_out, w_out, q_out, v_out):
    mine_b = b_ref[0]
    mine_c = c_ref[0]
    for field_ref, out_ref in ((z_ref, z_out), (w_ref, w_out), (q_ref, q_out), (v_ref, v_out)):
        moved = pltpu.roll(field_ref[mine_b], ((4 - mine_c) & 3) * 32, 1)
        nodes = jnp.concatenate([moved[k * 48 : (k + 1) * 48, 0:32] for k in range(6)], axis=1)
        nodes = jnp.dot(nodes, table_ref[...], precision=HIGHEST, preferred_element_type=F32)
        for i in range(6):
            out_ref[i] = nodes[i * 8 + 1 : i * 8 + 7, :]


def last_body(
    sums_ref, z_ref, w_ref, q_ref, v_ref, rhs_ref, pressure_ref, residual_ref, pressure, residual, done
):
    totals = jnp.sum(jnp.sum(sums_ref[...], axis=0), axis=1, keepdims=True)
    rz, zw, wq, rq, qv = [totals[n : n + 1] for n in range(5)]
    step_first = rz / zw
    rz_next = step_first * (step_first * wq - rq)
    share = 1.0 + rz_next / rz
    curvature = share * share * zw - 2.0 * share * step_first * wq + step_first * step_first * qv
    step_next = rz_next / curvature
    z_factor = (step_first + step_next * share)[None]
    q_factor = (step_next * step_first)[None]
    pressure[...] = z_factor * z_ref[...] - q_factor * q_ref[...]
    first = pltpu.make_async_copy(pressure, pressure_ref, done.at[0])
    first.start()
    residual[...] = rhs_ref[...] - z_factor * w_ref[...] + q_factor * v_ref[...]
    second = pltpu.make_async_copy(residual, residual_ref, done.at[1])
    second.start()
    first.wait()
    second.wait()


def call(body, outs, scratch=(), scalars=0):
    vmem = pl.BlockSpec(memory_space=pltpu.VMEM)
    smem = pl.BlockSpec(memory_space=pltpu.SMEM)

    def run(*operands):
        return pl.pallas_call(
            body,
            out_shape=[jax.ShapeDtypeStruct(shape, F32) for shape in outs],
            in_specs=[smem] * scalars + [vmem] * (len(operands) - scalars),
            out_specs=[vmem] * len(outs),
            scratch_shapes=list(scratch),
            compiler_params=pltpu.CompilerParams(vmem_limit_bytes=40 * 1024 * 1024),
        )(*operands)

    return run


def local(divergence, elem_size, helm_diag, fdm_vectors, fdm_values, coarse_rows, axial_link):
    count = lax.axis_size("gx")
    ahead = [(i, (i + 1) % count) for i in range(count)]
    behind = [((i + 1) % count, i) for i in range(count)]

    def exchange(up, down):
        return lax.ppermute(up, "gx", ahead), lax.ppermute(down, "gx", behind)

    forward, backward = gradient_tables()
    six = order_table(6)
    me = [lax.axis_index(axis).astype(jnp.int32).reshape(1) for axis in ("gy", "col")]
    field = (NB, ROWS_P, 128)
    velocity = (NB, ROWS_V, 128)
    state_shape = (16, 128)
    wide = (80, 128)
    plane = (64, 128)

    arguments = (
        divergence,
        helm_diag,
        fdm_vectors.reshape(192, EA),
        fdm_values.reshape(24, EA),
        elem_size,
        coarse_rows,
        axial_link,
        six,
        order_table(8),
    )
    vmem = pl.BlockSpec(memory_space=pltpu.VMEM)
    own_part, own_rows = pl.pallas_call(
        pack_body,
        out_shape=[jax.ShapeDtypeStruct((16, ROWS, 128), F32), jax.ShapeDtypeStruct((4, 32, 128), F32)],
        in_specs=[pl.BlockSpec(memory_space=pltpu.SMEM)] * 2 + [pl.BlockSpec(memory_space=pl.ANY)] * 9,
        out_specs=[vmem, vmem],
        scratch_shapes=[pltpu.VMEM(value.shape, F32) for value in arguments]
        + [
            pltpu.VMEM((40, 192), F32),
            pltpu.VMEM((248, 128), F32),
            pltpu.VMEM((4, 32, 128), F32),
            pltpu.SemaphoreType.DMA((9,)),
        ],
        compiler_params=pltpu.CompilerParams(vmem_limit_bytes=60 * 1024 * 1024),
    )(*me, *arguments)
    everything = lax.all_to_all(own_part, ("gy", "col"), 0, 0)

    dense, rhs, small, boxes, state, up, down = call(
        unpack_body,
        [(4, 512, 128), field, (NB, 40, 128), velocity, state_shape, wide, wide],
        [pltpu.VMEM((4, 512, 128), F32)],
        scalars=2,
    )(*me, everything, own_rows)
    helm, vectors = call(unpack_rest_body, [velocity, (NB, 192, 128)])(everything)

    def schwarz_front(boxes):
        return call(schwarz_front_body, [(NB, 384, 128)], [pltpu.VMEM((6, 8, 8, 128), F32)])(boxes, vectors)[0]

    def precondition(boxes, state, left, right, front):
        state, message = call(middle_body, [state_shape, state_shape])(dense, state, left, right)
        left_mid, right_mid = exchange(message, message)
        part, up, down = call(
            schwarz_body,
            [field, plane, plane],
            [
                pltpu.VMEM((8, 8, 8, 128), F32),
                pltpu.VMEM((8, 8, 8, 128), F32),
                pltpu.VMEM(velocity, F32),
                pltpu.VMEM((2, 8, 8, 128), F32),
                pltpu.VMEM((2, 8, 8, 128), F32),
            ],
        )(boxes, front, vectors, small, left, right)
        state, up, down = call(late_body, [state_shape, wide, wide])(
            dense, state, left_mid, right_mid, up, down
        )
        left, right = exchange(up, down)
        z, t, up, down = call(gradient_body, [field, (NB, 1536, 128), plane, plane])(
            dense, state, left, right, part, small, forward
        )
        left, right = exchange(up, down)
        return z, t, left, right

    spread = [pltpu.VMEM((3072, 512), BF16)]
    left, right = exchange(up, down)
    front = schwarz_front(boxes)
    left, right, helm, front = lax.optimization_barrier((left, right, helm, front))
    (inverse,) = call(helm_body, [velocity])(helm, left, right)
    z, t, left, right = precondition(boxes, state, left, right, front)
    w, boxes, state, up, down = call(
        first_image_body, [field, velocity, state_shape, wide, wide], spread
    )(t, left, right, inverse, small, backward, dense)
    left, right = exchange(up, down)
    front = schwarz_front(boxes)
    left, right, front = lax.optimization_barrier((left, right, front))
    q, t, left, right = precondition(boxes, state, left, right, front)
    (products,) = call(products_body, [(8, 128)])(rhs, z, w, q)
    (sums,) = call(energy_body, [(8, 128)])(t, left, right, inverse, products)
    sums = lax.all_to_all(jnp.broadcast_to(sums[None], (count, 8, 128)), "gx", 0, 0)
    (v,) = call(last_image_body, [field], spread)(t, left, right, inverse, small, backward)
    own = call(own_body, [(6, 6, 192)] * 4, scalars=2)(*me, z, w, q, v, six.T.copy())
    return tuple(
        pl.pallas_call(
            last_body,
            out_shape=[jax.ShapeDtypeStruct((6, 6, 192), F32)] * 2,
            in_specs=[pl.BlockSpec(memory_space=pltpu.VMEM)] * 6,
            out_specs=[pl.BlockSpec(memory_space=pl.ANY)] * 2,
            scratch_shapes=[pltpu.VMEM((6, 6, 192), F32)] * 2 + [pltpu.SemaphoreType.DMA((2,))],
            compiler_params=pltpu.CompilerParams(vmem_limit_bytes=40 * 1024 * 1024),
        )(sums, *own, divergence)
    )


def solution(mesh):
    in_specs = (
        P("gy", "col", "gx"),
        P(None, ("gx", "gy", "col")),
        P("gy", "col", "gx"),
        P(None, None, None, ("gx", "gy", "col")),
        P(None, None, ("gx", "gy", "col")),
        P(("gx", "gy", "col"), None),
        P("gx", "gy", "col"),
    )
    out_specs = (P("gy", "col", "gx"), P("gy", "col", "gx"))
    return jax.shard_map(local, mesh=mesh, in_specs=in_specs, out_specs=out_specs, check_vma=False)
```
